32 devices in a mesh: dp: 4 (over y, x), tensor: 8 (over z, core).
Axes of the slice: x: 2, y: 2, z: 4, core: 2. Of those that a mesh axis runs over, the one named last changes fastest.
Arguments:
- hidden_in: bfloat16 [256, 1024], P(('dp', 'tensor')), parts along dimension 0, may hold values from -50 to 50
- expert_ids: int32 [256, 2], P(('dp', 'tensor')), parts along dimension 0, may hold values from 0 to 1, all different within a row; in each aligned block of 8 rows (0 to 7, 8 to 15, ...) at most 8 rows name the same one
- gate_weights: float32 [256, 2], P(('dp', 'tensor')), parts along dimension 0, may hold values from 0.05 to 0.5
- targets: int32 [256], P('dp'), parts along dimension 0, may hold values from 0 to 4095
- seq_ids: int32 [256], P('dp'), parts along dimension 0, may hold values from 0 to 15, never falling along the last dimension, each value on 1 to 16 neighbouring positions
- moe_gain: float32 [1024], replicated, may hold values from 0.5 to 1.5
- w_gate: bfloat16 [1024, 2816], P(None, 'tensor'), may hold values from -0.1875 to 0.1875
- w_up: bfloat16 [1024, 2816], P(None, 'tensor'), may hold values from -0.1875 to 0.1875
- w_down: bfloat16 [2816, 1024], P('tensor'), may hold values from -0.15625 to 0.15625
- final_gain: float32 [1024], replicated, may hold values from 0.5 to 1.5
- head_weight: bfloat16 [1024, 4096], P(None, 'tensor'), may hold values from -66.498 to 66.498
- adapter_down: bfloat16 [1024, 64], replicated, may hold values from -0.1875 to 0.1875
- adapter_up: bfloat16 [64, 4096], P(None, 'tensor'), may hold values from -0.75 to 0.75
Outputs:
- policy_logp: float32 [256], P(('dp', 'tensor')), parts along dimension 0
- log_ratio: float32 [256], P(('dp', 'tensor')), parts along dimension 0
- seq_sums: float32 [64], P('dp'), parts along dimension 0
The draws below stay inside these ranges and needn't reach their ends.
There are 4 independent parts, one for each index of `dp`. The reference program is written for one: setup_inputs(seed, part) draws one part's arguments, and reference() takes and returns one part's arrays. A program takes and returns all parts, laid end to end along the dimension named above; an argument that names none is the same for every part. Nothing has to cross between parts.
Inputs may be any that keep to these rules, and one draw needn't show every extreme that they name: `expert_ids`: in the 8 rows of one device no expert is named more than 8 times, a bound that some block reaches; each row names 2 different experts. `seq_ids`: ids never fall along the tokens; a rollout has 1 to 16 tokens, one exactly 16.
All inputs are finite; a program needn't handle non-finite values.
Results may differ from the reference program's by a relative error of at most 0.011.
Values may be sent and summed in bfloat16 or wider, within the bound.
No kernel may reach another device: no remote copies, remote signals or barrier semaphores. Data moves between devices by JAX's collectives and lax.ppermute only.
A program may use at most 64 MiB of HBM per device.

```python
import math
import jax
import jax.numpy as jnp
import numpy as np
from jax import lax

D = 1024
MOE_FF = 1408
SPLIT = 4
EXPERTS = 2
TOP = 2
TOK_DEV = 8
TOKENS = 64
CAP = 8
VOCAB = 4096
RANK = 64
SEQS = 16
SEQ_MOST = 16
N_TENSOR = 8


def draw_hidden_in(key, part):
    keys = jax.random.split(jax.random.fold_in(key, 11), 3)
    row_scale = jnp.exp(jax.random.uniform(keys[0], (TOKENS, 1), jnp.float32, 0.0, math.log(10.0)))
    col_scale = jnp.exp(jax.random.uniform(keys[1], (1, D), jnp.float32, 0.0, math.log(10.0)))
    base_vals = jnp.clip(jax.random.normal(keys[2], (TOKENS, D), jnp.float32), -5.0, 5.0)
    return (base_vals * row_scale * col_scale * 0.1).astype(jnp.bfloat16)


def draw_head_weight(key, part):
    keys = jax.random.split(jax.random.fold_in(key, 23), 2)
    sigma = 3.0 / math.sqrt(D)
    col_scale = jnp.exp(jax.random.uniform(keys[0], (1, VOCAB), jnp.float32, 0.0, math.log(10.0))) * 0.4
    base_vals = jnp.clip(jax.random.normal(keys[1], (D, VOCAB), jnp.float32), -5.0, 5.0)
    weights = base_vals * col_scale * sigma
    return weights.astype(jnp.bfloat16)


def place_ends(entries, stream_key, least, top_value):
    shape = entries.shape
    place = [jax.random.randint(jax.random.fold_in(stream_key, axis), (), 0, shape[axis]) for axis in range(len(shape))]
    entries = entries.at[tuple(place)].set(least)
    longest = shape.index(max(shape))
    place[longest] = (place[longest] + 1) % shape[longest]
    return entries.at[tuple(place)].set(top_value)


def shard_levels(own_key, dims, shards, least, high):
    level = 1.0
    for axis_at, shards_of in shards:
        heights = jax.random.uniform(jax.random.fold_in(jax.random.fold_in(own_key, 6), axis_at), (shards_of,), jnp.float32, least / len(shards), high / len(shards))
        level = level * jnp.repeat(jnp.exp(heights), dims[axis_at] // shards_of).reshape((-1,) + (1,) * (len(dims) - 1 - axis_at))
    return level


def cumulative_ranks(number_of, lean):
    loads = [(1 << 20) // math.isqrt(grade ** lean) + 1 for grade in range(1, number_of + 1)]
    deviation = 1 + sum(loads) // (1 << 30)
    return np.cumsum(np.array([max(1, weight // deviation) for weight in loads]))


def skewed_ids(key, dims, number_of, skew):
    table = cumulative_ranks(number_of, skew)
    lot = jax.random.randint(jax.random.fold_in(key, 1), dims, 0, int(table[number_of - 1]))
    grade = jnp.searchsorted(jnp.asarray(table, jnp.int32), lot, side="right")
    return jax.random.permutation(jax.random.fold_in(key, 2), number_of)[grade].astype(jnp.int32)


def split_up(amount, total, limit, lean):
    portions = [(1 << 20) // math.isqrt(rank ** lean) + 1 for rank in range(2, amount + 1)]
    spare, counts = total - limit - (amount - 1), [1] * (amount - 1)
    while spare > 0:
        candidates = [i for i in range(amount - 1) if counts[i] < limit]
        pool, remaining = sum([portions[i] for i in candidates]), spare
        for i in candidates:
            more = min(limit - counts[i], max(1, remaining * portions[i] // pool), spare)
            counts[i] = counts[i] + more
            spare = spare - more
    return np.array([limit] + counts)


def uneven_parts(rng, amount, total, most, lean):
    if amount == 2:
        one = jax.random.randint(rng, (), max(1, total - most), min(most, total - 1) + 1)
        return jnp.stack([one, total - one])
    lengths = jnp.asarray(split_up(amount, total, most, lean), jnp.int32)
    couples = (amount - 1) // 2
    giver, receiver = lengths[1:1 + 2 * couples:2], lengths[2:2 + 2 * couples:2]
    slack = jnp.minimum(giver - 1, most - receiver)
    moved = jax.random.randint(jax.random.fold_in(rng, 1), (couples,), 0, 1 << 20) % (slack + 1)
    lengths = lengths.at[1:1 + 2 * couples:2].set(giver - moved).at[2:2 + 2 * couples:2].set(receiver + moved)
    return lengths[jax.random.permutation(jax.random.fold_in(rng, 2), amount)]


def routed_block(rng, own, number, rows, number_of, top, limit, slope):
    ranking = jax.random.permutation(rng, number_of)
    heavy_load, ordinary = portions_of(number_of, rows * top, limit, slope, True), portions_of(number_of, rows * top, limit, slope, False)
    places = jnp.arange(number_of)

    def named(lengths, turn):
        used = int((lengths > 0).sum())
        fixed = max(1, used // 4)
        shifted = fixed + (places - fixed + turn * (used - fixed)) % max(1, number_of - fixed)
        return jnp.zeros((number_of,), jnp.int32).at[ranking[jnp.where(places < fixed, places, shifted)]].set(jnp.asarray(lengths, jnp.int32))

    lengths = jnp.where(number % 4 == 0, named(heavy_load, number // 4), named(ordinary, number - number // 4 - 1))
    mixed = jax.random.permutation(jax.random.fold_in(own, 3), number_of)
    giver, taker = mixed[0:number_of // 2 * 2:2], mixed[1:number_of // 2 * 2:2]
    margin = jnp.minimum(lengths[giver] - 1, limit - lengths[taker]) // 2
    margin = jnp.where((giver == ranking[0]) | (taker == ranking[0]) | (lengths[taker] == 0), 0, jnp.maximum(margin, 0))
    shifted = jax.random.randint(jax.random.fold_in(own, 4), (number_of // 2,), 0, 1 << 20) % (margin + 1)
    lengths = lengths.at[giver].add(-shifted).at[taker].add(shifted)
    labels = jnp.searchsorted(jnp.cumsum(lengths), jnp.arange(rows * top), side="right").astype(jnp.int32)
    grid = labels.reshape(top, rows).T
    grid = grid[jax.random.permutation(jax.random.fold_in(own, 1), rows)]
    turn = jax.random.randint(jax.random.fold_in(own, 2), (rows, 1), 0, top)
    return jnp.take_along_axis(grid, (jnp.arange(top)[None, :] + turn) % top, axis=1)


def portions_of(amount, total, bound, slope, full):
    loads = [(1 << 20) // math.isqrt(rank ** slope) + 1 for rank in range(1, amount + 1)]
    largest = bound if full else min(bound, max(-(-total // amount), total * loads[0] // sum(loads)))
    least = 1 if total - largest >= amount - 1 else 0
    given, spare = [largest] + [least] * (amount - 1), total - largest - least * (amount - 1)
    while spare > 0:
        candidates = [i for i in range(1, amount) if given[i] < largest] or [i for i in range(1, amount) if given[i] < bound]
        pool, remaining = sum([loads[i] for i in candidates]), spare
        for i in candidates:
            more = min(bound - given[i], max(1, remaining * loads[i] // pool), spare)
            given[i] = given[i] + more
            spare = spare - more
    return np.array(given)


def normal_values(rng, shape, deviation, most, cuts=(), held_as=jnp.bfloat16):
    array = jax.random.normal(rng, shape, jnp.float32) * deviation
    if len(cuts) > 0:
        array = shard_levels(rng, shape, cuts, -0.22, 0.18) * array
    return jnp.clip(array, min=-most, max=most).astype(held_as)


def setup_inputs(seed: int = 0, part: int = 0) -> dict:
    arg_keys = jax.random.split(jax.random.key(seed), 14)
    part_splits = jax.random.split(jax.random.fold_in(arg_keys[13], part), 14)
    hidden_in = draw_hidden_in(jax.random.fold_in(jax.random.fold_in(arg_keys[13], part), 71), part)
    expert_ids_keys = jax.random.split(jax.random.fold_in(part_splits[1], 1), TOKENS // TOK_DEV)
    expert_ids_turns = jax.random.permutation(jax.random.fold_in(part_splits[1], 3), TOKENS // TOK_DEV)
    expert_ids = jax.vmap(lambda own, number: routed_block(jax.random.fold_in(part_splits[1], 2), own, number, TOK_DEV, EXPERTS, TOP, CAP, 1))(expert_ids_keys, expert_ids_turns).reshape((TOKENS, TOP))
    gate_weights = jnp.clip(jnp.exp(math.log(0.5) - 2.3025851 * jax.random.uniform(part_splits[2], (TOKENS, TOP), jnp.float32) ** shard_levels(part_splits[2], (TOKENS, TOP), ((0, 8),), -0.2, 0.2)), 0.05, 0.5)
    targets = place_ends(skewed_ids(part_splits[3], (TOKENS,), VOCAB, 2), jax.random.fold_in(part_splits[3], 3), 0, VOCAB - 1).astype(jnp.int32)
    seq_ids = jnp.searchsorted(jnp.cumsum(uneven_parts(part_splits[4], SEQS, TOKENS, SEQ_MOST, 2)), jnp.arange(TOKENS), side="right").astype(jnp.int32)
    moe_gain = jnp.clip(1.0 + 0.1 * jax.random.normal(arg_keys[5], (D,), jnp.float32), 0.5, 1.5)
    w_gate = normal_values(arg_keys[6], (D, EXPERTS * MOE_FF), D ** -0.5, 0.1875, ((1, 8),))
    w_up = normal_values(arg_keys[7], (D, EXPERTS * MOE_FF), D ** -0.5, 0.1875, ((1, 8),))
    w_down = normal_values(arg_keys[8], (EXPERTS * MOE_FF, D), MOE_FF ** -0.5, 0.15625, ((0, 8),))
    final_gain = jnp.clip(1.0 + 0.1 * jax.random.normal(arg_keys[9], (D,), jnp.float32), 0.5, 1.5)
    head_weight = draw_head_weight(jax.random.fold_in(arg_keys[13], 71), part)
    adapter_down = normal_values(arg_keys[11], (D, RANK), D ** -0.5, 0.1875)
    adapter_up = normal_values(arg_keys[12], (RANK, VOCAB), RANK ** -0.5, 0.75, ((1, 8),))
    return {"hidden_in": hidden_in, "expert_ids": expert_ids, "gate_weights": gate_weights, "targets": targets, "seq_ids": seq_ids, "moe_gain": moe_gain, "w_gate": w_gate, "w_up": w_up, "w_down": w_down, "final_gain": final_gain, "head_weight": head_weight, "adapter_down": adapter_down, "adapter_up": adapter_up}


epsilon = 1e-06

def rms_norm(values, norm_gain):
    mean_sq = lax.optimization_barrier(jnp.mean(values * values, axis=-1, keepdims=True))
    return values * lax.rsqrt(mean_sq + epsilon) * norm_gain

def reference(hidden_in, expert_ids, gate_weights, targets, seq_ids, moe_gain, w_gate, w_up, w_down, final_gain, head_weight, adapter_down, adapter_up):
    moe_input = rms_norm(hidden_in.astype(jnp.float32), moe_gain).astype(jnp.bfloat16)
    blocks = expert_ids.reshape(N_TENSOR, TOK_DEV * TOP)
    chosen_hot = (blocks[:, :, None] == jnp.arange(EXPERTS, dtype=jnp.int32)[None, None, :]).astype(jnp.int32)
    slot_pos = lax.optimization_barrier(jnp.sum((jnp.cumsum(chosen_hot, axis=1) - chosen_hot) * chosen_hot, axis=2))
    block_ids = jnp.arange(N_TENSOR, dtype=jnp.int32)[:, None]
    dest_slot = ((blocks * N_TENSOR + block_ids) * CAP + slot_pos).astype(jnp.int32)
    token_of = (block_ids * TOK_DEV + jnp.arange(TOK_DEV * TOP, dtype=jnp.int32)[None, :] // TOP).astype(jnp.int32)
    slot_rows = jnp.full((EXPERTS * N_TENSOR * CAP,), TOKENS, jnp.int32).at[dest_slot.reshape(-1)].set(token_of.reshape(-1))
    slot_table = slot_rows.reshape(EXPERTS, N_TENSOR * CAP)
    padded = jnp.concatenate([moe_input, jnp.zeros((1, D), jnp.bfloat16)], axis=0)
    piece_units = MOE_FF // SPLIT

    def one_expert(expert):
        row_index = lax.dynamic_index_in_dim(slot_table, expert, 0, keepdims=False)
        slot_input = jnp.take(padded, row_index, axis=0)
        gate_cols = lax.dynamic_slice_in_dim(w_gate, expert * MOE_FF, MOE_FF, 1)
        up_cols = lax.dynamic_slice_in_dim(w_up, expert * MOE_FF, MOE_FF, 1)
        gate_proj = jnp.dot(slot_input, gate_cols, preferred_element_type=jnp.float32)
        up_proj = jnp.dot(slot_input, up_cols, preferred_element_type=jnp.float32)
        inner_act = (jax.nn.silu(gate_proj) * up_proj).astype(jnp.bfloat16)
        down_rows = lax.dynamic_slice_in_dim(w_down, expert * MOE_FF, MOE_FF, 0).reshape(SPLIT, piece_units, D)
        partial_value = jnp.einsum('rqp,qpd->rqd', inner_act.reshape(-1, SPLIT, piece_units).astype(jnp.float32), down_rows.astype(jnp.float32), precision=lax.Precision.HIGHEST)
        return lax.optimization_barrier(jnp.sum(partial_value, axis=1))
    expert_out = lax.map(one_expert, jnp.arange(EXPERTS, dtype=jnp.int32))
    routed = jnp.take(expert_out.reshape(-1, D), dest_slot.reshape(TOKENS, TOP), axis=0)
    mixed = hidden_in.astype(jnp.float32) + lax.optimization_barrier(jnp.sum(gate_weights[:, :, None] * routed, axis=1))
    final_input = rms_norm(mixed, final_gain).astype(jnp.bfloat16)
    adapter_latent = jnp.dot(final_input, adapter_down, preferred_element_type=jnp.float32).astype(jnp.bfloat16)

    def one_block(block_index):
        row_start = block_index * 64
        block_rows = lax.dynamic_slice_in_dim(final_input, row_start, 64)
        block_latent = lax.dynamic_slice_in_dim(adapter_latent, row_start, 64)
        block_targets = lax.dynamic_slice_in_dim(targets, row_start, 64)
        base_logits = jnp.dot(block_rows, head_weight, preferred_element_type=jnp.float32)
        policy_logits = base_logits + jnp.dot(block_latent, adapter_up, preferred_element_type=jnp.float32)

        def target_logp(logits):
            picked = jnp.take_along_axis(logits, block_targets[:, None], axis=1)[:, 0]
            return picked - jax.nn.logsumexp(logits, axis=1)
        return jnp.stack([target_logp(base_logits), target_logp(policy_logits)], axis=1)
    log_probs = lax.map(one_block, jnp.arange(TOKENS // 64, dtype=jnp.int32)).reshape(TOKENS, 2)
    log_ratio = log_probs[:, 1] - log_probs[:, 0]
    seq_match = (seq_ids[None, :] == jnp.arange(SEQS, dtype=jnp.int32)[:, None]).astype(jnp.float32)
    seq_sums = jnp.dot(seq_match, log_ratio, precision=lax.Precision.HIGHEST)
    return (log_probs[:, 1], log_ratio, seq_sums)
```

```python
import jax
import jax.numpy as jnp
import numpy as np
from jax import lax
from jax.sharding import PartitionSpec as P

SPLIT = 4
SEQS = 16


epsilon = 1e-06


def rms_norm(values, norm_gain):
    mean_sq = jnp.mean(values * values, axis=-1, keepdims=True)
    return values * lax.rsqrt(mean_sq + epsilon) * norm_gain


def expert_piece(arrived, w_gate, w_up, w_down):
    features = arrived.shape[-1]
    flat_rows = arrived.reshape(-1, features)
    gate_proj = jnp.dot(flat_rows, w_gate, preferred_element_type=jnp.float32)
    up_proj = jnp.dot(flat_rows, w_up, preferred_element_type=jnp.float32)
    inner_act = (jax.nn.silu(gate_proj) * up_proj).astype(jnp.bfloat16)
    partial_value = jnp.dot(inner_act, w_down, preferred_element_type=jnp.float32)
    return lax.all_to_all(
        partial_value.reshape(arrived.shape), "tensor", split_axis=0, concat_axis=0, tiled=True
    )


def routed_on_device(
    hidden_in,
    expert_ids,
    gate_weights,
    targets,
    seq_ids,
    moe_gain,
    w_gate,
    w_up,
    w_down,
    final_gain,
    head_weight,
    adapter_down,
    adapter_up,
):
    tok_rows, features = hidden_in.shape
    top_count = expert_ids.shape[1]
    devices = lax.axis_size("tensor")
    experts = devices // SPLIT
    capacity = min(tok_rows, 2 * tok_rows * top_count // experts)
    my_index = lax.axis_index("tensor")
    moe_input = rms_norm(hidden_in.astype(jnp.float32), moe_gain).astype(jnp.bfloat16)
    flat_ids = expert_ids.reshape(-1)
    chosen_hot = (flat_ids[:, None] == jnp.arange(experts, dtype=jnp.int32)[None, :]).astype(
        jnp.int32
    )
    slot_pos = jnp.sum((jnp.cumsum(chosen_hot, axis=0) - chosen_hot) * chosen_hot, axis=1)
    target_slot = flat_ids * capacity + slot_pos
    placed = (
        target_slot[:, None] == jnp.arange(experts * capacity, dtype=jnp.int32)[None, :]
    ).reshape(tok_rows, top_count, experts * capacity)
    spread = jnp.any(placed, axis=1).astype(jnp.bfloat16)
    packed = lax.dot_general(
        spread, moe_input, (((0,), (0,)), ((), ())), preferred_element_type=jnp.float32
    ).astype(jnp.bfloat16)
    outgoing = jnp.broadcast_to(
        packed.reshape(experts, 1, capacity, features), (experts, SPLIT, capacity, features)
    ).reshape(devices, capacity, features)
    returned = expert_piece(
        lax.all_to_all(outgoing, "tensor", split_axis=0, concat_axis=0, tiled=True),
        w_gate,
        w_up,
        w_down,
    )
    summed = jnp.sum(returned.reshape(experts, SPLIT, capacity, features), axis=1).reshape(
        experts * capacity, features
    )
    mixing = jnp.sum(placed.astype(jnp.float32) * gate_weights[:, :, None], axis=1)
    residual_sum = hidden_in.astype(jnp.float32) + jnp.dot(
        mixing, summed, precision=lax.Precision.HIGHEST
    )
    final_input = rms_norm(residual_sum, final_gain).astype(jnp.bfloat16)
    vocab_dev = head_weight.shape[1]
    vocab_start = my_index * vocab_dev
    columns = jnp.arange(vocab_dev, dtype=jnp.int32)

    def summary(block_rows, block_latent, row_start):
        row_count = block_rows.shape[0]
        base_logits = jnp.dot(block_rows, head_weight, preferred_element_type=jnp.float32)
        policy_logits = base_logits + jnp.dot(
            block_latent, adapter_up, preferred_element_type=jnp.float32
        )
        wanted = lax.dynamic_slice_in_dim(targets, row_start, row_count) - vocab_start
        is_target = wanted[:, None] == columns[None, :]

        def reduce_logits(logits):
            top_value = jnp.max(logits, axis=1)
            exp_total = jnp.sum(jnp.exp(logits - top_value[:, None]), axis=1)
            picked = jnp.sum(jnp.where(is_target, logits, 0.0), axis=1)
            return (top_value, exp_total, picked)

        base_stats = reduce_logits(base_logits)
        policy_stats = reduce_logits(policy_logits)
        return tuple(
            (
                jnp.stack([earlier, later], axis=1)
                for earlier, later in zip(base_stats, policy_stats)
            )
        )

    def blocked(shard_rows, shard_latent, row_start):
        row_count = shard_rows.shape[0]
        block_size = 512 if row_count % 512 == 0 else row_count
        if block_size == row_count:
            return summary(shard_rows, shard_latent, row_start)

        def one_block(block_index):
            offset = block_index * block_size
            return summary(
                lax.dynamic_slice_in_dim(shard_rows, offset, block_size),
                lax.dynamic_slice_in_dim(shard_latent, offset, block_size),
                row_start + offset,
            )

        results = lax.map(one_block, jnp.arange(row_count // block_size, dtype=jnp.int32))
        return tuple((member.reshape(row_count, 2) for member in results))

    shard_rows = lax.all_gather(final_input, "tensor", axis=0, tiled=True)
    shard_latent = jnp.dot(shard_rows, adapter_down, preferred_element_type=jnp.float32).astype(
        jnp.bfloat16
    )
    block_stats = blocked(shard_rows, shard_latent, jnp.int32(0))
    maxima, exp_sums, target_logits = tuple((update for update in block_stats))
    ceiling = lax.pmax(maxima, "tensor")
    totals, picked_all = lax.psum((exp_sums * jnp.exp(maxima - ceiling), target_logits), "tensor")
    log_probs = picked_all - ceiling - jnp.log(totals)
    log_ratio = log_probs[:, 1] - log_probs[:, 0]
    seq_match = (seq_ids[None, :] == jnp.arange(SEQS, dtype=jnp.int32)[:, None]).astype(jnp.float32)
    seq_sums = jnp.dot(seq_match, log_ratio, precision=lax.Precision.HIGHEST)
    own_start = my_index * tok_rows
    policy_own = lax.dynamic_slice_in_dim(log_probs[:, 1], own_start, tok_rows)
    ratio_own = lax.dynamic_slice_in_dim(log_ratio, own_start, tok_rows)
    return (policy_own, ratio_own, seq_sums)


def exchange(values, mask):
    devices = lax.axis_size("tensor")
    return lax.ppermute(values, "tensor", [(i, i ^ mask) for i in range(devices)])


def bit(number, place):
    return (number >> place) & 1


def in_order(late, mine, other):
    return jnp.concatenate([jnp.where(late, other, mine), jnp.where(late, mine, other)], axis=0)


def thirds(values):
    high = lax.reduce_precision(values, 8, 7)
    middle = lax.reduce_precision(values - high, 8, 7)
    low = values - high - middle
    return [part.astype(jnp.bfloat16) for part in (high, middle, low)]


def dense_on_device(
    hidden_in,
    expert_ids,
    gate_weights,
    targets,
    seq_ids,
    moe_gain,
    w_gate,
    w_up,
    w_down,
    final_gain,
    head_weight,
    adapter_down,
    adapter_up,
):
    tok_rows, features = hidden_in.shape
    devices = lax.axis_size("tensor")
    bits = devices.bit_length() - 1
    experts = devices // SPLIT
    lanes = -(-3 * experts // 128) * 128
    my_index = lax.axis_index("tensor")
    far = [(b, (1 << b) + 1) for b in range(bits - 1, 0, -1)]
    parity = sum(bit(my_index, b) for b in range(bits)) & 1
    ranks = sorted(
        range(devices), key=lambda i: [i.bit_count() & 1] + [bit(i, b) for b in range(1, bits)]
    )
    token_at = np.array([i * tok_rows + r for i in ranks for r in range(tok_rows)])
    place_of = np.argsort(token_at)

    expert_of = jnp.arange(experts, dtype=jnp.int32)
    mixing = jnp.sum(
        jnp.where(expert_ids[:, :, None] == expert_of, gate_weights[:, :, None], 0.0), axis=1
    )
    columns = thirds(mixing)
    gap = jnp.zeros((tok_rows, lanes - 3 * experts), jnp.bfloat16)
    rows = jnp.concatenate([hidden_in, *columns, gap], axis=1)
    for b, mask in far:
        rows = in_order(bit(my_index, b) == 1, rows, exchange(rows, mask))
    rows = in_order(parity == 1, rows, exchange(rows, 1))

    hidden = rows[:, :features].astype(jnp.float32)
    moe_input = rms_norm(hidden, moe_gain).astype(jnp.bfloat16)
    weights = rows[:, features : features + 3 * experts].astype(jnp.float32)
    weights = weights.reshape(-1, 3, experts)
    weights = weights[:, 0] + weights[:, 1] + weights[:, 2]
    my_weight = jnp.sum(jnp.where(expert_of == my_index // SPLIT, weights, 0.0), axis=1)
    gate_proj = jnp.dot(moe_input, w_gate, preferred_element_type=jnp.float32)
    up_proj = jnp.dot(moe_input, w_up, preferred_element_type=jnp.float32)
    inner_act = (jax.nn.silu(gate_proj) * up_proj).astype(jnp.bfloat16)
    partial_value = jnp.dot(inner_act, w_down, preferred_element_type=jnp.float32)
    partial_value = partial_value * my_weight[:, None]

    half = rows.shape[0] // 2
    late = parity == 1
    first, second = partial_value[:half], partial_value[half:]
    total = jnp.where(late, second, first) + exchange(jnp.where(late, first, second), 1)
    for b, mask in far[::-1]:
        total = total + exchange(total.astype(jnp.bfloat16), mask).astype(jnp.float32)
    mixed = total + jnp.where(late, hidden[half:], hidden[:half])
    own_final = rms_norm(mixed, final_gain).astype(jnp.bfloat16)
    final_input = in_order(late, own_final, exchange(own_final, 1))

    latent = jnp.dot(final_input, adapter_down, preferred_element_type=jnp.float32).astype(
        jnp.bfloat16
    )
    base_logits = jnp.dot(final_input, head_weight, preferred_element_type=jnp.float32)
    policy_logits = base_logits + jnp.dot(latent, adapter_up, preferred_element_type=jnp.float32)
    vocab_dev = head_weight.shape[1]
    wanted = targets[token_at] - my_index * vocab_dev
    is_target = wanted[:, None] == jnp.arange(vocab_dev, dtype=jnp.int32)[None, :]

    def summary(logits):
        top_value = jnp.max(logits, axis=1)
        exp_total = jnp.sum(jnp.exp(logits - top_value[:, None]), axis=1)
        picked = jnp.sum(jnp.where(is_target, logits, 0.0), axis=1)
        return jnp.stack([top_value, exp_total, picked])

    stats = jnp.stack([summary(base_logits), summary(policy_logits)])
    for mask in [1] + [mask for _, mask in far]:
        other = exchange(stats, mask)
        ceiling = jnp.maximum(stats[:, 0], other[:, 0])
        exp_total = stats[:, 1] * jnp.exp(stats[:, 0] - ceiling) + other[:, 1] * jnp.exp(
            other[:, 0] - ceiling
        )
        stats = jnp.stack([ceiling, exp_total, stats[:, 2] + other[:, 2]], axis=1)
    log_probs = stats[:, 2] - stats[:, 0] - jnp.log(stats[:, 1])
    log_probs = log_probs[:, place_of]
    log_ratio = log_probs[1] - log_probs[0]
    seq_match = (seq_ids[None, :] == jnp.arange(SEQS, dtype=jnp.int32)[:, None]).astype(jnp.float32)
    seq_sums = jnp.sum(seq_match * log_ratio[None, :], axis=1)
    own_start = my_index * tok_rows
    policy_own = lax.dynamic_slice_in_dim(log_probs[1], own_start, tok_rows)
    ratio_own = lax.dynamic_slice_in_dim(log_ratio, own_start, tok_rows)
    return (policy_own, ratio_own, seq_sums)


def solution(mesh):
    in_specs = (
        P(("dp", "tensor"), None),
        P(("dp", "tensor"), None),
        P(("dp", "tensor"), None),
        P("dp"),
        P("dp"),
        P(),
        P(None, "tensor"),
        P(None, "tensor"),
        P("tensor", None),
        P(),
        P(None, "tensor"),
        P(),
        P(None, "tensor"),
    )
    out_specs = (P(("dp", "tensor")), P(("dp", "tensor")), P("dp"))
    devices = mesh.shape["tensor"]

    def on_device(hidden_in, expert_ids, *others):
        every_expert = expert_ids.shape[1] == devices // SPLIT
        step = dense_on_device if every_expert else routed_on_device
        return step(hidden_in, expert_ids, *others)

    return jax.shard_map(
        on_device, mesh=mesh, in_specs=in_specs, out_specs=out_specs, check_vma=False
    )
```

```python
import jax
import jax.numpy as jnp
from jax import lax
from jax.experimental import pallas as pl
from jax.experimental.pallas import tpu as pltpu
from jax.sharding import PartitionSpec as P

SPLIT = 4
SEQS = 16


epsilon = 1e-06


def rms_norm(values, norm_gain):
    mean_sq = jnp.mean(values * values, axis=-1, keepdims=True)
    return values * lax.rsqrt(mean_sq + epsilon) * norm_gain


def expert_piece(arrived, w_gate, w_up, w_down):
    features = arrived.shape[-1]
    flat_rows = arrived.reshape(-1, features)
    gate_proj = jnp.dot(flat_rows, w_gate, preferred_element_type=jnp.float32)
    up_proj = jnp.dot(flat_rows, w_up, preferred_element_type=jnp.float32)
    inner_act = (jax.nn.silu(gate_proj) * up_proj).astype(jnp.bfloat16)
    partial_value = jnp.dot(inner_act, w_down, preferred_element_type=jnp.float32)
    return lax.all_to_all(
        partial_value.reshape(arrived.shape), "tensor", split_axis=0, concat_axis=0, tiled=True
    )


def routed_on_device(
    hidden_in,
    expert_ids,
    gate_weights,
    targets,
    seq_ids,
    moe_gain,
    w_gate,
    w_up,
    w_down,
    final_gain,
    head_weight,
    adapter_down,
    adapter_up,
):
    tok_rows, features = hidden_in.shape
    top_count = expert_ids.shape[1]
    devices = lax.axis_size("tensor")
    experts = devices // SPLIT
    capacity = min(tok_rows, 2 * tok_rows * top_count // experts)
    my_index = lax.axis_index("tensor")
    moe_input = rms_norm(hidden_in.astype(jnp.float32), moe_gain).astype(jnp.bfloat16)
    flat_ids = expert_ids.reshape(-1)
    chosen_hot = (flat_ids[:, None] == jnp.arange(experts, dtype=jnp.int32)[None, :]).astype(
        jnp.int32
    )
    slot_pos = jnp.sum((jnp.cumsum(chosen_hot, axis=0) - chosen_hot) * chosen_hot, axis=1)
    target_slot = flat_ids * capacity + slot_pos
    placed = (
        target_slot[:, None] == jnp.arange(experts * capacity, dtype=jnp.int32)[None, :]
    ).reshape(tok_rows, top_count, experts * capacity)
    spread = jnp.any(placed, axis=1).astype(jnp.bfloat16)
    packed = lax.dot_general(
        spread, moe_input, (((0,), (0,)), ((), ())), preferred_element_type=jnp.float32
    ).astype(jnp.bfloat16)
    outgoing = jnp.broadcast_to(
        packed.reshape(experts, 1, capacity, features), (experts, SPLIT, capacity, features)
    ).reshape(devices, capacity, features)
    returned = expert_piece(
        lax.all_to_all(outgoing, "tensor", split_axis=0, concat_axis=0, tiled=True),
        w_gate,
        w_up,
        w_down,
    )
    summed = jnp.sum(returned.reshape(experts, SPLIT, capacity, features), axis=1).reshape(
        experts * capacity, features
    )
    mixing = jnp.sum(placed.astype(jnp.float32) * gate_weights[:, :, None], axis=1)
    residual_sum = hidden_in.astype(jnp.float32) + jnp.dot(
        mixing, summed, precision=lax.Precision.HIGHEST
    )
    final_input = rms_norm(residual_sum, final_gain).astype(jnp.bfloat16)
    vocab_dev = head_weight.shape[1]
    vocab_start = my_index * vocab_dev
    columns = jnp.arange(vocab_dev, dtype=jnp.int32)

    def summary(block_rows, block_latent, row_start):
        row_count = block_rows.shape[0]
        base_logits = jnp.dot(block_rows, head_weight, preferred_element_type=jnp.float32)
        policy_logits = base_logits + jnp.dot(
            block_latent, adapter_up, preferred_element_type=jnp.float32
        )
        wanted = lax.dynamic_slice_in_dim(targets, row_start, row_count) - vocab_start
        is_target = wanted[:, None] == columns[None, :]

        def reduce_logits(logits):
            top_value = jnp.max(logits, axis=1)
            exp_total = jnp.sum(jnp.exp(logits - top_value[:, None]), axis=1)
            picked = jnp.sum(jnp.where(is_target, logits, 0.0), axis=1)
            return (top_value, exp_total, picked)

        base_stats = reduce_logits(base_logits)
        policy_stats = reduce_logits(policy_logits)
        return tuple(
            (
                jnp.stack([earlier, later], axis=1)
                for earlier, later in zip(base_stats, policy_stats)
            )
        )

    def blocked(shard_rows, shard_latent, row_start):
        row_count = shard_rows.shape[0]
        block_size = 512 if row_count % 512 == 0 else row_count
        if block_size == row_count:
            return summary(shard_rows, shard_latent, row_start)

        def one_block(block_index):
            offset = block_index * block_size
            return summary(
                lax.dynamic_slice_in_dim(shard_rows, offset, block_size),
                lax.dynamic_slice_in_dim(shard_latent, offset, block_size),
                row_start + offset,
            )

        results = lax.map(one_block, jnp.arange(row_count // block_size, dtype=jnp.int32))
        return tuple((member.reshape(row_count, 2) for member in results))

    shard_rows = lax.all_gather(final_input, "tensor", axis=0, tiled=True)
    shard_latent = jnp.dot(shard_rows, adapter_down, preferred_element_type=jnp.float32).astype(
        jnp.bfloat16
    )
    block_stats = blocked(shard_rows, shard_latent, jnp.int32(0))
    maxima, exp_sums, target_logits = tuple((update for update in block_stats))
    ceiling = lax.pmax(maxima, "tensor")
    totals, picked_all = lax.psum((exp_sums * jnp.exp(maxima - ceiling), target_logits), "tensor")
    log_probs = picked_all - ceiling - jnp.log(totals)
    log_ratio = log_probs[:, 1] - log_probs[:, 0]
    seq_match = (seq_ids[None, :] == jnp.arange(SEQS, dtype=jnp.int32)[:, None]).astype(jnp.float32)
    seq_sums = jnp.dot(seq_match, log_ratio, precision=lax.Precision.HIGHEST)
    own_start = my_index * tok_rows
    policy_own = lax.dynamic_slice_in_dim(log_probs[:, 1], own_start, tok_rows)
    ratio_own = lax.dynamic_slice_in_dim(log_ratio, own_start, tok_rows)
    return (policy_own, ratio_own, seq_sums)


def exchange(values, mask):
    devices = lax.axis_size("tensor")
    return lax.ppermute(values, "tensor", [(i, i ^ mask) for i in range(devices)])


def bit(number, place):
    return (number >> place) & 1


def in_order(late, mine, other):
    return jnp.concatenate([jnp.where(late, other, mine), jnp.where(late, mine, other)], axis=0)


def thirds(values):
    high = lax.reduce_precision(values, 8, 7)
    middle = lax.reduce_precision(values - high, 8, 7)
    low = values - high - middle
    return [part.astype(jnp.bfloat16) for part in (high, middle, low)]


def token_at(place, tok_rows, bits):
    devices = 1 << bits
    rank = place // tok_rows
    parity = rank >> (bits - 1)
    device = parity * 0
    low = parity
    for b in range(1, bits):
        one = (rank >> (bits - 1 - b)) & 1
        device = device + one * (1 << b)
        low = low ^ one
    return (device + low) * tok_rows + place % tok_rows


def expert_kernel(own_ref, other_ref, gain_ref, gate_ref, up_ref, down_ref, keep_ref, give_ref):
    half, features = keep_ref.shape
    devices = lax.axis_size("tensor")
    experts = devices // SPLIT
    expert = lax.axis_index("tensor") // SPLIT
    rows = jnp.concatenate([own_ref[...], other_ref[...]], axis=0)
    hidden = rows[:, :features].astype(jnp.float32)
    moe_input = rms_norm(hidden, gain_ref[...]).astype(jnp.bfloat16)
    extra = rows[:, features:].astype(jnp.float32)
    lane = lax.broadcasted_iota(jnp.int32, extra.shape, 1)
    mine = (lane % experts == expert) & (lane < 3 * experts)
    weight = jnp.sum(jnp.where(mine, extra, 0.0), axis=1, keepdims=True)
    gate_proj = jnp.dot(moe_input, gate_ref[...], preferred_element_type=jnp.float32)
    up_proj = jnp.dot(moe_input, up_ref[...], preferred_element_type=jnp.float32)
    inner_act = (jax.nn.silu(gate_proj) * up_proj).astype(jnp.bfloat16)
    partial_value = jnp.dot(inner_act, down_ref[...], preferred_element_type=jnp.float32) * weight
    keep_ref[...] = partial_value[:half]
    give_ref[...] = partial_value[half:]


def norm_kernel(total_ref, arrived_ref, own_ref, gain_ref, out_ref):
    features = out_ref.shape[1]
    mixed = total_ref[...] + arrived_ref[...].astype(jnp.float32)
    mixed = mixed + own_ref[:, :features].astype(jnp.float32)
    out_ref[...] = rms_norm(mixed, gain_ref[...]).astype(jnp.bfloat16)


def head_kernel(
    tok_rows, bits, own_ref, other_ref, targets_ref, head_ref, down_ref, up_ref, stats_ref
):
    my_index = lax.axis_index("tensor")
    late = sum(bit(my_index, b) for b in range(bits)) & 1 == 1
    own, other = own_ref[...], other_ref[...]
    rows = in_order(late, own, other)
    tokens, vocab_dev = rows.shape[0], head_ref.shape[1]
    latent = jnp.dot(rows, down_ref[...], preferred_element_type=jnp.float32)
    latent = latent.astype(jnp.bfloat16)
    base_logits = jnp.dot(rows, head_ref[...], preferred_element_type=jnp.float32)
    policy_logits = base_logits + jnp.dot(latent, up_ref[...], preferred_element_type=jnp.float32)
    place = lax.broadcasted_iota(jnp.int32, (tokens, tokens), 0)
    token = lax.broadcasted_iota(jnp.int32, (tokens, tokens), 1)
    here = token_at(place, tok_rows, bits) == token
    wanted = jnp.sum(
        jnp.where(here, targets_ref[...].astype(jnp.float32), 0.0), axis=1, keepdims=True
    ).astype(jnp.int32)
    column = lax.broadcasted_iota(jnp.int32, (tokens, vocab_dev), 1)
    is_target = column == wanted - my_index * vocab_dev
    lane = lax.broadcasted_iota(jnp.int32, (tokens, 128), 1)
    packed = jnp.zeros((tokens, 128), jnp.float32)
    for at, logits in enumerate((base_logits, policy_logits)):
        top_value = jnp.max(logits, axis=1, keepdims=True)
        exp_total = jnp.sum(jnp.exp(logits - top_value), axis=1, keepdims=True)
        picked = jnp.sum(jnp.where(is_target, logits, 0.0), axis=1, keepdims=True)
        for kind, value in enumerate((top_value, exp_total, picked)):
            packed = jnp.where(lane == 2 * kind + at, value, packed)
    stats_ref[...] = packed.T[:8]


def merge(one, two):
    ceiling = jnp.maximum(one[0:2], two[0:2])
    exp_total = one[2:4] * jnp.exp(one[0:2] - ceiling) + two[2:4] * jnp.exp(two[0:2] - ceiling)
    return ceiling, exp_total, one[4:6] + two[4:6]


def result_kernel(tok_rows, bits, one_ref, two_ref, seq_ref, policy_ref, ratio_ref, sums_ref):
    ceiling, exp_total, picked = merge(one_ref[...], two_ref[...])
    log_probs = picked - ceiling - jnp.log(exp_total)
    tokens = log_probs.shape[1]
    policy = log_probs[1:2]
    ratio = policy - log_probs[0:1]
    place = lax.broadcasted_iota(jnp.int32, (tokens, tokens), 0)
    token = lax.broadcasted_iota(jnp.int32, (tokens, tokens), 1)
    here = token_at(place, tok_rows, bits) == token
    seq = jnp.sum(jnp.where(here, seq_ref[...].astype(jnp.float32), 0.0), axis=1, keepdims=True)
    row = lax.broadcasted_iota(jnp.int32, (tokens, 128), 0)
    lane = lax.broadcasted_iota(jnp.int32, (tokens, 128), 1)
    own = token_at(row, tok_rows, bits) == lax.axis_index("tensor") * tok_rows + lane
    own_column = (own & (lane < tok_rows)).astype(jnp.float32)
    seq_column = (seq.astype(jnp.int32) == lane).astype(jnp.float32)

    def pick(values, columns):
        return jnp.dot(
            jnp.broadcast_to(values, (8, tokens)),
            columns,
            precision=lax.Precision.HIGHEST,
            preferred_element_type=jnp.float32,
        )

    policy_ref[...] = pick(policy, own_column)[0:1, :tok_rows]
    ratio_ref[...] = pick(ratio, own_column)[0:1, :tok_rows]
    sums_ref[...] = pick(ratio, seq_column)[0:1, :SEQS]


def call(kernel, shapes, *operands, flops=0):
    size = sum(operand.size * operand.dtype.itemsize for operand in operands)
    return pl.pallas_call(
        kernel,
        out_shape=shapes,
        compiler_params=pltpu.CompilerParams(vmem_limit_bytes=32 << 20),
        cost_estimate=pl.CostEstimate(flops=flops, bytes_accessed=size, transcendentals=0),
    )(*operands)


def dense_on_device(
    hidden_in,
    expert_ids,
    gate_weights,
    targets,
    seq_ids,
    moe_gain,
    w_gate,
    w_up,
    w_down,
    final_gain,
    head_weight,
    adapter_down,
    adapter_up,
):
    tok_rows, features = hidden_in.shape
    devices = lax.axis_size("tensor")
    bits = devices.bit_length() - 1
    experts = devices // SPLIT
    tokens = devices * tok_rows
    half = tokens // 2
    lanes = -(-3 * experts // 128) * 128
    my_index = lax.axis_index("tensor")
    far = [(b, (1 << b) + 1) for b in range(bits - 1, 0, -1)]

    def array(rows, columns, dtype):
        return jax.ShapeDtypeStruct((rows, columns), dtype)

    expert_of = jnp.arange(experts, dtype=jnp.int32)
    mixing = jnp.sum(
        jnp.where(expert_ids[:, :, None] == expert_of, gate_weights[:, :, None], 0.0), axis=1
    )
    gap = jnp.zeros((tok_rows, lanes - 3 * experts), jnp.bfloat16)
    own = jnp.concatenate([hidden_in, *thirds(mixing), gap], axis=1)
    for b, mask in far:
        own = in_order(bit(my_index, b) == 1, own, exchange(own, mask))
    other = exchange(own, 1)

    total, give = call(
        expert_kernel,
        [array(half, features, jnp.float32)] * 2,
        own,
        other,
        moe_gain[None],
        w_gate,
        w_up,
        w_down,
        flops=6 * tokens * features * w_gate.shape[1],
    )
    total = total + exchange(give, 1)
    for _, mask in far[:0:-1]:
        total = total + exchange(total.astype(jnp.bfloat16), mask).astype(jnp.float32)
    arrived = exchange(total.astype(jnp.bfloat16), far[0][1])
    own_final = call(
        norm_kernel, array(half, features, jnp.bfloat16), total, arrived, own, final_gain[None]
    )
    other_final = exchange(own_final, 1)

    stats = call(
        lambda *refs: head_kernel(tok_rows, bits, *refs),
        array(8, tokens, jnp.float32),
        own_final,
        other_final,
        targets[None],
        head_weight,
        adapter_down,
        adapter_up,
        flops=2 * tokens * features * head_weight.shape[1],
    )
    masks = [1] + [mask for _, mask in far[::-1]]
    for mask in masks[:-1]:
        pieces = merge(stats, exchange(stats, mask))
        stats = jnp.concatenate([*pieces, jnp.zeros((2, tokens), jnp.float32)], axis=0)
    policy_own, ratio_own, seq_sums = call(
        lambda *refs: result_kernel(tok_rows, bits, *refs),
        [array(1, tok_rows, jnp.float32)] * 2 + [array(1, SEQS, jnp.float32)],
        stats,
        exchange(stats, masks[-1]),
        seq_ids[None],
    )
    return (policy_own[0], ratio_own[0], seq_sums[0])


def solution(mesh):
    in_specs = (
        P(("dp", "tensor"), None),
        P(("dp", "tensor"), None),
        P(("dp", "tensor"), None),
        P("dp"),
        P("dp"),
        P(),
        P(None, "tensor"),
        P(None, "tensor"),
        P("tensor", None),
        P(),
        P(None, "tensor"),
        P(),
        P(None, "tensor"),
    )
    out_specs = (P(("dp", "tensor")), P(("dp", "tensor")), P("dp"))
    devices = mesh.shape["tensor"]

    def on_device(hidden_in, expert_ids, *others):
        every_expert = expert_ids.shape[1] == devices // SPLIT
        step = dense_on_device if every_expert else routed_on_device
        return step(hidden_in, expert_ids, *others)

    return jax.shard_map(
        on_device, mesh=mesh, in_specs=in_specs, out_specs=out_specs, check_vma=False
    )
```

```python
import functools

import jax
import jax.numpy as jnp
from jax import lax
from jax.experimental import pallas as pl
from jax.experimental.pallas import tpu as pltpu
from jax.sharding import PartitionSpec as P

SPLIT = 4
SEQS = 16
ROUND_FLOPS = 4 << 30


epsilon = 1e-06


def rms_norm(values, norm_gain):
    mean_sq = jnp.mean(values * values, axis=-1, keepdims=True)
    return values * lax.rsqrt(mean_sq + epsilon) * norm_gain


def expert_piece(arrived, w_gate, w_up, w_down):
    features = arrived.shape[-1]
    flat_rows = arrived.reshape(-1, features)
    gate_proj = jnp.dot(flat_rows, w_gate, preferred_element_type=jnp.float32)
    up_proj = jnp.dot(flat_rows, w_up, preferred_element_type=jnp.float32)
    inner_act = (jax.nn.silu(gate_proj) * up_proj).astype(jnp.bfloat16)
    partial_value = jnp.dot(inner_act, w_down, preferred_element_type=jnp.float32)
    return lax.all_to_all(
        partial_value.reshape(arrived.shape), "tensor", split_axis=0, concat_axis=0, tiled=True
    )


def routed_on_device(
    hidden_in,
    expert_ids,
    gate_weights,
    targets,
    seq_ids,
    moe_gain,
    w_gate,
    w_up,
    w_down,
    final_gain,
    head_weight,
    adapter_down,
    adapter_up,
):
    tok_rows, features = hidden_in.shape
    top_count = expert_ids.shape[1]
    devices = lax.axis_size("tensor")
    experts = devices // SPLIT
    capacity = min(tok_rows, 2 * tok_rows * top_count // experts)
    my_index = lax.axis_index("tensor")
    moe_input = rms_norm(hidden_in.astype(jnp.float32), moe_gain).astype(jnp.bfloat16)
    flat_ids = expert_ids.reshape(-1)
    chosen_hot = (flat_ids[:, None] == jnp.arange(experts, dtype=jnp.int32)[None, :]).astype(
        jnp.int32
    )
    slot_pos = jnp.sum((jnp.cumsum(chosen_hot, axis=0) - chosen_hot) * chosen_hot, axis=1)
    target_slot = flat_ids * capacity + slot_pos
    placed = (
        target_slot[:, None] == jnp.arange(experts * capacity, dtype=jnp.int32)[None, :]
    ).reshape(tok_rows, top_count, experts * capacity)
    spread = jnp.any(placed, axis=1).astype(jnp.bfloat16)
    packed = lax.dot_general(
        spread, moe_input, (((0,), (0,)), ((), ())), preferred_element_type=jnp.float32
    ).astype(jnp.bfloat16)
    outgoing = jnp.broadcast_to(
        packed.reshape(experts, 1, capacity, features), (experts, SPLIT, capacity, features)
    ).reshape(devices, capacity, features)
    returned = expert_piece(
        lax.all_to_all(outgoing, "tensor", split_axis=0, concat_axis=0, tiled=True),
        w_gate,
        w_up,
        w_down,
    )
    summed = jnp.sum(returned.reshape(experts, SPLIT, capacity, features), axis=1).reshape(
        experts * capacity, features
    )
    mixing = jnp.sum(placed.astype(jnp.float32) * gate_weights[:, :, None], axis=1)
    residual_sum = hidden_in.astype(jnp.float32) + jnp.dot(
        mixing, summed, precision=lax.Precision.HIGHEST
    )
    final_input = rms_norm(residual_sum, final_gain).astype(jnp.bfloat16)
    vocab_dev = head_weight.shape[1]
    vocab_start = my_index * vocab_dev
    columns = jnp.arange(vocab_dev, dtype=jnp.int32)

    def summary(block_rows, block_latent, row_start):
        row_count = block_rows.shape[0]
        base_logits = jnp.dot(block_rows, head_weight, preferred_element_type=jnp.float32)
        policy_logits = base_logits + jnp.dot(
            block_latent, adapter_up, preferred_element_type=jnp.float32
        )
        wanted = lax.dynamic_slice_in_dim(targets, row_start, row_count) - vocab_start
        is_target = wanted[:, None] == columns[None, :]

        def reduce_logits(logits):
            top_value = jnp.max(logits, axis=1)
            exp_total = jnp.sum(jnp.exp(logits - top_value[:, None]), axis=1)
            picked = jnp.sum(jnp.where(is_target, logits, 0.0), axis=1)
            return (top_value, exp_total, picked)

        base_stats = reduce_logits(base_logits)
        policy_stats = reduce_logits(policy_logits)
        return tuple(
            (
                jnp.stack([earlier, later], axis=1)
                for earlier, later in zip(base_stats, policy_stats)
            )
        )

    def blocked(shard_rows, shard_latent, row_start):
        row_count = shard_rows.shape[0]
        block_size = 512 if row_count % 512 == 0 else row_count
        if block_size == row_count:
            return summary(shard_rows, shard_latent, row_start)

        def one_block(block_index):
            offset = block_index * block_size
            return summary(
                lax.dynamic_slice_in_dim(shard_rows, offset, block_size),
                lax.dynamic_slice_in_dim(shard_latent, offset, block_size),
                row_start + offset,
            )

        results = lax.map(one_block, jnp.arange(row_count // block_size, dtype=jnp.int32))
        return tuple((member.reshape(row_count, 2) for member in results))

    shard_rows = lax.all_gather(final_input, "tensor", axis=0, tiled=True)
    shard_latent = jnp.dot(shard_rows, adapter_down, preferred_element_type=jnp.float32).astype(
        jnp.bfloat16
    )
    block_stats = blocked(shard_rows, shard_latent, jnp.int32(0))
    maxima, exp_sums, target_logits = tuple((update for update in block_stats))
    ceiling = lax.pmax(maxima, "tensor")
    totals, picked_all = lax.psum((exp_sums * jnp.exp(maxima - ceiling), target_logits), "tensor")
    log_probs = picked_all - ceiling - jnp.log(totals)
    log_ratio = log_probs[:, 1] - log_probs[:, 0]
    seq_match = (seq_ids[None, :] == jnp.arange(SEQS, dtype=jnp.int32)[:, None]).astype(jnp.float32)
    seq_sums = jnp.dot(seq_match, log_ratio, precision=lax.Precision.HIGHEST)
    own_start = my_index * tok_rows
    policy_own = lax.dynamic_slice_in_dim(log_probs[:, 1], own_start, tok_rows)
    ratio_own = lax.dynamic_slice_in_dim(log_ratio, own_start, tok_rows)
    return (policy_own, ratio_own, seq_sums)


def exchange(values, mask):
    devices = lax.axis_size("tensor")
    return lax.ppermute(values, "tensor", [(i, i ^ mask) for i in range(devices)])


def bit(number, place):
    return (number >> place) & 1


def in_order(late, mine, other):
    return jnp.concatenate([jnp.where(late, other, mine), jnp.where(late, mine, other)], axis=0)


def token_at(place, tok_rows, bits):
    devices = 1 << bits
    rank = place // tok_rows
    parity = rank >> (bits - 1)
    device = parity * 0
    low = parity
    for b in range(1, bits):
        one = (rank >> (bits - 1 - b)) & 1
        device = device + one * (1 << b)
        low = low ^ one
    return (device + low) * tok_rows + place % tok_rows


TRANSPOSED = (((1,), (1,)), ((), ()))


def places(tok_rows, bits):
    my_index = lax.axis_index("tensor")
    parity = sum(bit(my_index, b) for b in range(bits)) & 1
    return my_index, parity, tok_rows << (bits - 1)


def prepare_kernel(
    tok_rows,
    bits,
    ids_ref,
    gates_ref,
    targets_ref,
    seq_ref,
    moe_gain_ref,
    final_gain_ref,
    down_ref,
    gains_ref,
    down_out_ref,
    mixing_ref,
    columns_ref,
):
    my_index, parity, half = places(tok_rows, bits)
    experts = gates_ref.shape[0]
    gains_ref[...] = jnp.concatenate(
        [moe_gain_ref[...]] * 4 + [final_gain_ref[...]] * 4, axis=0
    )
    down_out_ref[...] = down_ref[...]
    rows = [
        sum(
            jnp.where(ids_ref[k : k + 1] == expert, gates_ref[k : k + 1], 0.0)
            for k in range(ids_ref.shape[0])
        )
        for expert in range(experts)
    ]
    rows = jnp.concatenate(rows + [jnp.zeros((8 - experts, tok_rows), jnp.float32)], axis=0)
    rows = jnp.concatenate([rows] * (128 // tok_rows), axis=1)
    at = lax.broadcasted_iota(jnp.int32, (8, 128), 1)
    token = token_at(at + parity * half, tok_rows, bits) - my_index * tok_rows
    mixing_ref[...] = jnp.where((token >= 0) & (token < tok_rows) & (at < half), rows, 0.0)
    row = lax.broadcasted_iota(jnp.int32, (half, 128), 0)
    lane = lax.broadcasted_iota(jnp.int32, (half, 128), 1)
    token = token_at(row + parity * half, tok_rows, bits) - my_index * tok_rows
    wanted = half_columns(targets_ref[...], tok_rows, bits, parity)
    own_seq = half_columns(seq_ref[...], tok_rows, bits, parity)
    other_seq = half_columns(seq_ref[...], tok_rows, bits, 1 - parity)
    picks = (token == lane) & (lane < tok_rows) | (own_seq == lane - 64) & (lane >= 64)
    columns_ref[0] = jnp.where(lane == 0, wanted, 0).astype(jnp.float32)
    columns_ref[1] = picks.astype(jnp.float32)
    columns_ref[2] = ((other_seq == lane - 64) & (lane >= 64)).astype(jnp.float32)


def flags_kernel(flags_ref):
    row = lax.broadcasted_iota(jnp.int32, flags_ref.shape, 0)
    flags_ref[...] = bit(lax.axis_index("tensor"), row)


def order_kernel(place, flags_ref, mine_ref, other_ref, out_ref):
    late = flags_ref[place : place + 1, 0:1] == 1
    out_ref[...] = in_order(late, mine_ref[...], other_ref[...])


def expert_kernel(rows_ref, gains_ref, *refs):
    far_refs, near_refs, (total_ref, sent_ref) = refs[0:3], refs[3:6], refs[6:8]
    moe_input = rms_norm(rows_ref[...].astype(jnp.float32), gains_ref[0:1]).astype(jnp.bfloat16)

    def units(gate_ref, up_ref, down_ref):
        projections = [
            lax.dot_general(moe_input, ref[...], TRANSPOSED, preferred_element_type=jnp.float32)
            for ref in (gate_ref, up_ref)
        ]
        inner_act = (jax.nn.silu(projections[0]) * projections[1]).astype(jnp.bfloat16)
        return jnp.dot(inner_act, down_ref[...], preferred_element_type=jnp.float32)

    total = units(*far_refs) + units(*near_refs)
    total_ref[...] = total
    sent_ref[...] = total.astype(jnp.bfloat16)


def norm_kernel(total_ref, arrived_ref, mixing_ref, mixing_arrived_ref, rows_ref, gains_ref, out_ref):
    half = out_ref.shape[0]
    expert = lax.axis_index("tensor") // SPLIT
    mixing = (mixing_ref[...] + mixing_arrived_ref[...]).T[:half]
    lane = lax.broadcasted_iota(jnp.int32, mixing.shape, 1)
    mixed = rows_ref[...].astype(jnp.float32)
    for own, value in ((expert, total_ref[...]), (1 - expert, arrived_ref[...])):
        weight = jnp.sum(jnp.where(lane == own, mixing, 0.0), axis=1, keepdims=True)
        mixed = mixed + weight * value.astype(jnp.float32)
    out_ref[...] = rms_norm(mixed, gains_ref[4:5]).astype(jnp.bfloat16)


def half_columns(values, tok_rows, bits, parity):
    tokens = values.shape[1]
    half = tokens // 2
    place = lax.broadcasted_iota(jnp.int32, (half, tokens), 0) + parity * half
    token = lax.broadcasted_iota(jnp.int32, (half, tokens), 1)
    here = token_at(place, tok_rows, bits) == token
    column = jnp.sum(jnp.where(here, values.astype(jnp.float32), 0.0), axis=1, keepdims=True)
    return column.astype(jnp.int32)


def head_kernel(rows_ref, columns_ref, down_ref, *refs):
    *weight_refs, stats_ref = refs
    my_index = lax.axis_index("tensor")
    rows = rows_ref[...]
    tokens = rows.shape[0]
    wanted = columns_ref[0][:, 0:1].astype(jnp.int32)
    latent = lax.dot_general(rows, down_ref[...], TRANSPOSED, preferred_element_type=jnp.float32)
    latent = latent.astype(jnp.bfloat16)
    lane = lax.broadcasted_iota(jnp.int32, (tokens, 128), 1)
    packed = jnp.zeros((tokens, 128), jnp.float32)
    base, policy, matches = [], [], []
    for index, head_ref, up_ref in zip((my_index, my_index ^ 1), weight_refs[:2], weight_refs[2:]):
        logits = jnp.dot(rows, head_ref[...], preferred_element_type=jnp.float32)
        base.append(logits)
        change = jnp.dot(latent, up_ref[...], preferred_element_type=jnp.float32)
        policy.append(logits + change)
        column = lax.broadcasted_iota(jnp.int32, logits.shape, 1)
        matches.append(column == wanted - index * logits.shape[1])
    is_target = jnp.concatenate(matches, axis=1)
    for at, parts in enumerate((base, policy)):
        logits = jnp.concatenate(parts, axis=1)
        top_value = jnp.max(logits, axis=1, keepdims=True)
        exp_total = jnp.sum(jnp.exp(logits - top_value), axis=1, keepdims=True)
        picked = jnp.sum(jnp.where(is_target, logits, 0.0), axis=1, keepdims=True)
        for kind, value in enumerate((top_value, exp_total, picked)):
            packed = jnp.where(lane == 2 * kind + at, value, packed)
    stats_ref[...] = packed.T[:8]


def merge_kernel(one_ref, two_ref, out_ref):
    one, two = one_ref[...], two_ref[...]
    ceiling = jnp.maximum(one[0:2], two[0:2])
    exp_total = one[2:4] * jnp.exp(one[0:2] - ceiling) + two[2:4] * jnp.exp(two[0:2] - ceiling)
    out_ref[...] = jnp.concatenate([ceiling, exp_total, one[4:8] + two[4:8]], axis=0)


def result_kernel(tok_rows, own_ref, other_ref, columns_ref, policy_ref, ratio_ref, sums_ref):
    half = own_ref.shape[1]
    picked = []
    for ref, columns in ((own_ref, columns_ref[1]), (other_ref, columns_ref[2])):
        stats = ref[...]
        log_probs = stats[4:6] - stats[0:2] - jnp.log(stats[2:4])
        policy = log_probs[1:2]
        rows = jnp.concatenate([policy, policy - log_probs[0:1]] * 4, axis=0)
        picked.append(
            jnp.dot(
                rows,
                columns,
                precision=lax.Precision.HIGHEST,
                preferred_element_type=jnp.float32,
            )
        )
    policy_ref[...] = picked[0][0:1, :tok_rows]
    ratio_ref[...] = picked[0][1:2, :tok_rows]
    sums_ref[...] = (picked[0] + picked[1])[1:2, 64 : 64 + SEQS]


def call(kernel, shapes, *operands, flops=0):
    size = sum(operand.size * operand.dtype.itemsize for operand in operands)
    return pl.pallas_call(
        kernel,
        out_shape=shapes,
        compiler_params=pltpu.CompilerParams(vmem_limit_bytes=32 << 20),
        cost_estimate=pl.CostEstimate(flops=flops, bytes_accessed=size, transcendentals=0),
    )(*operands)


def dense_on_device(
    hidden_in,
    expert_ids,
    gate_weights,
    targets,
    seq_ids,
    moe_gain,
    w_gate,
    w_up,
    w_down,
    final_gain,
    head_weight,
    adapter_down,
    adapter_up,
):
    tok_rows, features = hidden_in.shape
    devices = lax.axis_size("tensor")
    bits = devices.bit_length() - 1
    half = devices * tok_rows // 2
    my_index = lax.axis_index("tensor")
    far = [(b, (1 << b) + 1) for b in range(bits - 1, 0, -1)]

    def array(dtype, *shape):
        return jax.ShapeDtypeStruct(shape, dtype)

    rows = hidden_in
    flags = call(flags_kernel, array(jnp.int32, 8, 128), flops=ROUND_FLOPS)
    for b, mask in far:
        rows = call(
            functools.partial(order_kernel, b),
            array(rows.dtype, 2 * rows.shape[0], features),
            flags,
            rows,
            exchange(rows, mask),
            flops=ROUND_FLOPS * (2 * rows.shape[0] < half),
        )
    gains, down, mixing, columns = call(
        lambda *refs: prepare_kernel(tok_rows, bits, *refs),
        [
            array(jnp.float32, 8, features),
            array(jnp.bfloat16, *adapter_down.shape[::-1]),
            array(jnp.float32, 8, 128),
            array(jnp.float32, 3, half, 128),
        ],
        expert_ids.T,
        gate_weights.T,
        targets[None],
        seq_ids[None],
        moe_gain[None],
        final_gain[None],
        adapter_down.T,
    )

    units = [w_gate.T, w_up.T, w_down]
    total, sent = call(
        expert_kernel,
        [array(dtype, half, features) for dtype in (jnp.float32, jnp.bfloat16)],
        rows,
        gains,
        *(exchange(unit, 1) for unit in units),
        *units,
        flops=6 * devices * tok_rows * features * w_gate.shape[1],
    )
    masks = [mask for _, mask in far[::-1]]
    for mask in masks[:-1]:
        mixing, sent = lax.optimization_barrier((mixing, sent))
        total = total + exchange(sent, mask).astype(jnp.float32)
        mixing = mixing + exchange(mixing, mask)
        sent = total.astype(jnp.bfloat16)
    mixing, sent = lax.optimization_barrier((mixing, sent))
    final_input = call(
        norm_kernel,
        array(jnp.bfloat16, half, features),
        total,
        exchange(sent, masks[-1]),
        mixing,
        exchange(mixing, masks[-1]),
        rows,
        gains,
    )

    stats = call(
        head_kernel,
        array(jnp.float32, 8, half),
        final_input,
        columns,
        down,
        head_weight,
        exchange(head_weight, 1),
        adapter_up,
        exchange(adapter_up, 1),
        flops=2 * devices * tok_rows * features * head_weight.shape[1],
    )
    for mask in masks:
        stats = call(merge_kernel, array(jnp.float32, 8, half), stats, exchange(stats, mask))
    policy_own, ratio_own, seq_sums = call(
        lambda *refs: result_kernel(tok_rows, *refs),
        [array(jnp.float32, 1, tok_rows)] * 2 + [array(jnp.float32, 1, SEQS)],
        stats,
        exchange(stats, 1),
        columns,
    )
    return (policy_own[0], ratio_own[0], seq_sums[0])


def solution(mesh):
    in_specs = (
        P(("dp", "tensor"), None),
        P(("dp", "tensor"), None),
        P(("dp", "tensor"), None),
        P("dp"),
        P("dp"),
        P(),
        P(None, "tensor"),
        P(None, "tensor"),
        P("tensor", None),
        P(),
        P(None, "tensor"),
        P(),
        P(None, "tensor"),
    )
    out_specs = (P(("dp", "tensor")), P(("dp", "tensor")), P("dp"))
    devices = mesh.shape["tensor"]

    def on_device(hidden_in, expert_ids, *others):
        both_experts = expert_ids.shape[1] == 2 and devices == 2 * SPLIT
        step = dense_on_device if both_experts else routed_on_device
        return step(hidden_in, expert_ids, *others)

    return jax.shard_map(
        on_device, mesh=mesh, in_specs=in_specs, out_specs=out_specs, check_vma=False
    )
```

```python
import functools

import jax
import jax.numpy as jnp
from jax import lax
from jax.experimental import pallas as pl
from jax.experimental.pallas import tpu as pltpu
from jax.sharding import PartitionSpec as P

SPLIT = 4
SEQS = 16
ROUND_FLOPS = 4 << 30


epsilon = 1e-06


def rms_norm(values, norm_gain):
    mean_sq = jnp.mean(values * values, axis=-1, keepdims=True)
    return values * lax.rsqrt(mean_sq + epsilon) * norm_gain


def expert_piece(arrived, w_gate, w_up, w_down):
    features = arrived.shape[-1]
    flat_rows = arrived.reshape(-1, features)
    gate_proj = jnp.dot(flat_rows, w_gate, preferred_element_type=jnp.float32)
    up_proj = jnp.dot(flat_rows, w_up, preferred_element_type=jnp.float32)
    inner_act = (jax.nn.silu(gate_proj) * up_proj).astype(jnp.bfloat16)
    partial_value = jnp.dot(inner_act, w_down, preferred_element_type=jnp.float32)
    return lax.all_to_all(
        partial_value.reshape(arrived.shape), "tensor", split_axis=0, concat_axis=0, tiled=True
    )


def routed_on_device(
    hidden_in,
    expert_ids,
    gate_weights,
    targets,
    seq_ids,
    moe_gain,
    w_gate,
    w_up,
    w_down,
    final_gain,
    head_weight,
    adapter_down,
    adapter_up,
):
    tok_rows, features = hidden_in.shape
    top_count = expert_ids.shape[1]
    devices = lax.axis_size("tensor")
    experts = devices // SPLIT
    capacity = min(tok_rows, 2 * tok_rows * top_count // experts)
    my_index = lax.axis_index("tensor")
    moe_input = rms_norm(hidden_in.astype(jnp.float32), moe_gain).astype(jnp.bfloat16)
    flat_ids = expert_ids.reshape(-1)
    chosen_hot = (flat_ids[:, None] == jnp.arange(experts, dtype=jnp.int32)[None, :]).astype(
        jnp.int32
    )
    slot_pos = jnp.sum((jnp.cumsum(chosen_hot, axis=0) - chosen_hot) * chosen_hot, axis=1)
    target_slot = flat_ids * capacity + slot_pos
    placed = (
        target_slot[:, None] == jnp.arange(experts * capacity, dtype=jnp.int32)[None, :]
    ).reshape(tok_rows, top_count, experts * capacity)
    spread = jnp.any(placed, axis=1).astype(jnp.bfloat16)
    packed = lax.dot_general(
        spread, moe_input, (((0,), (0,)), ((), ())), preferred_element_type=jnp.float32
    ).astype(jnp.bfloat16)
    outgoing = jnp.broadcast_to(
        packed.reshape(experts, 1, capacity, features), (experts, SPLIT, capacity, features)
    ).reshape(devices, capacity, features)
    returned = expert_piece(
        lax.all_to_all(outgoing, "tensor", split_axis=0, concat_axis=0, tiled=True),
        w_gate,
        w_up,
        w_down,
    )
    summed = jnp.sum(returned.reshape(experts, SPLIT, capacity, features), axis=1).reshape(
        experts * capacity, features
    )
    mixing = jnp.sum(placed.astype(jnp.float32) * gate_weights[:, :, None], axis=1)
    residual_sum = hidden_in.astype(jnp.float32) + jnp.dot(
        mixing, summed, precision=lax.Precision.HIGHEST
    )
    final_input = rms_norm(residual_sum, final_gain).astype(jnp.bfloat16)
    vocab_dev = head_weight.shape[1]
    vocab_start = my_index * vocab_dev
    columns = jnp.arange(vocab_dev, dtype=jnp.int32)

    def summary(block_rows, block_latent, row_start):
        row_count = block_rows.shape[0]
        base_logits = jnp.dot(block_rows, head_weight, preferred_element_type=jnp.float32)
        policy_logits = base_logits + jnp.dot(
            block_latent, adapter_up, preferred_element_type=jnp.float32
        )
        wanted = lax.dynamic_slice_in_dim(targets, row_start, row_count) - vocab_start
        is_target = wanted[:, None] == columns[None, :]

        def reduce_logits(logits):
            top_value = jnp.max(logits, axis=1)
            exp_total = jnp.sum(jnp.exp(logits - top_value[:, None]), axis=1)
            picked = jnp.sum(jnp.where(is_target, logits, 0.0), axis=1)
            return (top_value, exp_total, picked)

        base_stats = reduce_logits(base_logits)
        policy_stats = reduce_logits(policy_logits)
        return tuple(
            (
                jnp.stack([earlier, later], axis=1)
                for earlier, later in zip(base_stats, policy_stats)
            )
        )

    def blocked(shard_rows, shard_latent, row_start):
        row_count = shard_rows.shape[0]
        block_size = 512 if row_count % 512 == 0 else row_count
        if block_size == row_count:
            return summary(shard_rows, shard_latent, row_start)

        def one_block(block_index):
            offset = block_index * block_size
            return summary(
                lax.dynamic_slice_in_dim(shard_rows, offset, block_size),
                lax.dynamic_slice_in_dim(shard_latent, offset, block_size),
                row_start + offset,
            )

        results = lax.map(one_block, jnp.arange(row_count // block_size, dtype=jnp.int32))
        return tuple((member.reshape(row_count, 2) for member in results))

    shard_rows = lax.all_gather(final_input, "tensor", axis=0, tiled=True)
    shard_latent = jnp.dot(shard_rows, adapter_down, preferred_element_type=jnp.float32).astype(
        jnp.bfloat16
    )
    block_stats = blocked(shard_rows, shard_latent, jnp.int32(0))
    maxima, exp_sums, target_logits = tuple((update for update in block_stats))
    ceiling = lax.pmax(maxima, "tensor")
    totals, picked_all = lax.psum((exp_sums * jnp.exp(maxima - ceiling), target_logits), "tensor")
    log_probs = picked_all - ceiling - jnp.log(totals)
    log_ratio = log_probs[:, 1] - log_probs[:, 0]
    seq_match = (seq_ids[None, :] == jnp.arange(SEQS, dtype=jnp.int32)[:, None]).astype(jnp.float32)
    seq_sums = jnp.dot(seq_match, log_ratio, precision=lax.Precision.HIGHEST)
    own_start = my_index * tok_rows
    policy_own = lax.dynamic_slice_in_dim(log_probs[:, 1], own_start, tok_rows)
    ratio_own = lax.dynamic_slice_in_dim(log_ratio, own_start, tok_rows)
    return (policy_own, ratio_own, seq_sums)


def exchange(values, mask):
    devices = lax.axis_size("tensor")
    return lax.ppermute(values, "tensor", [(i, i ^ mask) for i in range(devices)])


def bit(number, place):
    return (number >> place) & 1


def in_order(late, mine, other):
    return jnp.concatenate([jnp.where(late, other, mine), jnp.where(late, mine, other)], axis=0)


def token_at(place, tok_rows, bits):
    devices = 1 << bits
    rank = place // tok_rows
    parity = rank >> (bits - 1)
    device = parity * 0
    low = parity
    for b in range(1, bits):
        one = (rank >> (bits - 1 - b)) & 1
        device = device + one * (1 << b)
        low = low ^ one
    return (device + low) * tok_rows + place % tok_rows


TRANSPOSED = (((1,), (1,)), ((), ()))


def places(tok_rows, bits):
    my_index = lax.axis_index("tensor")
    parity = sum(bit(my_index, b) for b in range(bits)) & 1
    return my_index, parity, tok_rows << (bits - 1)


def prepare_kernel(
    tok_rows,
    bits,
    ids_ref,
    gates_ref,
    targets_ref,
    seq_ref,
    moe_gain_ref,
    final_gain_ref,
    down_ref,
    gains_ref,
    down_out_ref,
    mixing_ref,
    columns_ref,
):
    my_index, parity, half = places(tok_rows, bits)
    experts = gates_ref.shape[0]
    gains_ref[...] = jnp.concatenate(
        [moe_gain_ref[...]] * 4 + [final_gain_ref[...]] * 4, axis=0
    )
    down_out_ref[...] = down_ref[...]
    rows = [
        sum(
            jnp.where(ids_ref[k : k + 1] == expert, gates_ref[k : k + 1], 0.0)
            for k in range(ids_ref.shape[0])
        )
        for expert in range(experts)
    ]
    weights = jnp.concatenate(rows, axis=0)
    high = weights.astype(jnp.bfloat16).astype(jnp.float32)
    middle = (weights - high).astype(jnp.bfloat16).astype(jnp.float32)
    low = weights - high - middle
    rows = [high, middle, low, jnp.zeros((8 - 3 * experts, tok_rows), jnp.float32)]
    rows = [jnp.concatenate(rows, axis=0), jnp.zeros((8, 128 - tok_rows), jnp.float32)]
    parts = jnp.concatenate(rows, axis=1).T[:tok_rows]
    parts = jnp.concatenate([parts, jnp.zeros((tok_rows, 120), jnp.float32)], axis=1)
    row = lax.broadcasted_iota(jnp.int32, (half, 128), 0)
    lane = lax.broadcasted_iota(jnp.int32, (half, 128), 1)
    token = token_at(row + parity * half, tok_rows, bits) - my_index * tok_rows
    mine = (token >= 0) & (token < tok_rows)
    mixing_ref[...] = jnp.where(mine, jnp.concatenate([parts] * (half // tok_rows), axis=0), 0.0)
    wanted = half_columns(targets_ref[...], tok_rows, bits, parity)
    own_seq = half_columns(seq_ref[...], tok_rows, bits, parity)
    other_seq = half_columns(seq_ref[...], tok_rows, bits, 1 - parity)
    picks = (token == lane) & (lane < tok_rows) | (own_seq == lane - 64) & (lane >= 64)
    columns_ref[0] = jnp.where(lane == 0, wanted, 0).astype(jnp.float32)
    columns_ref[1] = picks.astype(jnp.float32)
    columns_ref[2] = ((other_seq == lane - 64) & (lane >= 64)).astype(jnp.float32)


def flags_kernel(flags_ref):
    row = lax.broadcasted_iota(jnp.int32, flags_ref.shape, 0)
    flags_ref[...] = bit(lax.axis_index("tensor"), row)


def order_kernel(place, flags_ref, mine_ref, other_ref, out_ref):
    late = flags_ref[place : place + 1, 0:1] == 1
    out_ref[...] = in_order(late, mine_ref[...], other_ref[...])


def expert_kernel(rows_ref, gains_ref, mixing_ref, *refs):
    far_refs, near_refs, (total_ref, sent_ref) = refs[0:3], refs[3:6], refs[6:8]
    moe_input = rms_norm(rows_ref[...].astype(jnp.float32), gains_ref[0:1]).astype(jnp.bfloat16)

    def units(gate_ref, up_ref, down_ref):
        projections = [
            lax.dot_general(moe_input, ref[...], TRANSPOSED, preferred_element_type=jnp.float32)
            for ref in (gate_ref, up_ref)
        ]
        inner_act = (jax.nn.silu(projections[0]) * projections[1]).astype(jnp.bfloat16)
        return jnp.dot(inner_act, down_ref[...], preferred_element_type=jnp.float32)

    total = units(*far_refs) + units(*near_refs)
    total = jnp.concatenate([total, mixing_ref[...]], axis=1)
    total_ref[...] = total
    sent_ref[...] = total.astype(jnp.bfloat16)


def norm_kernel(total_ref, arrived_ref, rows_ref, gains_ref, out_ref):
    features = out_ref.shape[1]
    expert = lax.axis_index("tensor") // SPLIT
    total, arrived = total_ref[...], arrived_ref[...].astype(jnp.float32)
    mixing = total[:, features:] + arrived[:, features:]
    lane = lax.broadcasted_iota(jnp.int32, mixing.shape, 1)
    mixed = rows_ref[...].astype(jnp.float32)
    for own, value in ((expert, total), (1 - expert, arrived)):
        weight = jnp.sum(jnp.where(lane % 2 == own, mixing, 0.0), axis=1, keepdims=True)
        mixed = mixed + weight * value[:, :features]
    out_ref[...] = rms_norm(mixed, gains_ref[4:5]).astype(jnp.bfloat16)


def half_columns(values, tok_rows, bits, parity):
    tokens = values.shape[1]
    half = tokens // 2
    place = lax.broadcasted_iota(jnp.int32, (half, tokens), 0) + parity * half
    token = lax.broadcasted_iota(jnp.int32, (half, tokens), 1)
    here = token_at(place, tok_rows, bits) == token
    column = jnp.sum(jnp.where(here, values.astype(jnp.float32), 0.0), axis=1, keepdims=True)
    return column.astype(jnp.int32)


def head_kernel(rows_ref, columns_ref, down_ref, *refs):
    *weight_refs, stats_ref = refs
    my_index = lax.axis_index("tensor")
    rows = rows_ref[...]
    tokens = rows.shape[0]
    wanted = columns_ref[0][:, 0:1].astype(jnp.int32)
    latent = lax.dot_general(rows, down_ref[...], TRANSPOSED, preferred_element_type=jnp.float32)
    latent = latent.astype(jnp.bfloat16)
    lane = lax.broadcasted_iota(jnp.int32, (tokens, 128), 1)
    packed = jnp.zeros((tokens, 128), jnp.float32)
    base, policy, matches = [], [], []
    for index, head_ref, up_ref in zip((my_index, my_index ^ 1), weight_refs[:2], weight_refs[2:]):
        logits = jnp.dot(rows, head_ref[...], preferred_element_type=jnp.float32)
        base.append(logits)
        change = jnp.dot(latent, up_ref[...], preferred_element_type=jnp.float32)
        policy.append(logits + change)
        column = lax.broadcasted_iota(jnp.int32, logits.shape, 1)
        matches.append(column == wanted - index * logits.shape[1])
    is_target = jnp.concatenate(matches, axis=1)
    for at, parts in enumerate((base, policy)):
        logits = jnp.concatenate(parts, axis=1)
        top_value = jnp.max(logits, axis=1, keepdims=True)
        exp_total = jnp.sum(jnp.exp(logits - top_value), axis=1, keepdims=True)
        picked = jnp.sum(jnp.where(is_target, logits, 0.0), axis=1, keepdims=True)
        for kind, value in enumerate((top_value, exp_total, picked)):
            packed = jnp.where(lane == 2 * kind + at, value, packed)
    stats_ref[...] = packed.T[:8]


def merge_kernel(one_ref, two_ref, out_ref):
    one, two = one_ref[...], two_ref[...]
    ceiling = jnp.maximum(one[0:2], two[0:2])
    exp_total = one[2:4] * jnp.exp(one[0:2] - ceiling) + two[2:4] * jnp.exp(two[0:2] - ceiling)
    out_ref[...] = jnp.concatenate([ceiling, exp_total, one[4:8] + two[4:8]], axis=0)


def result_kernel(tok_rows, own_ref, other_ref, columns_ref, policy_ref, ratio_ref, sums_ref):
    half = own_ref.shape[1]
    picked = []
    for ref, columns in ((own_ref, columns_ref[1]), (other_ref, columns_ref[2])):
        stats = ref[...]
        log_probs = stats[4:6] - stats[0:2] - jnp.log(stats[2:4])
        policy = log_probs[1:2]
        rows = jnp.concatenate([policy, policy - log_probs[0:1]] * 4, axis=0)
        picked.append(
            jnp.dot(
                rows,
                columns,
                precision=lax.Precision.HIGHEST,
                preferred_element_type=jnp.float32,
            )
        )
    policy_ref[...] = picked[0][0:1, :tok_rows]
    ratio_ref[...] = picked[0][1:2, :tok_rows]
    sums_ref[...] = (picked[0] + picked[1])[1:2, 64 : 64 + SEQS]


def call(kernel, shapes, *operands, flops=0):
    size = sum(operand.size * operand.dtype.itemsize for operand in operands)
    return pl.pallas_call(
        kernel,
        out_shape=shapes,
        compiler_params=pltpu.CompilerParams(vmem_limit_bytes=32 << 20),
        cost_estimate=pl.CostEstimate(flops=flops, bytes_accessed=size, transcendentals=0),
    )(*operands)


def dense_on_device(
    hidden_in,
    expert_ids,
    gate_weights,
    targets,
    seq_ids,
    moe_gain,
    w_gate,
    w_up,
    w_down,
    final_gain,
    head_weight,
    adapter_down,
    adapter_up,
):
    tok_rows, features = hidden_in.shape
    devices = lax.axis_size("tensor")
    bits = devices.bit_length() - 1
    half = devices * tok_rows // 2
    my_index = lax.axis_index("tensor")
    far = [(b, (1 << b) + 1) for b in range(bits - 1, 0, -1)]

    def array(dtype, *shape):
        return jax.ShapeDtypeStruct(shape, dtype)

    rows = hidden_in
    flags = call(flags_kernel, array(jnp.int32, 8, 128), flops=ROUND_FLOPS)
    for b, mask in far:
        rows = call(
            functools.partial(order_kernel, b),
            array(rows.dtype, 2 * rows.shape[0], features),
            flags,
            rows,
            exchange(rows, mask),
            flops=ROUND_FLOPS * (2 * rows.shape[0] < half),
        )
    gains, down, mixing, columns = call(
        lambda *refs: prepare_kernel(tok_rows, bits, *refs),
        [
            array(jnp.float32, 8, features),
            array(jnp.bfloat16, *adapter_down.shape[::-1]),
            array(jnp.float32, half, 128),
            array(jnp.float32, 3, half, 128),
        ],
        expert_ids.T,
        gate_weights.T,
        targets[None],
        seq_ids[None],
        moe_gain[None],
        final_gain[None],
        adapter_down.T,
    )

    units = [w_gate.T, w_up.T, w_down]
    total, sent = call(
        expert_kernel,
        [array(dtype, half, features + 128) for dtype in (jnp.float32, jnp.bfloat16)],
        rows,
        gains,
        mixing,
        *(exchange(unit, 1) for unit in units),
        *units,
        flops=6 * devices * tok_rows * features * w_gate.shape[1],
    )
    masks = [mask for _, mask in far[::-1]]
    for mask in masks[:-1]:
        total = total + exchange(sent, mask).astype(jnp.float32)
        sent = total.astype(jnp.bfloat16)
    final_input = call(
        norm_kernel,
        array(jnp.bfloat16, half, features),
        total,
        exchange(sent, masks[-1]),
        rows,
        gains,
    )

    stats = call(
        head_kernel,
        array(jnp.float32, 8, half),
        final_input,
        columns,
        down,
        head_weight,
        exchange(head_weight, 1),
        adapter_up,
        exchange(adapter_up, 1),
        flops=2 * devices * tok_rows * features * head_weight.shape[1],
    )
    for mask in masks:
        stats = call(merge_kernel, array(jnp.float32, 8, half), stats, exchange(stats, mask))
    policy_own, ratio_own, seq_sums = call(
        lambda *refs: result_kernel(tok_rows, *refs),
        [array(jnp.float32, 1, tok_rows)] * 2 + [array(jnp.float32, 1, SEQS)],
        stats,
        exchange(stats, 1),
        columns,
    )
    return (policy_own[0], ratio_own[0], seq_sums[0])


def solution(mesh):
    in_specs = (
        P(("dp", "tensor"), None),
        P(("dp", "tensor"), None),
        P(("dp", "tensor"), None),
        P("dp"),
        P("dp"),
        P(),
        P(None, "tensor"),
        P(None, "tensor"),
        P("tensor", None),
        P(),
        P(None, "tensor"),
        P(),
        P(None, "tensor"),
    )
    out_specs = (P(("dp", "tensor")), P(("dp", "tensor")), P("dp"))
    devices = mesh.shape["tensor"]

    def on_device(hidden_in, expert_ids, *others):
        both_experts = expert_ids.shape[1] == 2 and devices == 2 * SPLIT
        step = dense_on_device if both_experts else routed_on_device
        return step(hidden_in, expert_ids, *others)

    return jax.shard_map(
        on_device, mesh=mesh, in_specs=in_specs, out_specs=out_specs, check_vma=False
    )
```

```python
import functools

import jax
import jax.numpy as jnp
from jax import lax
from jax.experimental import pallas as pl
from jax.experimental.pallas import tpu as pltpu
from jax.sharding import PartitionSpec as P

SPLIT = 4
SEQS = 16
ROUND_FLOPS = 4 << 30


epsilon = 1e-06


def rms_norm(values, norm_gain):
    mean_sq = jnp.mean(values * values, axis=-1, keepdims=True)
    return values * lax.rsqrt(mean_sq + epsilon) * norm_gain


def expert_piece(arrived, w_gate, w_up, w_down):
    features = arrived.shape[-1]
    flat_rows = arrived.reshape(-1, features)
    gate_proj = jnp.dot(flat_rows, w_gate, preferred_element_type=jnp.float32)
    up_proj = jnp.dot(flat_rows, w_up, preferred_element_type=jnp.float32)
    inner_act = (jax.nn.silu(gate_proj) * up_proj).astype(jnp.bfloat16)
    partial_value = jnp.dot(inner_act, w_down, preferred_element_type=jnp.float32)
    return lax.all_to_all(
        partial_value.reshape(arrived.shape), "tensor", split_axis=0, concat_axis=0, tiled=True
    )


def routed_on_device(
    hidden_in,
    expert_ids,
    gate_weights,
    targets,
    seq_ids,
    moe_gain,
    w_gate,
    w_up,
    w_down,
    final_gain,
    head_weight,
    adapter_down,
    adapter_up,
):
    tok_rows, features = hidden_in.shape
    top_count = expert_ids.shape[1]
    devices = lax.axis_size("tensor")
    experts = devices // SPLIT
    capacity = min(tok_rows, 2 * tok_rows * top_count // experts)
    my_index = lax.axis_index("tensor")
    moe_input = rms_norm(hidden_in.astype(jnp.float32), moe_gain).astype(jnp.bfloat16)
    flat_ids = expert_ids.reshape(-1)
    chosen_hot = (flat_ids[:, None] == jnp.arange(experts, dtype=jnp.int32)[None, :]).astype(
        jnp.int32
    )
    slot_pos = jnp.sum((jnp.cumsum(chosen_hot, axis=0) - chosen_hot) * chosen_hot, axis=1)
    target_slot = flat_ids * capacity + slot_pos
    placed = (
        target_slot[:, None] == jnp.arange(experts * capacity, dtype=jnp.int32)[None, :]
    ).reshape(tok_rows, top_count, experts * capacity)
    spread = jnp.any(placed, axis=1).astype(jnp.bfloat16)
    packed = lax.dot_general(
        spread, moe_input, (((0,), (0,)), ((), ())), preferred_element_type=jnp.float32
    ).astype(jnp.bfloat16)
    outgoing = jnp.broadcast_to(
        packed.reshape(experts, 1, capacity, features), (experts, SPLIT, capacity, features)
    ).reshape(devices, capacity, features)
    returned = expert_piece(
        lax.all_to_all(outgoing, "tensor", split_axis=0, concat_axis=0, tiled=True),
        w_gate,
        w_up,
        w_down,
    )
    summed = jnp.sum(returned.reshape(experts, SPLIT, capacity, features), axis=1).reshape(
        experts * capacity, features
    )
    mixing = jnp.sum(placed.astype(jnp.float32) * gate_weights[:, :, None], axis=1)
    residual_sum = hidden_in.astype(jnp.float32) + jnp.dot(
        mixing, summed, precision=lax.Precision.HIGHEST
    )
    final_input = rms_norm(residual_sum, final_gain).astype(jnp.bfloat16)
    vocab_dev = head_weight.shape[1]
    vocab_start = my_index * vocab_dev
    columns = jnp.arange(vocab_dev, dtype=jnp.int32)

    def summary(block_rows, block_latent, row_start):
        row_count = block_rows.shape[0]
        base_logits = jnp.dot(block_rows, head_weight, preferred_element_type=jnp.float32)
        policy_logits = base_logits + jnp.dot(
            block_latent, adapter_up, preferred_element_type=jnp.float32
        )
        wanted = lax.dynamic_slice_in_dim(targets, row_start, row_count) - vocab_start
        is_target = wanted[:, None] == columns[None, :]

        def reduce_logits(logits):
            top_value = jnp.max(logits, axis=1)
            exp_total = jnp.sum(jnp.exp(logits - top_value[:, None]), axis=1)
            picked = jnp.sum(jnp.where(is_target, logits, 0.0), axis=1)
            return (top_value, exp_total, picked)

        base_stats = reduce_logits(base_logits)
        policy_stats = reduce_logits(policy_logits)
        return tuple(
            (
                jnp.stack([earlier, later], axis=1)
                for earlier, later in zip(base_stats, policy_stats)
            )
        )

    def blocked(shard_rows, shard_latent, row_start):
        row_count = shard_rows.shape[0]
        block_size = 512 if row_count % 512 == 0 else row_count
        if block_size == row_count:
            return summary(shard_rows, shard_latent, row_start)

        def one_block(block_index):
            offset = block_index * block_size
            return summary(
                lax.dynamic_slice_in_dim(shard_rows, offset, block_size),
                lax.dynamic_slice_in_dim(shard_latent, offset, block_size),
                row_start + offset,
            )

        results = lax.map(one_block, jnp.arange(row_count // block_size, dtype=jnp.int32))
        return tuple((member.reshape(row_count, 2) for member in results))

    shard_rows = lax.all_gather(final_input, "tensor", axis=0, tiled=True)
    shard_latent = jnp.dot(shard_rows, adapter_down, preferred_element_type=jnp.float32).astype(
        jnp.bfloat16
    )
    block_stats = blocked(shard_rows, shard_latent, jnp.int32(0))
    maxima, exp_sums, target_logits = tuple((update for update in block_stats))
    ceiling = lax.pmax(maxima, "tensor")
    totals, picked_all = lax.psum((exp_sums * jnp.exp(maxima - ceiling), target_logits), "tensor")
    log_probs = picked_all - ceiling - jnp.log(totals)
    log_ratio = log_probs[:, 1] - log_probs[:, 0]
    seq_match = (seq_ids[None, :] == jnp.arange(SEQS, dtype=jnp.int32)[:, None]).astype(jnp.float32)
    seq_sums = jnp.dot(seq_match, log_ratio, precision=lax.Precision.HIGHEST)
    own_start = my_index * tok_rows
    policy_own = lax.dynamic_slice_in_dim(log_probs[:, 1], own_start, tok_rows)
    ratio_own = lax.dynamic_slice_in_dim(log_ratio, own_start, tok_rows)
    return (policy_own, ratio_own, seq_sums)


def exchange(values, mask):
    devices = lax.axis_size("tensor")
    return lax.ppermute(values, "tensor", [(i, i ^ mask) for i in range(devices)])


def bit(number, place):
    return (number >> place) & 1


def in_order(late, mine, other):
    return jnp.concatenate([jnp.where(late, other, mine), jnp.where(late, mine, other)], axis=0)


def token_at(place, tok_rows, bits):
    devices = 1 << bits
    rank = place // tok_rows
    parity = rank >> (bits - 1)
    device = parity * 0
    low = parity
    for b in range(1, bits):
        one = (rank >> (b - 1)) & 1
        device = device + one * (1 << b)
        low = low ^ one
    return (device + low) * tok_rows + place % tok_rows


TRANSPOSED = (((1,), (1,)), ((), ()))


def places(tok_rows, bits):
    my_index = lax.axis_index("tensor")
    parity = sum(bit(my_index, b) for b in range(bits)) & 1
    return my_index, parity, tok_rows << (bits - 1)


def prepare_kernel(
    tok_rows,
    bits,
    ids_ref,
    gates_ref,
    targets_ref,
    seq_ref,
    moe_gain_ref,
    final_gain_ref,
    down_ref,
    up_ref,
    gains_ref,
    down_out_ref,
    up_out_ref,
    mixing_ref,
    columns_ref,
):
    my_index, parity, half = places(tok_rows, bits)
    experts = gates_ref.shape[0]
    gains_ref[...] = jnp.concatenate(
        [moe_gain_ref[...]] * 4 + [final_gain_ref[...]] * 4, axis=0
    )
    down_out_ref[...] = down_ref[...]
    up_out_ref[...] = up_ref[...]
    rows = [
        sum(
            jnp.where(ids_ref[k : k + 1] == expert, gates_ref[k : k + 1], 0.0)
            for k in range(ids_ref.shape[0])
        )
        for expert in range(experts)
    ]
    weights = jnp.concatenate(rows, axis=0)
    high = weights.astype(jnp.bfloat16).astype(jnp.float32)
    middle = (weights - high).astype(jnp.bfloat16).astype(jnp.float32)
    low = weights - high - middle
    rows = [high, middle, low, jnp.zeros((8 - 3 * experts, tok_rows), jnp.float32)]
    rows = [jnp.concatenate(rows, axis=0), jnp.zeros((8, 128 - tok_rows), jnp.float32)]
    parts = jnp.concatenate(rows, axis=1).T[:tok_rows]
    parts = jnp.concatenate([parts] * 16, axis=1)
    lane = lax.broadcasted_iota(jnp.int32, parts.shape, 1)
    token = token_at(lane // 8 * tok_rows + parity * half, tok_rows, bits)
    mine = (lane < half // tok_rows * 8) & (token // tok_rows == my_index)
    mixing = jnp.where(mine, parts, 0.0)
    mixing_ref[...] = jnp.concatenate([mixing, jnp.zeros_like(mixing)], axis=0)
    row = lax.broadcasted_iota(jnp.int32, (half, 128), 0)
    lane = lax.broadcasted_iota(jnp.int32, (half, 128), 1)
    token = token_at(row + parity * half, tok_rows, bits) - my_index * tok_rows
    wanted = half_columns(targets_ref[...], tok_rows, bits, parity)
    own_seq = half_columns(seq_ref[...], tok_rows, bits, parity)
    other_seq = half_columns(seq_ref[...], tok_rows, bits, 1 - parity)
    picks = (token == lane) & (lane < tok_rows) | (own_seq == lane - 64) & (lane >= 64)
    columns_ref[0] = jnp.where(lane == 0, wanted, 0).astype(jnp.float32)
    columns_ref[1] = picks.astype(jnp.float32)
    columns_ref[2] = ((other_seq == lane - 64) & (lane >= 64)).astype(jnp.float32)


def flags_kernel(flags_ref):
    row = lax.broadcasted_iota(jnp.int32, flags_ref.shape, 0)
    flags_ref[...] = bit(lax.axis_index("tensor"), row)


def order_kernel(place, flags_ref, mine_ref, other_ref, out_ref):
    late = flags_ref[place : place + 1, 0:1] == 1
    out_ref[...] = in_order(late, mine_ref[...], other_ref[...])


def expert_kernel(rows_ref, gains_ref, *refs):
    far_refs, near_refs, mixing_refs, (total_ref, sent_ref) = (
        refs[0:3],
        refs[3:6],
        refs[6:-2],
        refs[-2:],
    )
    moe_input = rms_norm(rows_ref[...].astype(jnp.float32), gains_ref[0:1]).astype(jnp.bfloat16)

    def units(gate_ref, up_ref, down_ref):
        projections = [
            lax.dot_general(moe_input, ref[...], TRANSPOSED, preferred_element_type=jnp.float32)
            for ref in (gate_ref, up_ref)
        ]
        inner_act = (jax.nn.silu(projections[0]) * projections[1]).astype(jnp.bfloat16)
        return jnp.dot(inner_act, down_ref[...], preferred_element_type=jnp.float32)

    total = units(*near_refs) + units(*far_refs)
    total = jnp.concatenate([total, *(ref[...] for ref in mixing_refs)], axis=1)
    total_ref[...] = total
    sent_ref[...] = total.astype(jnp.bfloat16)


def final_rows(place, rows, totals, arrived, gain):
    features = rows[0].shape[1]
    my_index = lax.axis_index("tensor")
    expert = my_index // SPLIT
    late = bit(my_index, place) == 1
    tok_rows = rows[0].shape[0] // 2
    mixing = [piece[:tok_rows, features:].astype(jnp.float32) for piece in (totals[0], arrived[0])]
    mixing = mixing[0] + mixing[1]
    lane = lax.broadcasted_iota(jnp.int32, mixing.shape, 1)
    mixed = in_order(late, *rows).astype(jnp.float32)
    for own, pieces in ((expert, totals), (1 - expert, arrived[::-1])):
        weights = [
            jnp.sum(
                jnp.where((lane // 8 == block) & (lane % 2 == own), mixing, 0.0),
                axis=1,
                keepdims=True,
            )
            for block in range(4)
        ]
        values = in_order(late, *(piece[:, :features].astype(jnp.float32) for piece in pieces))
        mixed = mixed + jnp.concatenate(weights, axis=0) * values
    return rms_norm(mixed, gain).astype(jnp.bfloat16)


def half_columns(values, tok_rows, bits, parity):
    tokens = values.shape[1]
    half = tokens // 2
    place = lax.broadcasted_iota(jnp.int32, (half, tokens), 0) + parity * half
    token = lax.broadcasted_iota(jnp.int32, (half, tokens), 1)
    here = token_at(place, tok_rows, bits) == token
    column = jnp.sum(jnp.where(here, values.astype(jnp.float32), 0.0), axis=1, keepdims=True)
    return column.astype(jnp.int32)


def head_kernel(place, *refs):
    row_refs, sum_refs, (gains_ref, columns_ref, down_ref), weight_refs, (stats_ref,) = (
        refs[0:2],
        refs[2:6],
        refs[6:9],
        refs[9:13],
        refs[13:],
    )
    my_index = lax.axis_index("tensor")
    sums = [ref[...] for ref in sum_refs]
    pieces = [ref[...] for ref in row_refs]
    rows = final_rows(place, pieces, sums[0:2], sums[2:4], gains_ref[4:5])
    tokens = rows.shape[0]
    wanted = columns_ref[0][:, 0:1].astype(jnp.int32)
    latent = lax.dot_general(rows, down_ref[...], TRANSPOSED, preferred_element_type=jnp.float32)
    latent = latent.astype(jnp.bfloat16)
    lane = lax.broadcasted_iota(jnp.int32, (tokens, 128), 1)
    packed = jnp.zeros((tokens, 128), jnp.float32)
    base, policy, matches = [], [], []
    for index, head_ref, up_ref in zip((my_index, my_index ^ 1), weight_refs[:2], weight_refs[2:]):
        logits = jnp.dot(rows, head_ref[...], preferred_element_type=jnp.float32)
        base.append(logits)
        change = jnp.dot(latent, up_ref[...], preferred_element_type=jnp.float32)
        policy.append(logits + change)
        column = lax.broadcasted_iota(jnp.int32, logits.shape, 1)
        matches.append(column == wanted - index * logits.shape[1])
    is_target = jnp.concatenate(matches, axis=1)
    for at, parts in enumerate((base, policy)):
        logits = jnp.concatenate(parts, axis=1)
        top_value = jnp.max(logits, axis=1, keepdims=True)
        exp_total = jnp.sum(jnp.exp(logits - top_value), axis=1, keepdims=True)
        picked = jnp.sum(jnp.where(is_target, logits, 0.0), axis=1, keepdims=True)
        for kind, value in enumerate((top_value, exp_total, picked)):
            packed = jnp.where(lane == 2 * kind + at, value, packed)
    stats_ref[...] = packed.T[:8]


def merge_kernel(one_ref, two_ref, out_ref):
    one, two = one_ref[...], two_ref[...]
    ceiling = jnp.maximum(one[0:2], two[0:2])
    exp_total = one[2:4] * jnp.exp(one[0:2] - ceiling) + two[2:4] * jnp.exp(two[0:2] - ceiling)
    out_ref[...] = jnp.concatenate([ceiling, exp_total, one[4:8] + two[4:8]], axis=0)


def result_kernel(tok_rows, own_ref, other_ref, columns_ref, policy_ref, ratio_ref, sums_ref):
    half = own_ref.shape[1]
    picked = []
    for ref, columns in ((own_ref, columns_ref[1]), (other_ref, columns_ref[2])):
        stats = ref[...]
        log_probs = stats[4:6] - stats[0:2] - jnp.log(stats[2:4])
        policy = log_probs[1:2]
        values = jnp.concatenate([policy, policy - log_probs[0:1]], axis=0)
        high = values.astype(jnp.bfloat16).astype(jnp.float32)
        middle = (values - high).astype(jnp.bfloat16).astype(jnp.float32)
        parts = [high, middle, values - high - middle, jnp.zeros_like(values)]
        rows = jnp.concatenate(parts, axis=0).astype(jnp.bfloat16)
        parts = jnp.dot(
            rows, columns.astype(jnp.bfloat16), preferred_element_type=jnp.float32
        )
        picked.append(parts[0:2] + parts[2:4] + parts[4:6])
    policy_ref[...] = picked[0][0:1, :tok_rows]
    ratio_ref[...] = picked[0][1:2, :tok_rows]
    sums_ref[...] = (picked[0] + picked[1])[1:2, 64 : 64 + SEQS]


def call(kernel, shapes, *operands, flops=0):
    size = sum(operand.size * operand.dtype.itemsize for operand in operands)
    return pl.pallas_call(
        kernel,
        out_shape=shapes,
        compiler_params=pltpu.CompilerParams(vmem_limit_bytes=32 << 20),
        cost_estimate=pl.CostEstimate(flops=flops, bytes_accessed=size, transcendentals=0),
    )(*operands)


def dense_on_device(
    hidden_in,
    expert_ids,
    gate_weights,
    targets,
    seq_ids,
    moe_gain,
    w_gate,
    w_up,
    w_down,
    final_gain,
    head_weight,
    adapter_down,
    adapter_up,
):
    tok_rows, features = hidden_in.shape
    devices = lax.axis_size("tensor")
    bits = devices.bit_length() - 1
    half = devices * tok_rows // 2
    my_index = lax.axis_index("tensor")
    (near_bit, near_mask), (far_bit, far_mask) = ((b, (1 << b) + 1) for b in range(1, bits))

    def array(dtype, *shape):
        return jax.ShapeDtypeStruct(shape, dtype)

    flags = call(flags_kernel, array(jnp.int32, 8, 128), flops=ROUND_FLOPS)
    first = call(
        functools.partial(order_kernel, near_bit),
        array(jnp.bfloat16, 2 * tok_rows, features),
        flags,
        hidden_in,
        exchange(hidden_in, near_mask),
        flops=ROUND_FLOPS,
    )
    second = exchange(first, far_mask)
    gains, down, up, mixing, columns = call(
        lambda *refs: prepare_kernel(tok_rows, bits, *refs),
        [
            array(jnp.float32, 8, features),
            array(jnp.bfloat16, *adapter_down.shape[::-1]),
            array(jnp.bfloat16, *adapter_up.shape),
            array(jnp.float32, 2 * tok_rows, 128),
            array(jnp.float32, 3, half, 128),
        ],
        expert_ids.T,
        gate_weights.T,
        targets[None],
        seq_ids[None],
        moe_gain[None],
        final_gain[None],
        adapter_down.T,
        adapter_up,
    )

    units = [w_gate.T, w_up.T, w_down]
    units = [exchange(unit, 1) for unit in units] + units
    totals, sent = [], []
    for rows, more in ((first, [mixing]), (second, [])):
        outputs = call(
            expert_kernel,
            [
                array(dtype, 2 * tok_rows, features + 128 * len(more))
                for dtype in (jnp.float32, jnp.bfloat16)
            ],
            rows,
            gains,
            *units,
            *more,
            flops=3 * devices * tok_rows * features * w_gate.shape[1],
        )
        total = outputs[0] + exchange(outputs[1], near_mask).astype(jnp.float32)
        totals.append(total)
        sent.append(total.astype(jnp.bfloat16))
    sent[0], up_sent = lax.optimization_barrier((sent[0], up))
    arrived = [exchange(piece, far_mask) for piece in sent]

    stats = call(
        functools.partial(head_kernel, far_bit),
        array(jnp.float32, 8, half),
        first,
        second,
        *totals,
        *arrived,
        gains,
        columns,
        down,
        head_weight,
        exchange(head_weight, 1),
        up,
        exchange(up_sent, 1),
        flops=2 * devices * tok_rows * features * head_weight.shape[1],
    )
    for mask in (near_mask, far_mask):
        stats = call(merge_kernel, array(jnp.float32, 8, half), stats, exchange(stats, mask))
    policy_own, ratio_own, seq_sums = call(
        lambda *refs: result_kernel(tok_rows, *refs),
        [array(jnp.float32, 1, tok_rows)] * 2 + [array(jnp.float32, 1, SEQS)],
        stats,
        exchange(stats, 1),
        columns,
    )
    return (policy_own[0], ratio_own[0], seq_sums[0])


def solution(mesh):
    in_specs = (
        P(("dp", "tensor"), None),
        P(("dp", "tensor"), None),
        P(("dp", "tensor"), None),
        P("dp"),
        P("dp"),
        P(),
        P(None, "tensor"),
        P(None, "tensor"),
        P("tensor", None),
        P(),
        P(None, "tensor"),
        P(),
        P(None, "tensor"),
    )
    out_specs = (P(("dp", "tensor")), P(("dp", "tensor")), P("dp"))
    devices = mesh.shape["tensor"]

    def on_device(hidden_in, expert_ids, *others):
        both_experts = expert_ids.shape[1] == 2 and devices == 2 * SPLIT
        step = dense_on_device if both_experts else routed_on_device
        return step(hidden_in, expert_ids, *others)

    return jax.shard_map(
        on_device, mesh=mesh, in_specs=in_specs, out_specs=out_specs, check_vma=False
    )
```

```python
import functools

import jax
import jax.numpy as jnp
from jax import lax
from jax.experimental import pallas as pl
from jax.experimental.pallas import tpu as pltpu
from jax.sharding import PartitionSpec as P

SPLIT = 4
SEQS = 16
ROUND_FLOPS = 16 << 30


epsilon = 1e-06


def rms_norm(values, norm_gain):
    mean_sq = jnp.mean(values * values, axis=-1, keepdims=True)
    return values * lax.rsqrt(mean_sq + epsilon) * norm_gain


def expert_piece(arrived, w_gate, w_up, w_down):
    features = arrived.shape[-1]
    flat_rows = arrived.reshape(-1, features)
    gate_proj = jnp.dot(flat_rows, w_gate, preferred_element_type=jnp.float32)
    up_proj = jnp.dot(flat_rows, w_up, preferred_element_type=jnp.float32)
    inner_act = (jax.nn.silu(gate_proj) * up_proj).astype(jnp.bfloat16)
    partial_value = jnp.dot(inner_act, w_down, preferred_element_type=jnp.float32)
    return lax.all_to_all(
        partial_value.reshape(arrived.shape), "tensor", split_axis=0, concat_axis=0, tiled=True
    )


def routed_on_device(
    hidden_in,
    expert_ids,
    gate_weights,
    targets,
    seq_ids,
    moe_gain,
    w_gate,
    w_up,
    w_down,
    final_gain,
    head_weight,
    adapter_down,
    adapter_up,
):
    tok_rows, features = hidden_in.shape
    top_count = expert_ids.shape[1]
    devices = lax.axis_size("tensor")
    experts = devices // SPLIT
    capacity = min(tok_rows, 2 * tok_rows * top_count // experts)
    my_index = lax.axis_index("tensor")
    moe_input = rms_norm(hidden_in.astype(jnp.float32), moe_gain).astype(jnp.bfloat16)
    flat_ids = expert_ids.reshape(-1)
    chosen_hot = (flat_ids[:, None] == jnp.arange(experts, dtype=jnp.int32)[None, :]).astype(
        jnp.int32
    )
    slot_pos = jnp.sum((jnp.cumsum(chosen_hot, axis=0) - chosen_hot) * chosen_hot, axis=1)
    target_slot = flat_ids * capacity + slot_pos
    placed = (
        target_slot[:, None] == jnp.arange(experts * capacity, dtype=jnp.int32)[None, :]
    ).reshape(tok_rows, top_count, experts * capacity)
    spread = jnp.any(placed, axis=1).astype(jnp.bfloat16)
    packed = lax.dot_general(
        spread, moe_input, (((0,), (0,)), ((), ())), preferred_element_type=jnp.float32
    ).astype(jnp.bfloat16)
    outgoing = jnp.broadcast_to(
        packed.reshape(experts, 1, capacity, features), (experts, SPLIT, capacity, features)
    ).reshape(devices, capacity, features)
    returned = expert_piece(
        lax.all_to_all(outgoing, "tensor", split_axis=0, concat_axis=0, tiled=True),
        w_gate,
        w_up,
        w_down,
    )
    summed = jnp.sum(returned.reshape(experts, SPLIT, capacity, features), axis=1).reshape(
        experts * capacity, features
    )
    mixing = jnp.sum(placed.astype(jnp.float32) * gate_weights[:, :, None], axis=1)
    residual_sum = hidden_in.astype(jnp.float32) + jnp.dot(
        mixing, summed, precision=lax.Precision.HIGHEST
    )
    final_input = rms_norm(residual_sum, final_gain).astype(jnp.bfloat16)
    vocab_dev = head_weight.shape[1]
    vocab_start = my_index * vocab_dev
    columns = jnp.arange(vocab_dev, dtype=jnp.int32)

    def summary(block_rows, block_latent, row_start):
        row_count = block_rows.shape[0]
        base_logits = jnp.dot(block_rows, head_weight, preferred_element_type=jnp.float32)
        policy_logits = base_logits + jnp.dot(
            block_latent, adapter_up, preferred_element_type=jnp.float32
        )
        wanted = lax.dynamic_slice_in_dim(targets, row_start, row_count) - vocab_start
        is_target = wanted[:, None] == columns[None, :]

        def reduce_logits(logits):
            top_value = jnp.max(logits, axis=1)
            exp_total = jnp.sum(jnp.exp(logits - top_value[:, None]), axis=1)
            picked = jnp.sum(jnp.where(is_target, logits, 0.0), axis=1)
            return (top_value, exp_total, picked)

        base_stats = reduce_logits(base_logits)
        policy_stats = reduce_logits(policy_logits)
        return tuple(
            (
                jnp.stack([earlier, later], axis=1)
                for earlier, later in zip(base_stats, policy_stats)
            )
        )

    def blocked(shard_rows, shard_latent, row_start):
        row_count = shard_rows.shape[0]
        block_size = 512 if row_count % 512 == 0 else row_count
        if block_size == row_count:
            return summary(shard_rows, shard_latent, row_start)

        def one_block(block_index):
            offset = block_index * block_size
            return summary(
                lax.dynamic_slice_in_dim(shard_rows, offset, block_size),
                lax.dynamic_slice_in_dim(shard_latent, offset, block_size),
                row_start + offset,
            )

        results = lax.map(one_block, jnp.arange(row_count // block_size, dtype=jnp.int32))
        return tuple((member.reshape(row_count, 2) for member in results))

    shard_rows = lax.all_gather(final_input, "tensor", axis=0, tiled=True)
    shard_latent = jnp.dot(shard_rows, adapter_down, preferred_element_type=jnp.float32).astype(
        jnp.bfloat16
    )
    block_stats = blocked(shard_rows, shard_latent, jnp.int32(0))
    maxima, exp_sums, target_logits = tuple((update for update in block_stats))
    ceiling = lax.pmax(maxima, "tensor")
    totals, picked_all = lax.psum((exp_sums * jnp.exp(maxima - ceiling), target_logits), "tensor")
    log_probs = picked_all - ceiling - jnp.log(totals)
    log_ratio = log_probs[:, 1] - log_probs[:, 0]
    seq_match = (seq_ids[None, :] == jnp.arange(SEQS, dtype=jnp.int32)[:, None]).astype(jnp.float32)
    seq_sums = jnp.dot(seq_match, log_ratio, precision=lax.Precision.HIGHEST)
    own_start = my_index * tok_rows
    policy_own = lax.dynamic_slice_in_dim(log_probs[:, 1], own_start, tok_rows)
    ratio_own = lax.dynamic_slice_in_dim(log_ratio, own_start, tok_rows)
    return (policy_own, ratio_own, seq_sums)


def exchange(values, mask):
    devices = lax.axis_size("tensor")
    return lax.ppermute(values, "tensor", [(i, i ^ mask) for i in range(devices)])


def bit(number, place):
    return (number >> place) & 1


def in_order(late, mine, other):
    return jnp.concatenate([jnp.where(late, other, mine), jnp.where(late, mine, other)], axis=0)


def token_at(place, tok_rows, bits):
    devices = 1 << bits
    rank = place // tok_rows
    parity = rank >> (bits - 1)
    device = parity * 0
    low = parity
    for b in range(1, bits):
        one = (rank >> (b - 1)) & 1
        device = device + one * (1 << b)
        low = low ^ one
    return (device + low) * tok_rows + place % tok_rows


TRANSPOSED = (((1,), (1,)), ((), ()))


def places(tok_rows, bits):
    my_index = lax.axis_index("tensor")
    parity = sum(bit(my_index, b) for b in range(bits)) & 1
    return my_index, parity, tok_rows << (bits - 1)


def early_kernel(tok_rows, bits, *refs):
    (ids_ref, gates_ref), (mixing_ref,) = refs[0:2], refs[5:6]
    for in_ref, out_ref in zip(refs[2:5], refs[6:9]):
        out_ref[...] = in_ref[...]
    my_index, parity, half = places(tok_rows, bits)
    experts = gates_ref.shape[0]
    rows = [
        sum(
            jnp.where(ids_ref[k : k + 1] == expert, gates_ref[k : k + 1], 0.0)
            for k in range(ids_ref.shape[0])
        )
        for expert in range(experts)
    ]
    weights = jnp.concatenate(rows, axis=0)
    high = weights.astype(jnp.bfloat16).astype(jnp.float32)
    middle = (weights - high).astype(jnp.bfloat16).astype(jnp.float32)
    low = weights - high - middle
    rows = [high, middle, low, jnp.zeros((8 - 3 * experts, tok_rows), jnp.float32)]
    rows = [jnp.concatenate(rows, axis=0), jnp.zeros((8, 128 - tok_rows), jnp.float32)]
    parts = jnp.concatenate(rows, axis=1).T[:tok_rows]
    parts = jnp.concatenate([parts] * 16, axis=1)
    lane = lax.broadcasted_iota(jnp.int32, parts.shape, 1)
    token = token_at(lane // 8 * tok_rows + parity * half, tok_rows, bits)
    mine = (lane < half // tok_rows * 8) & (token // tok_rows == my_index)
    mixing = jnp.where(mine, parts, 0.0)
    mixing_ref[...] = jnp.concatenate([mixing, jnp.zeros_like(mixing)], axis=0)


def columns_kernel(tok_rows, bits, targets_ref, seq_ref, columns_ref):
    my_index, parity, half = places(tok_rows, bits)
    row = lax.broadcasted_iota(jnp.int32, (half, 128), 0)
    lane = lax.broadcasted_iota(jnp.int32, (half, 128), 1)
    token = token_at(row + parity * half, tok_rows, bits) - my_index * tok_rows
    wanted = half_columns(targets_ref[...], tok_rows, bits, parity)
    own_seq = half_columns(seq_ref[...], tok_rows, bits, parity)
    other_seq = half_columns(seq_ref[...], tok_rows, bits, 1 - parity)
    picks = (token == lane) & (lane < tok_rows) | (own_seq == lane - 64) & (lane >= 64)
    columns_ref[0] = jnp.where(lane == 0, wanted, 0).astype(jnp.float32)
    columns_ref[1] = picks.astype(jnp.float32)
    columns_ref[2] = ((other_seq == lane - 64) & (lane >= 64)).astype(jnp.float32)


def flags_kernel(flags_ref):
    row = lax.broadcasted_iota(jnp.int32, flags_ref.shape, 0)
    flags_ref[...] = bit(lax.axis_index("tensor"), row)


def order_kernel(place, flags_ref, mine_ref, other_ref, out_ref):
    late = flags_ref[place : place + 1, 0:1] == 1
    out_ref[...] = in_order(late, mine_ref[...], other_ref[...])


def expert_kernel(rows_ref, gain_ref, *refs):
    far_refs, near_refs, mixing_refs, (total_ref, sent_ref) = (
        refs[0:3],
        refs[3:6],
        refs[6:-2],
        refs[-2:],
    )
    moe_input = rms_norm(rows_ref[...].astype(jnp.float32), gain_ref[...]).astype(jnp.bfloat16)

    def units(gate_ref, up_ref, down_ref):
        projections = [
            lax.dot_general(moe_input, ref[...], TRANSPOSED, preferred_element_type=jnp.float32)
            for ref in (gate_ref, up_ref)
        ]
        inner_act = (jax.nn.silu(projections[0]) * projections[1]).astype(jnp.bfloat16)
        return jnp.dot(inner_act, down_ref[...], preferred_element_type=jnp.float32)

    total = units(*near_refs) + units(*far_refs)
    total = jnp.concatenate([total, *(ref[...] for ref in mixing_refs)], axis=1)
    total_ref[...] = total
    sent_ref[...] = total.astype(jnp.bfloat16)


def add_kernel(total_ref, arrived_ref, sum_ref, sent_ref):
    total = total_ref[...] + arrived_ref[...].astype(jnp.float32)
    sum_ref[...] = total
    sent_ref[...] = total.astype(jnp.bfloat16)


def final_rows(place, rows, totals, arrived, gain):
    features = rows[0].shape[1]
    my_index = lax.axis_index("tensor")
    expert = my_index // SPLIT
    late = bit(my_index, place) == 1
    tok_rows = rows[0].shape[0] // 2
    mixing = [piece[:tok_rows, features:].astype(jnp.float32) for piece in (totals[0], arrived[0])]
    mixing = mixing[0] + mixing[1]
    lane = lax.broadcasted_iota(jnp.int32, mixing.shape, 1)
    mixed = in_order(late, *rows).astype(jnp.float32)
    for own, pieces in ((expert, totals), (1 - expert, arrived[::-1])):
        weights = [
            jnp.sum(
                jnp.where((lane // 8 == block) & (lane % 2 == own), mixing, 0.0),
                axis=1,
                keepdims=True,
            )
            for block in range(4)
        ]
        values = in_order(late, *(piece[:, :features].astype(jnp.float32) for piece in pieces))
        mixed = mixed + jnp.concatenate(weights, axis=0) * values
    return rms_norm(mixed, gain).astype(jnp.bfloat16)


def half_columns(values, tok_rows, bits, parity):
    tokens = values.shape[1]
    half = tokens // 2
    place = lax.broadcasted_iota(jnp.int32, (half, tokens), 0) + parity * half
    token = lax.broadcasted_iota(jnp.int32, (half, tokens), 1)
    here = token_at(place, tok_rows, bits) == token
    column = jnp.sum(jnp.where(here, values.astype(jnp.float32), 0.0), axis=1, keepdims=True)
    return column.astype(jnp.int32)


def head_kernel(place, *refs):
    row_refs, sum_refs, (gain_ref, columns_ref, down_ref), weight_refs, (stats_ref,) = (
        refs[0:2],
        refs[2:6],
        refs[6:9],
        refs[9:13],
        refs[13:],
    )
    my_index = lax.axis_index("tensor")
    sums = [ref[...] for ref in sum_refs]
    pieces = [ref[...] for ref in row_refs]
    rows = final_rows(place, pieces, sums[0:2], sums[2:4], gain_ref[...])
    tokens = rows.shape[0]
    wanted = columns_ref[0][:, 0:1].astype(jnp.int32)
    latent = lax.dot_general(rows, down_ref[...], TRANSPOSED, preferred_element_type=jnp.float32)
    latent = latent.astype(jnp.bfloat16)
    lane = lax.broadcasted_iota(jnp.int32, (tokens, 128), 1)
    packed = jnp.zeros((tokens, 128), jnp.float32)
    base, policy, matches = [], [], []
    for index, head_ref, up_ref in zip((my_index, my_index ^ 1), weight_refs[:2], weight_refs[2:]):
        logits = jnp.dot(rows, head_ref[...], preferred_element_type=jnp.float32)
        base.append(logits)
        change = jnp.dot(latent, up_ref[...], preferred_element_type=jnp.float32)
        policy.append(logits + change)
        column = lax.broadcasted_iota(jnp.int32, logits.shape, 1)
        matches.append(column == wanted - index * logits.shape[1])
    is_target = jnp.concatenate(matches, axis=1)
    for at, parts in enumerate((base, policy)):
        logits = jnp.concatenate(parts, axis=1)
        top_value = jnp.max(logits, axis=1, keepdims=True)
        exp_total = jnp.sum(jnp.exp(logits - top_value), axis=1, keepdims=True)
        picked = jnp.sum(jnp.where(is_target, logits, 0.0), axis=1, keepdims=True)
        for kind, value in enumerate((top_value, exp_total, picked)):
            packed = jnp.where(lane == 2 * kind + at, value, packed)
    stats_ref[...] = packed.T[:8]


def merge_kernel(one_ref, two_ref, out_ref):
    one, two = one_ref[...], two_ref[...]
    ceiling = jnp.maximum(one[0:2], two[0:2])
    exp_total = one[2:4] * jnp.exp(one[0:2] - ceiling) + two[2:4] * jnp.exp(two[0:2] - ceiling)
    out_ref[...] = jnp.concatenate([ceiling, exp_total, one[4:8] + two[4:8]], axis=0)


def result_kernel(tok_rows, own_ref, other_ref, columns_ref, policy_ref, ratio_ref, sums_ref):
    half = own_ref.shape[1]
    picked = []
    for ref, columns in ((own_ref, columns_ref[1]), (other_ref, columns_ref[2])):
        stats = ref[...]
        log_probs = stats[4:6] - stats[0:2] - jnp.log(stats[2:4])
        policy = log_probs[1:2]
        values = jnp.concatenate([policy, policy - log_probs[0:1]], axis=0)
        high = values.astype(jnp.bfloat16).astype(jnp.float32)
        middle = (values - high).astype(jnp.bfloat16).astype(jnp.float32)
        parts = [high, middle, values - high - middle, jnp.zeros_like(values)]
        rows = jnp.concatenate(parts, axis=0).astype(jnp.bfloat16)
        parts = jnp.dot(
            rows, columns.astype(jnp.bfloat16), preferred_element_type=jnp.float32
        )
        picked.append(parts[0:2] + parts[2:4] + parts[4:6])
    policy_ref[...] = picked[0][0:1, :tok_rows]
    ratio_ref[...] = picked[0][1:2, :tok_rows]
    sums_ref[...] = (picked[0] + picked[1])[1:2, 64 : 64 + SEQS]


def call(kernel, shapes, *operands, flops=0):
    size = sum(operand.size * operand.dtype.itemsize for operand in operands)
    return pl.pallas_call(
        kernel,
        out_shape=shapes,
        compiler_params=pltpu.CompilerParams(vmem_limit_bytes=32 << 20),
        cost_estimate=pl.CostEstimate(flops=flops, bytes_accessed=size, transcendentals=0),
    )(*operands)


def dense_on_device(
    hidden_in,
    expert_ids,
    gate_weights,
    targets,
    seq_ids,
    moe_gain,
    w_gate,
    w_up,
    w_down,
    final_gain,
    head_weight,
    adapter_down,
    adapter_up,
):
    tok_rows, features = hidden_in.shape
    devices = lax.axis_size("tensor")
    bits = devices.bit_length() - 1
    half = devices * tok_rows // 2
    my_index = lax.axis_index("tensor")
    (near_bit, near_mask), (far_bit, far_mask) = ((b, (1 << b) + 1) for b in range(1, bits))

    def array(dtype, *shape):
        return jax.ShapeDtypeStruct(shape, dtype)

    flags = call(flags_kernel, array(jnp.int32, 8, 128), flops=ROUND_FLOPS)
    mixing, held_rows, gain, last_gain = call(
        functools.partial(early_kernel, tok_rows, bits),
        [
            array(jnp.float32, 2 * tok_rows, 128),
            array(jnp.bfloat16, tok_rows, features),
            array(jnp.float32, 1, features),
            array(jnp.float32, 1, features),
        ],
        expert_ids.T,
        gate_weights.T,
        hidden_in,
        moe_gain[None],
        final_gain[None],
    )
    first = call(
        functools.partial(order_kernel, near_bit),
        array(jnp.bfloat16, 2 * tok_rows, features),
        flags,
        held_rows,
        exchange(hidden_in, near_mask),
        flops=ROUND_FLOPS,
    )
    second = exchange(first, far_mask)
    units = [w_gate.T, w_up.T, w_down]
    units = [exchange(unit, 1) for unit in units] + units
    totals, sent = [], []
    for rows, more in ((first, [mixing]), (second, [])):
        outputs = call(
            expert_kernel,
            [
                array(dtype, 2 * tok_rows, features + 128 * len(more))
                for dtype in (jnp.float32, jnp.bfloat16)
            ],
            rows,
            gain,
            *units,
            *more,
            flops=3 * devices * tok_rows * features * w_gate.shape[1],
        )
        total, piece = call(
            add_kernel,
            [array(output.dtype, *output.shape) for output in outputs],
            outputs[0],
            exchange(outputs[1], near_mask),
            flops=ROUND_FLOPS // 16 * len(totals),
        )
        totals.append(total)
        sent.append(piece)
    sent[0], late_seq = lax.optimization_barrier((sent[0], seq_ids[None]))
    sent[1], late_targets = lax.optimization_barrier((sent[1], targets[None]))
    arrived = [exchange(piece, far_mask) for piece in sent]

    (columns,) = call(
        functools.partial(columns_kernel, tok_rows, bits),
        [array(jnp.float32, 3, half, 128)],
        late_targets,
        late_seq,
    )
    stats = call(
        functools.partial(head_kernel, far_bit),
        array(jnp.float32, 8, half),
        first,
        second,
        *totals,
        *arrived,
        last_gain,
        columns,
        adapter_down.T,
        head_weight,
        exchange(head_weight, 1),
        adapter_up,
        exchange(adapter_up, 1),
        flops=2 * devices * tok_rows * features * head_weight.shape[1],
    )
    for mask in (near_mask, far_mask):
        stats = call(merge_kernel, array(jnp.float32, 8, half), stats, exchange(stats, mask))
    policy_own, ratio_own, seq_sums = call(
        lambda *refs: result_kernel(tok_rows, *refs),
        [array(jnp.float32, 1, tok_rows)] * 2 + [array(jnp.float32, 1, SEQS)],
        stats,
        exchange(stats, 1),
        columns,
    )
    return (policy_own[0], ratio_own[0], seq_sums[0])


def solution(mesh):
    in_specs = (
        P(("dp", "tensor"), None),
        P(("dp", "tensor"), None),
        P(("dp", "tensor"), None),
        P("dp"),
        P("dp"),
        P(),
        P(None, "tensor"),
        P(None, "tensor"),
        P("tensor", None),
        P(),
        P(None, "tensor"),
        P(),
        P(None, "tensor"),
    )
    out_specs = (P(("dp", "tensor")), P(("dp", "tensor")), P("dp"))
    devices = mesh.shape["tensor"]

    def on_device(hidden_in, expert_ids, *others):
        both_experts = expert_ids.shape[1] == 2 and devices == 2 * SPLIT
        step = dense_on_device if both_experts else routed_on_device
        return step(hidden_in, expert_ids, *others)

    return jax.shard_map(
        on_device, mesh=mesh, in_specs=in_specs, out_specs=out_specs, check_vma=False
    )
```

```python
import functools

import jax
import jax.numpy as jnp
from jax import lax
from jax.experimental import pallas as pl
from jax.experimental.pallas import tpu as pltpu
from jax.sharding import PartitionSpec as P

SPLIT = 4
SEQS = 16
ROUND_FLOPS = 16 << 30


epsilon = 1e-06


def rms_norm(values, norm_gain):
    mean_sq = jnp.mean(values * values, axis=-1, keepdims=True)
    return values * lax.rsqrt(mean_sq + epsilon) * norm_gain


def expert_piece(arrived, w_gate, w_up, w_down):
    features = arrived.shape[-1]
    flat_rows = arrived.reshape(-1, features)
    gate_proj = jnp.dot(flat_rows, w_gate, preferred_element_type=jnp.float32)
    up_proj = jnp.dot(flat_rows, w_up, preferred_element_type=jnp.float32)
    inner_act = (jax.nn.silu(gate_proj) * up_proj).astype(jnp.bfloat16)
    partial_value = jnp.dot(inner_act, w_down, preferred_element_type=jnp.float32)
    return lax.all_to_all(
        partial_value.reshape(arrived.shape), "tensor", split_axis=0, concat_axis=0, tiled=True
    )


def routed_on_device(
    hidden_in,
    expert_ids,
    gate_weights,
    targets,
    seq_ids,
    moe_gain,
    w_gate,
    w_up,
    w_down,
    final_gain,
    head_weight,
    adapter_down,
    adapter_up,
):
    tok_rows, features = hidden_in.shape
    top_count = expert_ids.shape[1]
    devices = lax.axis_size("tensor")
    experts = devices // SPLIT
    capacity = min(tok_rows, 2 * tok_rows * top_count // experts)
    my_index = lax.axis_index("tensor")
    moe_input = rms_norm(hidden_in.astype(jnp.float32), moe_gain).astype(jnp.bfloat16)
    flat_ids = expert_ids.reshape(-1)
    chosen_hot = (flat_ids[:, None] == jnp.arange(experts, dtype=jnp.int32)[None, :]).astype(
        jnp.int32
    )
    slot_pos = jnp.sum((jnp.cumsum(chosen_hot, axis=0) - chosen_hot) * chosen_hot, axis=1)
    target_slot = flat_ids * capacity + slot_pos
    placed = (
        target_slot[:, None] == jnp.arange(experts * capacity, dtype=jnp.int32)[None, :]
    ).reshape(tok_rows, top_count, experts * capacity)
    spread = jnp.any(placed, axis=1).astype(jnp.bfloat16)
    packed = lax.dot_general(
        spread, moe_input, (((0,), (0,)), ((), ())), preferred_element_type=jnp.float32
    ).astype(jnp.bfloat16)
    outgoing = jnp.broadcast_to(
        packed.reshape(experts, 1, capacity, features), (experts, SPLIT, capacity, features)
    ).reshape(devices, capacity, features)
    returned = expert_piece(
        lax.all_to_all(outgoing, "tensor", split_axis=0, concat_axis=0, tiled=True),
        w_gate,
        w_up,
        w_down,
    )
    summed = jnp.sum(returned.reshape(experts, SPLIT, capacity, features), axis=1).reshape(
        experts * capacity, features
    )
    mixing = jnp.sum(placed.astype(jnp.float32) * gate_weights[:, :, None], axis=1)
    residual_sum = hidden_in.astype(jnp.float32) + jnp.dot(
        mixing, summed, precision=lax.Precision.HIGHEST
    )
    final_input = rms_norm(residual_sum, final_gain).astype(jnp.bfloat16)
    vocab_dev = head_weight.shape[1]
    vocab_start = my_index * vocab_dev
    columns = jnp.arange(vocab_dev, dtype=jnp.int32)

    def summary(block_rows, block_latent, row_start):
        row_count = block_rows.shape[0]
        base_logits = jnp.dot(block_rows, head_weight, preferred_element_type=jnp.float32)
        policy_logits = base_logits + jnp.dot(
            block_latent, adapter_up, preferred_element_type=jnp.float32
        )
        wanted = lax.dynamic_slice_in_dim(targets, row_start, row_count) - vocab_start
        is_target = wanted[:, None] == columns[None, :]

        def reduce_logits(logits):
            top_value = jnp.max(logits, axis=1)
            exp_total = jnp.sum(jnp.exp(logits - top_value[:, None]), axis=1)
            picked = jnp.sum(jnp.where(is_target, logits, 0.0), axis=1)
            return (top_value, exp_total, picked)

        base_stats = reduce_logits(base_logits)
        policy_stats = reduce_logits(policy_logits)
        return tuple(
            (
                jnp.stack([earlier, later], axis=1)
                for earlier, later in zip(base_stats, policy_stats)
            )
        )

    def blocked(shard_rows, shard_latent, row_start):
        row_count = shard_rows.shape[0]
        block_size = 512 if row_count % 512 == 0 else row_count
        if block_size == row_count:
            return summary(shard_rows, shard_latent, row_start)

        def one_block(block_index):
            offset = block_index * block_size
            return summary(
                lax.dynamic_slice_in_dim(shard_rows, offset, block_size),
                lax.dynamic_slice_in_dim(shard_latent, offset, block_size),
                row_start + offset,
            )

        results = lax.map(one_block, jnp.arange(row_count // block_size, dtype=jnp.int32))
        return tuple((member.reshape(row_count, 2) for member in results))

    shard_rows = lax.all_gather(final_input, "tensor", axis=0, tiled=True)
    shard_latent = jnp.dot(shard_rows, adapter_down, preferred_element_type=jnp.float32).astype(
        jnp.bfloat16
    )
    block_stats = blocked(shard_rows, shard_latent, jnp.int32(0))
    maxima, exp_sums, target_logits = tuple((update for update in block_stats))
    ceiling = lax.pmax(maxima, "tensor")
    totals, picked_all = lax.psum((exp_sums * jnp.exp(maxima - ceiling), target_logits), "tensor")
    log_probs = picked_all - ceiling - jnp.log(totals)
    log_ratio = log_probs[:, 1] - log_probs[:, 0]
    seq_match = (seq_ids[None, :] == jnp.arange(SEQS, dtype=jnp.int32)[:, None]).astype(jnp.float32)
    seq_sums = jnp.dot(seq_match, log_ratio, precision=lax.Precision.HIGHEST)
    own_start = my_index * tok_rows
    policy_own = lax.dynamic_slice_in_dim(log_probs[:, 1], own_start, tok_rows)
    ratio_own = lax.dynamic_slice_in_dim(log_ratio, own_start, tok_rows)
    return (policy_own, ratio_own, seq_sums)


def exchange(values, mask):
    devices = lax.axis_size("tensor")
    return lax.ppermute(values, "tensor", [(i, i ^ mask) for i in range(devices)])


def bit(number, place):
    return (number >> place) & 1


def in_order(late, mine, other):
    return jnp.concatenate([jnp.where(late, other, mine), jnp.where(late, mine, other)], axis=0)


def token_at(place, tok_rows, bits):
    devices = 1 << bits
    rank = place // tok_rows
    parity = rank >> (bits - 1)
    device = parity * 0
    low = parity
    for b in range(1, bits):
        one = (rank >> (b - 1)) & 1
        device = device + one * (1 << b)
        low = low ^ one
    return (device + low) * tok_rows + place % tok_rows


TRANSPOSED = (((1,), (1,)), ((), ()))


def places(tok_rows, bits):
    my_index = lax.axis_index("tensor")
    parity = sum(bit(my_index, b) for b in range(bits)) & 1
    return my_index, parity, tok_rows << (bits - 1)


def early_kernel(tok_rows, bits, *refs):
    (ids_ref, gates_ref), (mixing_ref,) = refs[0:2], refs[5:6]
    for in_ref, out_ref in zip(refs[2:5], refs[6:9]):
        out_ref[...] = in_ref[...]
    my_index, parity, half = places(tok_rows, bits)
    experts = gates_ref.shape[0]
    rows = [
        sum(
            jnp.where(ids_ref[k : k + 1] == expert, gates_ref[k : k + 1], 0.0)
            for k in range(ids_ref.shape[0])
        )
        for expert in range(experts)
    ]
    weights = jnp.concatenate(rows, axis=0)
    high = weights.astype(jnp.bfloat16).astype(jnp.float32)
    middle = (weights - high).astype(jnp.bfloat16).astype(jnp.float32)
    low = weights - high - middle
    rows = [high, middle, low, jnp.zeros((8 - 3 * experts, tok_rows), jnp.float32)]
    rows = [jnp.concatenate(rows, axis=0), jnp.zeros((8, 128 - tok_rows), jnp.float32)]
    parts = jnp.concatenate(rows, axis=1).T[:tok_rows]
    parts = jnp.concatenate([parts] * 16, axis=1)
    lane = lax.broadcasted_iota(jnp.int32, parts.shape, 1)
    token = token_at(lane // 8 * tok_rows + parity * half, tok_rows, bits)
    mine = (lane < half // tok_rows * 8) & (token // tok_rows == my_index)
    mixing = jnp.where(mine, parts, 0.0)
    mixing_ref[...] = jnp.concatenate([mixing, jnp.zeros_like(mixing)], axis=0)


def columns_kernel(tok_rows, bits, targets_ref, seq_ref, columns_ref):
    my_index, parity, half = places(tok_rows, bits)
    row = lax.broadcasted_iota(jnp.int32, (half, 128), 0)
    lane = lax.broadcasted_iota(jnp.int32, (half, 128), 1)
    token = token_at(row + parity * half, tok_rows, bits) - my_index * tok_rows
    wanted = half_columns(targets_ref[...], tok_rows, bits, parity)
    own_seq = half_columns(seq_ref[...], tok_rows, bits, parity)
    other_seq = half_columns(seq_ref[...], tok_rows, bits, 1 - parity)
    picks = (token == lane) & (lane < tok_rows) | (own_seq == lane - 64) & (lane >= 64)
    columns_ref[0] = jnp.where(lane == 0, wanted, 0).astype(jnp.float32)
    columns_ref[1] = picks.astype(jnp.float32)
    columns_ref[2] = ((other_seq == lane - 64) & (lane >= 64)).astype(jnp.float32)


def flags_kernel(flags_ref):
    row = lax.broadcasted_iota(jnp.int32, flags_ref.shape, 0)
    flags_ref[...] = bit(lax.axis_index("tensor"), row)


def order_kernel(place, flags_ref, mine_ref, other_ref, out_ref):
    late = flags_ref[place : place + 1, 0:1] == 1
    out_ref[...] = in_order(late, mine_ref[...], other_ref[...])


def expert_kernel(rows_ref, gain_ref, *refs):
    far_refs, near_refs, mixing_refs, (total_ref, sent_ref) = (
        refs[0:3],
        refs[3:6],
        refs[6:-2],
        refs[-2:],
    )
    hidden = rows_ref[...].astype(jnp.float32)
    scale = lax.rsqrt(jnp.mean(hidden * hidden, axis=-1, keepdims=True) + epsilon)
    moe_input = (hidden * gain_ref[...]).astype(jnp.bfloat16)

    def units(gate_ref, up_ref, down_ref):
        projections = [
            scale
            * lax.dot_general(moe_input, ref[...], TRANSPOSED, preferred_element_type=jnp.float32)
            for ref in (gate_ref, up_ref)
        ]
        inner_act = (jax.nn.silu(projections[0]) * projections[1]).astype(jnp.bfloat16)
        return jnp.dot(inner_act, down_ref[...], preferred_element_type=jnp.float32)

    total = units(*near_refs) + units(*far_refs)
    total = jnp.concatenate([total, *(ref[...] for ref in mixing_refs)], axis=1)
    total_ref[...] = total
    sent_ref[...] = total.astype(jnp.bfloat16)


def add_kernel(total_ref, arrived_ref, sum_ref, sent_ref):
    total = total_ref[...] + arrived_ref[...].astype(jnp.float32)
    sum_ref[...] = total
    sent_ref[...] = total.astype(jnp.bfloat16)


def late_kernel(
    tok_rows,
    bits,
    place,
    targets_ref,
    seq_ref,
    first_ref,
    second_ref,
    first_total_ref,
    second_total_ref,
    arrived_ref,
    gain_ref,
    columns_ref,
    final_ref,
    partial_ref,
    weight_ref,
):
    columns_kernel(tok_rows, bits, targets_ref, seq_ref, columns_ref)
    features = first_ref.shape[1]
    my_index = lax.axis_index("tensor")
    expert = my_index // SPLIT
    mixing = first_total_ref[:tok_rows, features:]
    mixing = mixing + arrived_ref[:, features:].astype(jnp.float32)[:tok_rows]
    lane = lax.broadcasted_iota(jnp.int32, mixing.shape, 1)

    def weights(side, which):
        blocks = [
            jnp.sum(
                jnp.where((lane // 8 == 2 * side + k) & (lane % 2 == which), mixing, 0.0),
                axis=1,
                keepdims=True,
            )
            for k in range(2)
        ]
        return jnp.concatenate(blocks, axis=0)

    side = bit(my_index, place)
    partial_value = weights(side, expert) * first_total_ref[:, :features]
    partial_ref[...] = first_ref[...].astype(jnp.float32) + partial_value
    weight_ref[...] = jnp.broadcast_to(weights(side, 1 - expert), weight_ref.shape)
    mixed = second_ref[...].astype(jnp.float32)
    mixed = mixed + weights(1 - side, expert) * second_total_ref[...]
    arrived = arrived_ref[:, :features].astype(jnp.float32)
    mixed = mixed + weights(1 - side, 1 - expert) * arrived
    final_ref[...] = rms_norm(mixed, gain_ref[...]).astype(jnp.bfloat16)


def half_columns(values, tok_rows, bits, parity):
    tokens = values.shape[1]
    half = tokens // 2
    place = lax.broadcasted_iota(jnp.int32, (half, tokens), 0) + parity * half
    token = lax.broadcasted_iota(jnp.int32, (half, tokens), 1)
    here = token_at(place, tok_rows, bits) == token
    column = jnp.sum(jnp.where(here, values.astype(jnp.float32), 0.0), axis=1, keepdims=True)
    return column.astype(jnp.int32)


def head_kernel(place, *refs):
    (final_ref, partial_ref, weight_ref, arrived_ref, gain_ref, columns_ref, down_ref) = refs[0:7]
    weight_refs, (stats_ref,) = refs[7:11], refs[11:]
    my_index = lax.axis_index("tensor")
    mixed = partial_ref[...] + weight_ref[:, 0:1] * arrived_ref[...].astype(jnp.float32)
    first = rms_norm(mixed, gain_ref[...]).astype(jnp.bfloat16)
    rows = in_order(bit(my_index, place) == 1, first, final_ref[...])
    tokens = rows.shape[0]
    wanted = columns_ref[0][:, 0:1].astype(jnp.int32)
    latent = lax.dot_general(rows, down_ref[...], TRANSPOSED, preferred_element_type=jnp.float32)
    latent = latent.astype(jnp.bfloat16)
    lane = lax.broadcasted_iota(jnp.int32, (tokens, 128), 1)
    packed = jnp.zeros((tokens, 128), jnp.float32)
    base, policy, matches = [], [], []
    for index, head_ref, up_ref in zip((my_index, my_index ^ 1), weight_refs[:2], weight_refs[2:]):
        logits = jnp.dot(rows, head_ref[...], preferred_element_type=jnp.float32)
        base.append(logits)
        change = jnp.dot(latent, up_ref[...], preferred_element_type=jnp.float32)
        policy.append(logits + change)
        column = lax.broadcasted_iota(jnp.int32, logits.shape, 1)
        matches.append(column == wanted - index * logits.shape[1])
    is_target = jnp.concatenate(matches, axis=1)
    for at, parts in enumerate((base, policy)):
        logits = jnp.concatenate(parts, axis=1)
        top_value = jnp.max(logits, axis=1, keepdims=True)
        exp_total = jnp.sum(jnp.exp(logits - top_value), axis=1, keepdims=True)
        picked = jnp.sum(jnp.where(is_target, logits, 0.0), axis=1, keepdims=True)
        for kind, value in enumerate((top_value, exp_total, picked)):
            packed = jnp.where(lane == 2 * kind + at, value, packed)
    stats_ref[...] = packed.T[:8]


def merge_kernel(one_ref, two_ref, out_ref):
    one, two = one_ref[...], two_ref[...]
    ceiling = jnp.maximum(one[0:2], two[0:2])
    exp_total = one[2:4] * jnp.exp(one[0:2] - ceiling) + two[2:4] * jnp.exp(two[0:2] - ceiling)
    out_ref[...] = jnp.concatenate([ceiling, exp_total, one[4:8] + two[4:8]], axis=0)


def result_kernel(tok_rows, own_ref, other_ref, columns_ref, policy_ref, ratio_ref, sums_ref):
    half = own_ref.shape[1]
    picked = []
    for ref, columns in ((own_ref, columns_ref[1]), (other_ref, columns_ref[2])):
        stats = ref[...]
        log_probs = stats[4:6] - stats[0:2] - jnp.log(stats[2:4])
        policy = log_probs[1:2]
        values = jnp.concatenate([policy, policy - log_probs[0:1]], axis=0)
        high = values.astype(jnp.bfloat16).astype(jnp.float32)
        middle = (values - high).astype(jnp.bfloat16).astype(jnp.float32)
        parts = [high, middle, values - high - middle, jnp.zeros_like(values)]
        rows = jnp.concatenate(parts, axis=0).astype(jnp.bfloat16)
        parts = jnp.dot(
            rows, columns.astype(jnp.bfloat16), preferred_element_type=jnp.float32
        )
        picked.append(parts[0:2] + parts[2:4] + parts[4:6])
    policy_ref[...] = picked[0][0:1, :tok_rows]
    ratio_ref[...] = picked[0][1:2, :tok_rows]
    sums_ref[...] = (picked[0] + picked[1])[1:2, 64 : 64 + SEQS]


def call(kernel, shapes, *operands, flops=0):
    size = sum(operand.size * operand.dtype.itemsize for operand in operands)
    return pl.pallas_call(
        kernel,
        out_shape=shapes,
        compiler_params=pltpu.CompilerParams(vmem_limit_bytes=32 << 20),
        cost_estimate=pl.CostEstimate(flops=flops, bytes_accessed=size, transcendentals=0),
    )(*operands)


def dense_on_device(
    hidden_in,
    expert_ids,
    gate_weights,
    targets,
    seq_ids,
    moe_gain,
    w_gate,
    w_up,
    w_down,
    final_gain,
    head_weight,
    adapter_down,
    adapter_up,
):
    tok_rows, features = hidden_in.shape
    devices = lax.axis_size("tensor")
    bits = devices.bit_length() - 1
    half = devices * tok_rows // 2
    my_index = lax.axis_index("tensor")
    (near_bit, near_mask), (far_bit, far_mask) = ((b, (1 << b) + 1) for b in range(1, bits))

    def array(dtype, *shape):
        return jax.ShapeDtypeStruct(shape, dtype)

    flags = call(flags_kernel, array(jnp.int32, 8, 128), flops=ROUND_FLOPS)
    flags, down_sent = lax.optimization_barrier((flags, w_down))
    mixing, held_rows, gain, last_gain = call(
        functools.partial(early_kernel, tok_rows, bits),
        [
            array(jnp.float32, 2 * tok_rows, 128),
            array(jnp.bfloat16, tok_rows, features),
            array(jnp.float32, 1, features),
            array(jnp.float32, 1, features),
        ],
        expert_ids.T,
        gate_weights.T,
        hidden_in,
        moe_gain[None],
        final_gain[None],
    )
    first = call(
        functools.partial(order_kernel, near_bit),
        array(jnp.bfloat16, 2 * tok_rows, features),
        flags,
        held_rows,
        exchange(hidden_in, near_mask),
        flops=ROUND_FLOPS,
    )
    second = exchange(first, far_mask)
    units = [w_gate.T, w_up.T, w_down]
    units = [exchange(unit, 1) for unit in units[:2] + [down_sent]] + units
    totals, sent = [], []
    for rows, more in ((first, [mixing]), (second, [])):
        outputs = call(
            expert_kernel,
            [
                array(dtype, 2 * tok_rows, features + 128 * len(more))
                for dtype in (jnp.float32, jnp.bfloat16)
            ],
            rows,
            gain,
            *units,
            *more,
            flops=3 * devices * tok_rows * features * w_gate.shape[1],
        )
        total, piece = call(
            add_kernel,
            [array(output.dtype, *output.shape) for output in outputs],
            outputs[0],
            exchange(outputs[1], near_mask),
            flops=ROUND_FLOPS // 16 * len(totals),
        )
        totals.append(total)
        sent.append(piece)
    sent[0], late_seq = lax.optimization_barrier((sent[0], seq_ids[None]))
    sent[1], late_targets = lax.optimization_barrier((sent[1], targets[None]))
    arrived = [exchange(piece, far_mask) for piece in sent]

    columns, *late = call(
        functools.partial(late_kernel, tok_rows, bits, far_bit),
        [
            array(jnp.float32, 3, half, 128),
            array(jnp.bfloat16, 2 * tok_rows, features),
            array(jnp.float32, 2 * tok_rows, features),
            array(jnp.float32, 2 * tok_rows, 128),
        ],
        late_targets,
        late_seq,
        first,
        second,
        *totals,
        arrived[0],
        last_gain,
    )
    stats = call(
        functools.partial(head_kernel, far_bit),
        array(jnp.float32, 8, half),
        *late,
        arrived[1],
        last_gain,
        columns,
        adapter_down.T,
        head_weight,
        exchange(head_weight, 1),
        adapter_up,
        exchange(adapter_up, 1),
        flops=2 * devices * tok_rows * features * head_weight.shape[1],
    )
    for mask in (near_mask, far_mask):
        stats = call(merge_kernel, array(jnp.float32, 8, half), stats, exchange(stats, mask))
    policy_own, ratio_own, seq_sums = call(
        lambda *refs: result_kernel(tok_rows, *refs),
        [array(jnp.float32, 1, tok_rows)] * 2 + [array(jnp.float32, 1, SEQS)],
        stats,
        exchange(stats, 1),
        columns,
    )
    return (policy_own[0], ratio_own[0], seq_sums[0])


def solution(mesh):
    in_specs = (
        P(("dp", "tensor"), None),
        P(("dp", "tensor"), None),
        P(("dp", "tensor"), None),
        P("dp"),
        P("dp"),
        P(),
        P(None, "tensor"),
        P(None, "tensor"),
        P("tensor", None),
        P(),
        P(None, "tensor"),
        P(),
        P(None, "tensor"),
    )
    out_specs = (P(("dp", "tensor")), P(("dp", "tensor")), P("dp"))
    devices = mesh.shape["tensor"]

    def on_device(hidden_in, expert_ids, *others):
        both_experts = expert_ids.shape[1] == 2 and devices == 2 * SPLIT
        step = dense_on_device if both_experts else routed_on_device
        return step(hidden_in, expert_ids, *others)

    return jax.shard_map(
        on_device, mesh=mesh, in_specs=in_specs, out_specs=out_specs, check_vma=False
    )
```

```python
import functools

import jax
import jax.numpy as jnp
from jax import lax
from jax.experimental import pallas as pl
from jax.experimental.pallas import tpu as pltpu
from jax.sharding import PartitionSpec as P

SPLIT = 4
SEQS = 16
ROUND_FLOPS = 16 << 30


epsilon = 1e-06


def rms_norm(values, norm_gain):
    mean_sq = jnp.mean(values * values, axis=-1, keepdims=True)
    return values * lax.rsqrt(mean_sq + epsilon) * norm_gain


def expert_piece(arrived, w_gate, w_up, w_down):
    features = arrived.shape[-1]
    flat_rows = arrived.reshape(-1, features)
    gate_proj = jnp.dot(flat_rows, w_gate, preferred_element_type=jnp.float32)
    up_proj = jnp.dot(flat_rows, w_up, preferred_element_type=jnp.float32)
    inner_act = (jax.nn.silu(gate_proj) * up_proj).astype(jnp.bfloat16)
    partial_value = jnp.dot(inner_act, w_down, preferred_element_type=jnp.float32)
    return lax.all_to_all(
        partial_value.reshape(arrived.shape), "tensor", split_axis=0, concat_axis=0, tiled=True
    )


def routed_on_device(
    hidden_in,
    expert_ids,
    gate_weights,
    targets,
    seq_ids,
    moe_gain,
    w_gate,
    w_up,
    w_down,
    final_gain,
    head_weight,
    adapter_down,
    adapter_up,
):
    tok_rows, features = hidden_in.shape
    top_count = expert_ids.shape[1]
    devices = lax.axis_size("tensor")
    experts = devices // SPLIT
    capacity = min(tok_rows, 2 * tok_rows * top_count // experts)
    my_index = lax.axis_index("tensor")
    moe_input = rms_norm(hidden_in.astype(jnp.float32), moe_gain).astype(jnp.bfloat16)
    flat_ids = expert_ids.reshape(-1)
    chosen_hot = (flat_ids[:, None] == jnp.arange(experts, dtype=jnp.int32)[None, :]).astype(
        jnp.int32
    )
    slot_pos = jnp.sum((jnp.cumsum(chosen_hot, axis=0) - chosen_hot) * chosen_hot, axis=1)
    target_slot = flat_ids * capacity + slot_pos
    placed = (
        target_slot[:, None] == jnp.arange(experts * capacity, dtype=jnp.int32)[None, :]
    ).reshape(tok_rows, top_count, experts * capacity)
    spread = jnp.any(placed, axis=1).astype(jnp.bfloat16)
    packed = lax.dot_general(
        spread, moe_input, (((0,), (0,)), ((), ())), preferred_element_type=jnp.float32
    ).astype(jnp.bfloat16)
    outgoing = jnp.broadcast_to(
        packed.reshape(experts, 1, capacity, features), (experts, SPLIT, capacity, features)
    ).reshape(devices, capacity, features)
    returned = expert_piece(
        lax.all_to_all(outgoing, "tensor", split_axis=0, concat_axis=0, tiled=True),
        w_gate,
        w_up,
        w_down,
    )
    summed = jnp.sum(returned.reshape(experts, SPLIT, capacity, features), axis=1).reshape(
        experts * capacity, features
    )
    mixing = jnp.sum(placed.astype(jnp.float32) * gate_weights[:, :, None], axis=1)
    residual_sum = hidden_in.astype(jnp.float32) + jnp.dot(
        mixing, summed, precision=lax.Precision.HIGHEST
    )
    final_input = rms_norm(residual_sum, final_gain).astype(jnp.bfloat16)
    vocab_dev = head_weight.shape[1]
    vocab_start = my_index * vocab_dev
    columns = jnp.arange(vocab_dev, dtype=jnp.int32)

    def summary(block_rows, block_latent, row_start):
        row_count = block_rows.shape[0]
        base_logits = jnp.dot(block_rows, head_weight, preferred_element_type=jnp.float32)
        policy_logits = base_logits + jnp.dot(
            block_latent, adapter_up, preferred_element_type=jnp.float32
        )
        wanted = lax.dynamic_slice_in_dim(targets, row_start, row_count) - vocab_start
        is_target = wanted[:, None] == columns[None, :]

        def reduce_logits(logits):
            top_value = jnp.max(logits, axis=1)
            exp_total = jnp.sum(jnp.exp(logits - top_value[:, None]), axis=1)
            picked = jnp.sum(jnp.where(is_target, logits, 0.0), axis=1)
            return (top_value, exp_total, picked)

        base_stats = reduce_logits(base_logits)
        policy_stats = reduce_logits(policy_logits)
        return tuple(
            (
                jnp.stack([earlier, later], axis=1)
                for earlier, later in zip(base_stats, policy_stats)
            )
        )

    def blocked(shard_rows, shard_latent, row_start):
        row_count = shard_rows.shape[0]
        block_size = 512 if row_count % 512 == 0 else row_count
        if block_size == row_count:
            return summary(shard_rows, shard_latent, row_start)

        def one_block(block_index):
            offset = block_index * block_size
            return summary(
                lax.dynamic_slice_in_dim(shard_rows, offset, block_size),
                lax.dynamic_slice_in_dim(shard_latent, offset, block_size),
                row_start + offset,
            )

        results = lax.map(one_block, jnp.arange(row_count // block_size, dtype=jnp.int32))
        return tuple((member.reshape(row_count, 2) for member in results))

    shard_rows = lax.all_gather(final_input, "tensor", axis=0, tiled=True)
    shard_latent = jnp.dot(shard_rows, adapter_down, preferred_element_type=jnp.float32).astype(
        jnp.bfloat16
    )
    block_stats = blocked(shard_rows, shard_latent, jnp.int32(0))
    maxima, exp_sums, target_logits = tuple((update for update in block_stats))
    ceiling = lax.pmax(maxima, "tensor")
    totals, picked_all = lax.psum((exp_sums * jnp.exp(maxima - ceiling), target_logits), "tensor")
    log_probs = picked_all - ceiling - jnp.log(totals)
    log_ratio = log_probs[:, 1] - log_probs[:, 0]
    seq_match = (seq_ids[None, :] == jnp.arange(SEQS, dtype=jnp.int32)[:, None]).astype(jnp.float32)
    seq_sums = jnp.dot(seq_match, log_ratio, precision=lax.Precision.HIGHEST)
    own_start = my_index * tok_rows
    policy_own = lax.dynamic_slice_in_dim(log_probs[:, 1], own_start, tok_rows)
    ratio_own = lax.dynamic_slice_in_dim(log_ratio, own_start, tok_rows)
    return (policy_own, ratio_own, seq_sums)


def exchange(values, mask):
    devices = lax.axis_size("tensor")
    return lax.ppermute(values, "tensor", [(i, i ^ mask) for i in range(devices)])


def bit(number, place):
    return (number >> place) & 1


def in_order(late, mine, other):
    return jnp.concatenate([jnp.where(late, other, mine), jnp.where(late, mine, other)], axis=0)


def token_at(place, tok_rows, bits):
    devices = 1 << bits
    rank = place // tok_rows
    parity = rank >> (bits - 1)
    device = parity * 0
    low = parity
    for b in range(1, bits):
        one = (rank >> (b - 1)) & 1
        device = device + one * (1 << b)
        low = low ^ one
    return (device + low) * tok_rows + place % tok_rows


TRANSPOSED = (((1,), (1,)), ((), ()))


def places(tok_rows, bits):
    my_index = lax.axis_index("tensor")
    parity = sum(bit(my_index, b) for b in range(bits)) & 1
    return my_index, parity, tok_rows << (bits - 1)


def early_kernel(tok_rows, bits, *refs):
    (ids_ref, gates_ref), (mixing_ref,) = refs[0:2], refs[5:6]
    for in_ref, out_ref in zip(refs[2:5], refs[6:9]):
        out_ref[...] = in_ref[...]
    my_index, parity, half = places(tok_rows, bits)
    experts = gates_ref.shape[0]
    rows = [
        sum(
            jnp.where(ids_ref[k : k + 1] == expert, gates_ref[k : k + 1], 0.0)
            for k in range(ids_ref.shape[0])
        )
        for expert in range(experts)
    ]
    weights = jnp.concatenate(rows, axis=0)
    high = weights.astype(jnp.bfloat16).astype(jnp.float32)
    middle = (weights - high).astype(jnp.bfloat16).astype(jnp.float32)
    low = weights - high - middle
    rows = [high, middle, low, jnp.zeros((8 - 3 * experts, tok_rows), jnp.float32)]
    rows = [jnp.concatenate(rows, axis=0), jnp.zeros((8, 128 - tok_rows), jnp.float32)]
    parts = jnp.concatenate(rows, axis=1).T[:tok_rows]
    parts = jnp.concatenate([parts] * 16, axis=1)
    lane = lax.broadcasted_iota(jnp.int32, parts.shape, 1)
    token = token_at(lane // 8 * tok_rows + parity * half, tok_rows, bits)
    mine = (lane < half // tok_rows * 8) & (token // tok_rows == my_index)
    mixing = jnp.where(mine, parts, 0.0)
    mixing_ref[...] = jnp.concatenate([mixing, jnp.zeros_like(mixing)], axis=0)


def columns_kernel(tok_rows, bits, targets_ref, seq_ref, columns_ref):
    my_index, parity, half = places(tok_rows, bits)
    row = lax.broadcasted_iota(jnp.int32, (half, 128), 0)
    lane = lax.broadcasted_iota(jnp.int32, (half, 128), 1)
    token = token_at(row + parity * half, tok_rows, bits) - my_index * tok_rows
    wanted = half_columns(targets_ref[...], tok_rows, bits, parity)
    own_seq = half_columns(seq_ref[...], tok_rows, bits, parity)
    other_seq = half_columns(seq_ref[...], tok_rows, bits, 1 - parity)
    picks = (token == lane) & (lane < tok_rows) | (own_seq == lane - 64) & (lane >= 64)
    columns_ref[0] = jnp.where(lane == 0, wanted, 0).astype(jnp.float32)
    columns_ref[1] = picks.astype(jnp.float32)
    columns_ref[2] = ((other_seq == lane - 64) & (lane >= 64)).astype(jnp.float32)


def flags_kernel(flags_ref):
    row = lax.broadcasted_iota(jnp.int32, flags_ref.shape, 0)
    flags_ref[...] = bit(lax.axis_index("tensor"), row)


def order_kernel(place, flags_ref, mine_ref, other_ref, out_ref):
    late = flags_ref[place : place + 1, 0:1] == 1
    rows = in_order(late, *(ref[...].astype(jnp.float32) for ref in (mine_ref, other_ref)))
    out_ref[...] = rows.astype(out_ref.dtype)


def expert_kernel(rows_ref, gain_ref, *refs):
    far_refs, near_refs, mixing_refs, (total_ref, sent_ref) = (
        refs[0:3],
        refs[3:6],
        refs[6:-2],
        refs[-2:],
    )
    hidden = rows_ref[...].astype(jnp.float32)
    scale = lax.rsqrt(jnp.mean(hidden * hidden, axis=-1, keepdims=True) + epsilon)
    moe_input = (hidden * gain_ref[...]).astype(jnp.bfloat16)

    def units(gate_ref, up_ref, down_ref):
        projections = [
            scale
            * lax.dot_general(moe_input, ref[...], TRANSPOSED, preferred_element_type=jnp.float32)
            for ref in (gate_ref, up_ref)
        ]
        inner_act = (jax.nn.silu(projections[0]) * projections[1]).astype(jnp.bfloat16)
        return jnp.dot(inner_act, down_ref[...], preferred_element_type=jnp.float32)

    total = units(*near_refs) + units(*far_refs)
    total = jnp.concatenate([total, *(ref[...] for ref in mixing_refs)], axis=1)
    total_ref[...] = total
    sent_ref[...] = total.astype(jnp.bfloat16)


def add_kernel(total_ref, arrived_ref, sum_ref, sent_ref):
    total = total_ref[...] + arrived_ref[...].astype(jnp.float32)
    sum_ref[...] = total
    sent_ref[...] = total.astype(jnp.bfloat16)


def late_kernel(
    tok_rows,
    bits,
    place,
    targets_ref,
    seq_ref,
    first_ref,
    second_ref,
    first_total_ref,
    second_total_ref,
    arrived_ref,
    gain_ref,
    columns_ref,
    final_ref,
    partial_ref,
    weight_ref,
):
    columns_kernel(tok_rows, bits, targets_ref, seq_ref, columns_ref)
    features = first_ref.shape[1]
    my_index = lax.axis_index("tensor")
    expert = my_index // SPLIT
    mixing = first_total_ref[:tok_rows, features:]
    mixing = mixing + arrived_ref[:, features:].astype(jnp.float32)[:tok_rows]
    lane = lax.broadcasted_iota(jnp.int32, mixing.shape, 1)

    def weights(side, which):
        blocks = [
            jnp.sum(
                jnp.where((lane // 8 == 2 * side + k) & (lane % 2 == which), mixing, 0.0),
                axis=1,
                keepdims=True,
            )
            for k in range(2)
        ]
        return jnp.concatenate(blocks, axis=0)

    side = bit(my_index, place)
    partial_value = weights(side, expert) * first_total_ref[:, :features]
    partial_ref[...] = first_ref[...].astype(jnp.float32) + partial_value
    weight_ref[...] = jnp.broadcast_to(weights(side, 1 - expert), weight_ref.shape)
    mixed = second_ref[...].astype(jnp.float32)
    mixed = mixed + weights(1 - side, expert) * second_total_ref[...]
    arrived = arrived_ref[:, :features].astype(jnp.float32)
    mixed = mixed + weights(1 - side, 1 - expert) * arrived
    final_ref[...] = rms_norm(mixed, gain_ref[...]).astype(jnp.bfloat16)


def half_columns(values, tok_rows, bits, parity):
    tokens = values.shape[1]
    half = tokens // 2
    place = lax.broadcasted_iota(jnp.int32, (half, tokens), 0) + parity * half
    token = lax.broadcasted_iota(jnp.int32, (half, tokens), 1)
    here = token_at(place, tok_rows, bits) == token
    column = jnp.sum(jnp.where(here, values.astype(jnp.float32), 0.0), axis=1, keepdims=True)
    return column.astype(jnp.int32)


def head_kernel(place, *refs):
    (final_ref, partial_ref, weight_ref, arrived_ref, gain_ref, columns_ref, down_ref) = refs[0:7]
    weight_refs, (stats_ref,) = refs[7:11], refs[11:]
    my_index = lax.axis_index("tensor")
    mixed = partial_ref[...] + weight_ref[:, 0:1] * arrived_ref[...].astype(jnp.float32)
    first = rms_norm(mixed, gain_ref[...]).astype(jnp.bfloat16)
    rows = in_order(bit(my_index, place) == 1, first, final_ref[...])
    tokens = rows.shape[0]
    wanted = columns_ref[0][:, 0:1].astype(jnp.int32)
    latent = lax.dot_general(rows, down_ref[...], TRANSPOSED, preferred_element_type=jnp.float32)
    latent = latent.astype(jnp.bfloat16)
    lane = lax.broadcasted_iota(jnp.int32, (tokens, 128), 1)
    packed = jnp.zeros((tokens, 128), jnp.float32)
    base, policy, matches = [], [], []
    for index, head_ref, up_ref in zip((my_index, my_index ^ 1), weight_refs[:2], weight_refs[2:]):
        logits = jnp.dot(rows, head_ref[...], preferred_element_type=jnp.float32)
        base.append(logits)
        change = jnp.dot(latent, up_ref[...], preferred_element_type=jnp.float32)
        policy.append(logits + change)
        column = lax.broadcasted_iota(jnp.int32, logits.shape, 1)
        matches.append(column == wanted - index * logits.shape[1])
    is_target = jnp.concatenate(matches, axis=1)
    for at, parts in enumerate((base, policy)):
        logits = jnp.concatenate(parts, axis=1)
        top_value = jnp.max(logits, axis=1, keepdims=True)
        exp_total = jnp.sum(jnp.exp(logits - top_value), axis=1, keepdims=True)
        picked = jnp.sum(jnp.where(is_target, logits, 0.0), axis=1, keepdims=True)
        for kind, value in enumerate((top_value, exp_total, picked)):
            packed = jnp.where(lane == 2 * kind + at, value, packed)
    stats_ref[...] = packed.T[:8]


def merge_kernel(one_ref, two_ref, out_ref):
    one, two = one_ref[...], two_ref[...]
    ceiling = jnp.maximum(one[0:2], two[0:2])
    exp_total = one[2:4] * jnp.exp(one[0:2] - ceiling) + two[2:4] * jnp.exp(two[0:2] - ceiling)
    out_ref[...] = jnp.concatenate([ceiling, exp_total, one[4:8] + two[4:8]], axis=0)


def result_kernel(tok_rows, own_ref, other_ref, columns_ref, policy_ref, ratio_ref, sums_ref):
    half = own_ref.shape[1]
    picked = []
    for ref, columns in ((own_ref, columns_ref[1]), (other_ref, columns_ref[2])):
        stats = ref[...]
        log_probs = stats[4:6] - stats[0:2] - jnp.log(stats[2:4])
        policy = log_probs[1:2]
        values = jnp.concatenate([policy, policy - log_probs[0:1]], axis=0)
        high = values.astype(jnp.bfloat16).astype(jnp.float32)
        middle = (values - high).astype(jnp.bfloat16).astype(jnp.float32)
        parts = [high, middle, values - high - middle, jnp.zeros_like(values)]
        rows = jnp.concatenate(parts, axis=0).astype(jnp.bfloat16)
        parts = jnp.dot(
            rows, columns.astype(jnp.bfloat16), preferred_element_type=jnp.float32
        )
        picked.append(parts[0:2] + parts[2:4] + parts[4:6])
    policy_ref[...] = picked[0][0:1, :tok_rows]
    ratio_ref[...] = picked[0][1:2, :tok_rows]
    sums_ref[...] = (picked[0] + picked[1])[1:2, 64 : 64 + SEQS]


def call(kernel, shapes, *operands, flops=0):
    size = sum(operand.size * operand.dtype.itemsize for operand in operands)
    return pl.pallas_call(
        kernel,
        out_shape=shapes,
        compiler_params=pltpu.CompilerParams(vmem_limit_bytes=32 << 20),
        cost_estimate=pl.CostEstimate(flops=flops, bytes_accessed=size, transcendentals=0),
    )(*operands)


def dense_on_device(
    hidden_in,
    expert_ids,
    gate_weights,
    targets,
    seq_ids,
    moe_gain,
    w_gate,
    w_up,
    w_down,
    final_gain,
    head_weight,
    adapter_down,
    adapter_up,
):
    tok_rows, features = hidden_in.shape
    devices = lax.axis_size("tensor")
    bits = devices.bit_length() - 1
    half = devices * tok_rows // 2
    my_index = lax.axis_index("tensor")
    (near_bit, near_mask), (far_bit, far_mask) = ((b, (1 << b) + 1) for b in range(1, bits))

    def array(dtype, *shape):
        return jax.ShapeDtypeStruct(shape, dtype)

    flags = call(flags_kernel, array(jnp.int32, 8, 128), flops=ROUND_FLOPS)
    flags, sent_d = lax.optimization_barrier((flags, w_down))
    mixing, held_rows, gain, last_gain = call(
        functools.partial(early_kernel, tok_rows, bits),
        [
            array(jnp.float32, 2 * tok_rows, 128),
            array(jnp.bfloat16, tok_rows, features),
            array(jnp.float32, 1, features),
            array(jnp.float32, 1, features),
        ],
        expert_ids.T,
        gate_weights.T,
        hidden_in,
        moe_gain[None],
        final_gain[None],
    )
    first = call(
        functools.partial(order_kernel, near_bit),
        array(jnp.bfloat16, 2 * tok_rows, features),
        flags,
        held_rows,
        exchange(hidden_in, near_mask),
        flops=ROUND_FLOPS,
    )
    second = exchange(first, far_mask)
    units = [w_gate.T, w_up.T, w_down]
    units = [exchange(unit, 1) for unit in (units[0], units[1], sent_d)] + units
    totals, sent = [], []
    for rows, more in ((first, [mixing]), (second, [])):
        outputs = call(
            expert_kernel,
            [
                array(dtype, 2 * tok_rows, features + 128 * len(more))
                for dtype in (jnp.float32, jnp.bfloat16)
            ],
            rows,
            gain,
            *units,
            *more,
            flops=3 * devices * tok_rows * features * w_gate.shape[1],
        )
        total, piece = call(
            add_kernel,
            [array(output.dtype, *output.shape) for output in outputs],
            outputs[0],
            exchange(outputs[1], near_mask),
            flops=ROUND_FLOPS // 16 * len(totals),
        )
        totals.append(total)
        sent.append(piece)
    sent[0], late_seq = lax.optimization_barrier((sent[0], seq_ids[None]))
    sent[1], late_targets = lax.optimization_barrier((sent[1], targets[None]))
    arrived = [exchange(piece, far_mask) for piece in sent]

    columns, *late = call(
        functools.partial(late_kernel, tok_rows, bits, far_bit),
        [
            array(jnp.float32, 3, half, 128),
            array(jnp.bfloat16, 2 * tok_rows, features),
            array(jnp.float32, 2 * tok_rows, features),
            array(jnp.float32, 2 * tok_rows, 128),
        ],
        late_targets,
        late_seq,
        first,
        second,
        *totals,
        arrived[0],
        last_gain,
    )
    stats = call(
        functools.partial(head_kernel, far_bit),
        array(jnp.float32, 8, half),
        *late,
        arrived[1],
        last_gain,
        columns,
        adapter_down.T,
        head_weight,
        exchange(head_weight, 1),
        adapter_up,
        exchange(adapter_up, 1),
        flops=2 * devices * tok_rows * features * head_weight.shape[1],
    )
    for mask in (far_mask, near_mask):
        stats = call(merge_kernel, array(jnp.float32, 8, half), stats, exchange(stats, mask))
    policy_own, ratio_own, seq_sums = call(
        lambda *refs: result_kernel(tok_rows, *refs),
        [array(jnp.float32, 1, tok_rows)] * 2 + [array(jnp.float32, 1, SEQS)],
        stats,
        exchange(stats, 1),
        columns,
    )
    return (policy_own[0], ratio_own[0], seq_sums[0])


def solution(mesh):
    in_specs = (
        P(("dp", "tensor"), None),
        P(("dp", "tensor"), None),
        P(("dp", "tensor"), None),
        P("dp"),
        P("dp"),
        P(),
        P(None, "tensor"),
        P(None, "tensor"),
        P("tensor", None),
        P(),
        P(None, "tensor"),
        P(),
        P(None, "tensor"),
    )
    out_specs = (P(("dp", "tensor")), P(("dp", "tensor")), P("dp"))
    devices = mesh.shape["tensor"]

    def on_device(hidden_in, expert_ids, *others):
        both_experts = expert_ids.shape[1] == 2 and devices == 2 * SPLIT
        step = dense_on_device if both_experts else routed_on_device
        return step(hidden_in, expert_ids, *others)

    return jax.shard_map(
        on_device, mesh=mesh, in_specs=in_specs, out_specs=out_specs, check_vma=False
    )
```

```python
import functools

import jax
import jax.numpy as jnp
from jax import lax
from jax.experimental import pallas as pl
from jax.experimental.pallas import tpu as pltpu
from jax.sharding import PartitionSpec as P

SPLIT = 4
SEQS = 16
ROUND_FLOPS = 16 << 30


epsilon = 1e-06


def rms_norm(values, norm_gain):
    mean_sq = jnp.mean(values * values, axis=-1, keepdims=True)
    return values * lax.rsqrt(mean_sq + epsilon) * norm_gain


def expert_piece(arrived, w_gate, w_up, w_down):
    features = arrived.shape[-1]
    flat_rows = arrived.reshape(-1, features)
    gate_proj = jnp.dot(flat_rows, w_gate, preferred_element_type=jnp.float32)
    up_proj = jnp.dot(flat_rows, w_up, preferred_element_type=jnp.float32)
    inner_act = (jax.nn.silu(gate_proj) * up_proj).astype(jnp.bfloat16)
    partial_value = jnp.dot(inner_act, w_down, preferred_element_type=jnp.float32)
    return lax.all_to_all(
        partial_value.reshape(arrived.shape), "tensor", split_axis=0, concat_axis=0, tiled=True
    )


def routed_on_device(
    hidden_in,
    expert_ids,
    gate_weights,
    targets,
    seq_ids,
    moe_gain,
    w_gate,
    w_up,
    w_down,
    final_gain,
    head_weight,
    adapter_down,
    adapter_up,
):
    tok_rows, features = hidden_in.shape
    top_count = expert_ids.shape[1]
    devices = lax.axis_size("tensor")
    experts = devices // SPLIT
    capacity = min(tok_rows, 2 * tok_rows * top_count // experts)
    my_index = lax.axis_index("tensor")
    moe_input = rms_norm(hidden_in.astype(jnp.float32), moe_gain).astype(jnp.bfloat16)
    flat_ids = expert_ids.reshape(-1)
    chosen_hot = (flat_ids[:, None] == jnp.arange(experts, dtype=jnp.int32)[None, :]).astype(
        jnp.int32
    )
    slot_pos = jnp.sum((jnp.cumsum(chosen_hot, axis=0) - chosen_hot) * chosen_hot, axis=1)
    target_slot = flat_ids * capacity + slot_pos
    placed = (
        target_slot[:, None] == jnp.arange(experts * capacity, dtype=jnp.int32)[None, :]
    ).reshape(tok_rows, top_count, experts * capacity)
    spread = jnp.any(placed, axis=1).astype(jnp.bfloat16)
    packed = lax.dot_general(
        spread, moe_input, (((0,), (0,)), ((), ())), preferred_element_type=jnp.float32
    ).astype(jnp.bfloat16)
    outgoing = jnp.broadcast_to(
        packed.reshape(experts, 1, capacity, features), (experts, SPLIT, capacity, features)
    ).reshape(devices, capacity, features)
    returned = expert_piece(
        lax.all_to_all(outgoing, "tensor", split_axis=0, concat_axis=0, tiled=True),
        w_gate,
        w_up,
        w_down,
    )
    summed = jnp.sum(returned.reshape(experts, SPLIT, capacity, features), axis=1).reshape(
        experts * capacity, features
    )
    mixing = jnp.sum(placed.astype(jnp.float32) * gate_weights[:, :, None], axis=1)
    residual_sum = hidden_in.astype(jnp.float32) + jnp.dot(
        mixing, summed, precision=lax.Precision.HIGHEST
    )
    final_input = rms_norm(residual_sum, final_gain).astype(jnp.bfloat16)
    vocab_dev = head_weight.shape[1]
    vocab_start = my_index * vocab_dev
    columns = jnp.arange(vocab_dev, dtype=jnp.int32)

    def summary(block_rows, block_latent, row_start):
        row_count = block_rows.shape[0]
        base_logits = jnp.dot(block_rows, head_weight, preferred_element_type=jnp.float32)
        policy_logits = base_logits + jnp.dot(
            block_latent, adapter_up, preferred_element_type=jnp.float32
        )
        wanted = lax.dynamic_slice_in_dim(targets, row_start, row_count) - vocab_start
        is_target = wanted[:, None] == columns[None, :]

        def reduce_logits(logits):
            top_value = jnp.max(logits, axis=1)
            exp_total = jnp.sum(jnp.exp(logits - top_value[:, None]), axis=1)
            picked = jnp.sum(jnp.where(is_target, logits, 0.0), axis=1)
            return (top_value, exp_total, picked)

        base_stats = reduce_logits(base_logits)
        policy_stats = reduce_logits(policy_logits)
        return tuple(
            (
                jnp.stack([earlier, later], axis=1)
                for earlier, later in zip(base_stats, policy_stats)
            )
        )

    def blocked(shard_rows, shard_latent, row_start):
        row_count = shard_rows.shape[0]
        block_size = 512 if row_count % 512 == 0 else row_count
        if block_size == row_count:
            return summary(shard_rows, shard_latent, row_start)

        def one_block(block_index):
            offset = block_index * block_size
            return summary(
                lax.dynamic_slice_in_dim(shard_rows, offset, block_size),
                lax.dynamic_slice_in_dim(shard_latent, offset, block_size),
                row_start + offset,
            )

        results = lax.map(one_block, jnp.arange(row_count // block_size, dtype=jnp.int32))
        return tuple((member.reshape(row_count, 2) for member in results))

    shard_rows = lax.all_gather(final_input, "tensor", axis=0, tiled=True)
    shard_latent = jnp.dot(shard_rows, adapter_down, preferred_element_type=jnp.float32).astype(
        jnp.bfloat16
    )
    block_stats = blocked(shard_rows, shard_latent, jnp.int32(0))
    maxima, exp_sums, target_logits = tuple((update for update in block_stats))
    ceiling = lax.pmax(maxima, "tensor")
    totals, picked_all = lax.psum((exp_sums * jnp.exp(maxima - ceiling), target_logits), "tensor")
    log_probs = picked_all - ceiling - jnp.log(totals)
    log_ratio = log_probs[:, 1] - log_probs[:, 0]
    seq_match = (seq_ids[None, :] == jnp.arange(SEQS, dtype=jnp.int32)[:, None]).astype(jnp.float32)
    seq_sums = jnp.dot(seq_match, log_ratio, precision=lax.Precision.HIGHEST)
    own_start = my_index * tok_rows
    policy_own = lax.dynamic_slice_in_dim(log_probs[:, 1], own_start, tok_rows)
    ratio_own = lax.dynamic_slice_in_dim(log_ratio, own_start, tok_rows)
    return (policy_own, ratio_own, seq_sums)


def exchange(values, mask):
    devices = lax.axis_size("tensor")
    return lax.ppermute(values, "tensor", [(i, i ^ mask) for i in range(devices)])


def bit(number, place):
    return (number >> place) & 1


def in_order(late, mine, other):
    return jnp.concatenate([jnp.where(late, other, mine), jnp.where(late, mine, other)], axis=0)


def token_at(place, tok_rows, bits):
    devices = 1 << bits
    rank = place // tok_rows
    parity = rank >> (bits - 1)
    device = parity * 0
    low = parity
    for b in range(1, bits):
        one = (rank >> (b - 1)) & 1
        device = device + one * (1 << b)
        low = low ^ one
    return (device + low) * tok_rows + place % tok_rows


TRANSPOSED = (((1,), (1,)), ((), ()))


def places(tok_rows, bits):
    my_index = lax.axis_index("tensor")
    parity = sum(bit(my_index, b) for b in range(bits)) & 1
    return my_index, parity, tok_rows << (bits - 1)


def early_kernel(tok_rows, bits, *refs):
    (ids_ref, gates_ref), (mixing_ref,) = refs[0:2], refs[5:6]
    for in_ref, out_ref in zip(refs[2:5], refs[6:9]):
        out_ref[...] = in_ref[...]
    my_index, parity, half = places(tok_rows, bits)
    experts = gates_ref.shape[0]
    rows = [
        sum(
            jnp.where(ids_ref[k : k + 1] == expert, gates_ref[k : k + 1], 0.0)
            for k in range(ids_ref.shape[0])
        )
        for expert in range(experts)
    ]
    weights = jnp.concatenate(rows, axis=0)
    high = weights.astype(jnp.bfloat16).astype(jnp.float32)
    middle = (weights - high).astype(jnp.bfloat16).astype(jnp.float32)
    low = weights - high - middle
    rows = [high, middle, low, jnp.zeros((8 - 3 * experts, tok_rows), jnp.float32)]
    rows = [jnp.concatenate(rows, axis=0), jnp.zeros((8, 128 - tok_rows), jnp.float32)]
    parts = jnp.concatenate(rows, axis=1).T[:tok_rows]
    parts = jnp.concatenate([parts] * 16, axis=1)
    lane = lax.broadcasted_iota(jnp.int32, parts.shape, 1)
    token = token_at(lane // 8 * tok_rows + parity * half, tok_rows, bits)
    mine = (lane < half // tok_rows * 8) & (token // tok_rows == my_index)
    mixing = jnp.where(mine, parts, 0.0)
    mixing_ref[...] = jnp.concatenate([mixing, jnp.zeros_like(mixing)], axis=0)


def columns_kernel(tok_rows, bits, targets_ref, seq_ref, columns_ref):
    my_index, parity, half = places(tok_rows, bits)
    row = lax.broadcasted_iota(jnp.int32, (half, 128), 0)
    lane = lax.broadcasted_iota(jnp.int32, (half, 128), 1)
    token = token_at(row + parity * half, tok_rows, bits) - my_index * tok_rows
    wanted = half_columns(targets_ref[...], tok_rows, bits, parity)
    own_seq = half_columns(seq_ref[...], tok_rows, bits, parity)
    other_seq = half_columns(seq_ref[...], tok_rows, bits, 1 - parity)
    picks = (token == lane) & (lane < tok_rows) | (own_seq == lane - 64) & (lane >= 64)
    columns_ref[0] = jnp.where(lane == 0, wanted, 0).astype(jnp.float32)
    columns_ref[1] = picks.astype(jnp.float32)
    columns_ref[2] = ((other_seq == lane - 64) & (lane >= 64)).astype(jnp.float32)


def flags_kernel(flags_ref):
    row = lax.broadcasted_iota(jnp.int32, flags_ref.shape, 0)
    flags_ref[...] = bit(lax.axis_index("tensor"), row)


def order_kernel(place, flags_ref, mine_ref, other_ref, out_ref):
    late = flags_ref[place : place + 1, 0:1] == 1
    rows = in_order(late, *(ref[...].astype(jnp.float32) for ref in (mine_ref, other_ref)))
    out_ref[...] = rows.astype(out_ref.dtype)


def expert_kernel(rows_ref, gain_ref, *refs):
    far_refs, near_refs, mixing_refs, (total_ref, sent_ref) = (
        refs[0:3],
        refs[3:6],
        refs[6:-2],
        refs[-2:],
    )
    moe_input = rms_norm(rows_ref[...].astype(jnp.float32), gain_ref[...]).astype(jnp.bfloat16)

    def units(gate_ref, up_ref, down_ref):
        projections = [
            lax.dot_general(moe_input, ref[...], TRANSPOSED, preferred_element_type=jnp.float32)
            for ref in (gate_ref, up_ref)
        ]
        inner_act = (jax.nn.silu(projections[0]) * projections[1]).astype(jnp.bfloat16)
        return jnp.dot(inner_act, down_ref[...], preferred_element_type=jnp.float32)

    total = units(*near_refs) + units(*far_refs)
    total = jnp.concatenate([total, *(ref[...] for ref in mixing_refs)], axis=1)
    total_ref[...] = total
    sent_ref[...] = total.astype(jnp.bfloat16)


def add_kernel(total_ref, arrived_ref, sum_ref, sent_ref):
    total = total_ref[...] + arrived_ref[...].astype(jnp.float32)
    sum_ref[...] = total
    sent_ref[...] = total.astype(jnp.bfloat16)


def late_kernel(
    tok_rows,
    bits,
    place,
    targets_ref,
    seq_ref,
    first_ref,
    second_ref,
    first_total_ref,
    second_total_ref,
    arrived_ref,
    gain_ref,
    columns_ref,
    final_ref,
    partial_ref,
    weight_ref,
):
    columns_kernel(tok_rows, bits, targets_ref, seq_ref, columns_ref)
    features = first_ref.shape[1]
    my_index = lax.axis_index("tensor")
    expert = my_index // SPLIT
    mixing = first_total_ref[:tok_rows, features:]
    mixing = mixing + arrived_ref[:, features:].astype(jnp.float32)[:tok_rows]
    lane = lax.broadcasted_iota(jnp.int32, mixing.shape, 1)

    def weights(side, which):
        blocks = [
            jnp.sum(
                jnp.where((lane // 8 == 2 * side + k) & (lane % 2 == which), mixing, 0.0),
                axis=1,
                keepdims=True,
            )
            for k in range(2)
        ]
        return jnp.concatenate(blocks, axis=0)

    side = bit(my_index, place)
    partial_value = weights(side, expert) * first_total_ref[:, :features]
    partial_ref[...] = first_ref[...].astype(jnp.float32) + partial_value
    weight_ref[...] = jnp.broadcast_to(weights(side, 1 - expert), weight_ref.shape)
    mixed = second_ref[...].astype(jnp.float32)
    mixed = mixed + weights(1 - side, expert) * second_total_ref[...]
    arrived = arrived_ref[:, :features].astype(jnp.float32)
    mixed = mixed + weights(1 - side, 1 - expert) * arrived
    final_ref[...] = rms_norm(mixed, gain_ref[...]).astype(jnp.bfloat16)


def half_columns(values, tok_rows, bits, parity):
    tokens = values.shape[1]
    half = tokens // 2
    place = lax.broadcasted_iota(jnp.int32, (half, tokens), 0) + parity * half
    token = lax.broadcasted_iota(jnp.int32, (half, tokens), 1)
    here = token_at(place, tok_rows, bits) == token
    column = jnp.sum(jnp.where(here, values.astype(jnp.float32), 0.0), axis=1, keepdims=True)
    return column.astype(jnp.int32)


def head_kernel(place, *refs):
    (final_ref, partial_ref, weight_ref, arrived_ref, gain_ref, columns_ref, down_ref) = refs[0:7]
    weight_refs, (stats_ref,) = refs[7:11], refs[11:]
    my_index = lax.axis_index("tensor")
    mixed = partial_ref[...] + weight_ref[:, 0:1] * arrived_ref[...].astype(jnp.float32)
    first = rms_norm(mixed, gain_ref[...]).astype(jnp.bfloat16)
    rows = in_order(bit(my_index, place) == 1, first, final_ref[...])
    tokens = rows.shape[0]
    wanted = columns_ref[0][:, 0:1].astype(jnp.int32)
    latent = lax.dot_general(rows, down_ref[...], TRANSPOSED, preferred_element_type=jnp.float32)
    latent = latent.astype(jnp.bfloat16)
    lane = lax.broadcasted_iota(jnp.int32, (tokens, 128), 1)
    packed = jnp.zeros((tokens, 128), jnp.float32)
    base, policy, matches = [], [], []
    for index, head_ref, up_ref in zip((my_index, my_index ^ 1), weight_refs[:2], weight_refs[2:]):
        logits = jnp.dot(rows, head_ref[...], preferred_element_type=jnp.float32)
        base.append(logits)
        change = jnp.dot(latent, up_ref[...], preferred_element_type=jnp.float32)
        policy.append(logits + change)
        column = lax.broadcasted_iota(jnp.int32, logits.shape, 1)
        matches.append(column == wanted - index * logits.shape[1])
    is_target = jnp.concatenate(matches, axis=1)
    for at, parts in enumerate((base, policy)):
        logits = jnp.concatenate(parts, axis=1)
        top_value = jnp.max(logits, axis=1, keepdims=True)
        exp_total = jnp.sum(jnp.exp(logits - top_value), axis=1, keepdims=True)
        picked = jnp.sum(jnp.where(is_target, logits, 0.0), axis=1, keepdims=True)
        for kind, value in enumerate((top_value, exp_total, picked)):
            packed = jnp.where(lane == 2 * kind + at, value, packed)
    stats_ref[...] = packed.T[:8]


def merge_kernel(one_ref, two_ref, out_ref):
    one, two = one_ref[...], two_ref[...]
    ceiling = jnp.maximum(one[0:2], two[0:2])
    exp_total = one[2:4] * jnp.exp(one[0:2] - ceiling) + two[2:4] * jnp.exp(two[0:2] - ceiling)
    out_ref[...] = jnp.concatenate([ceiling, exp_total, one[4:8] + two[4:8]], axis=0)


def result_kernel(tok_rows, own_ref, other_ref, columns_ref, policy_ref, ratio_ref, sums_ref):
    half = own_ref.shape[1]
    picked = []
    for ref, columns in ((own_ref, columns_ref[1]), (other_ref, columns_ref[2])):
        stats = ref[...]
        log_probs = stats[4:6] - stats[0:2] - jnp.log(stats[2:4])
        policy = log_probs[1:2]
        values = jnp.concatenate([policy, policy - log_probs[0:1]], axis=0)
        high = values.astype(jnp.bfloat16).astype(jnp.float32)
        middle = (values - high).astype(jnp.bfloat16).astype(jnp.float32)
        parts = [high, middle, values - high - middle, jnp.zeros_like(values)]
        rows = jnp.concatenate(parts, axis=0).astype(jnp.bfloat16)
        parts = jnp.dot(
            rows, columns.astype(jnp.bfloat16), preferred_element_type=jnp.float32
        )
        picked.append(parts[0:2] + parts[2:4] + parts[4:6])
    policy_ref[...] = picked[0][0:1, :tok_rows]
    ratio_ref[...] = picked[0][1:2, :tok_rows]
    sums_ref[...] = (picked[0] + picked[1])[1:2, 64 : 64 + SEQS]


def call(kernel, shapes, *operands, flops=0):
    size = sum(operand.size * operand.dtype.itemsize for operand in operands)
    return pl.pallas_call(
        kernel,
        out_shape=shapes,
        compiler_params=pltpu.CompilerParams(vmem_limit_bytes=32 << 20),
        cost_estimate=pl.CostEstimate(flops=flops, bytes_accessed=size, transcendentals=0),
    )(*operands)


def dense_on_device(
    hidden_in,
    expert_ids,
    gate_weights,
    targets,
    seq_ids,
    moe_gain,
    w_gate,
    w_up,
    w_down,
    final_gain,
    head_weight,
    adapter_down,
    adapter_up,
):
    tok_rows, features = hidden_in.shape
    devices = lax.axis_size("tensor")
    bits = devices.bit_length() - 1
    half = devices * tok_rows // 2
    my_index = lax.axis_index("tensor")
    (near_bit, near_mask), (far_bit, far_mask) = ((b, (1 << b) + 1) for b in range(1, bits))

    def array(dtype, *shape):
        return jax.ShapeDtypeStruct(shape, dtype)

    flags = call(flags_kernel, array(jnp.int32, 8, 128), flops=ROUND_FLOPS)
    flags, sent_d = lax.optimization_barrier((flags, w_down))
    mixing, held_rows, gain, last_gain = call(
        functools.partial(early_kernel, tok_rows, bits),
        [
            array(jnp.float32, 2 * tok_rows, 128),
            array(jnp.bfloat16, tok_rows, features),
            array(jnp.float32, 1, features),
            array(jnp.float32, 1, features),
        ],
        expert_ids.T,
        gate_weights.T,
        hidden_in,
        moe_gain[None],
        final_gain[None],
    )
    first = call(
        functools.partial(order_kernel, near_bit),
        array(jnp.bfloat16, 2 * tok_rows, features),
        flags,
        held_rows,
        exchange(hidden_in, near_mask),
        flops=ROUND_FLOPS,
    )
    second = exchange(first, far_mask)
    units = [w_gate.T, w_up.T, w_down]
    units = [exchange(unit, 1) for unit in (units[0], units[1], sent_d)] + units
    totals, sent = [], []
    for rows, more in ((first, [mixing]), (second, [])):
        outputs = call(
            expert_kernel,
            [
                array(dtype, 2 * tok_rows, features + 128 * len(more))
                for dtype in (jnp.float32, jnp.bfloat16)
            ],
            rows,
            gain,
            *units,
            *more,
            flops=3 * devices * tok_rows * features * w_gate.shape[1],
        )
        total, piece = call(
            add_kernel,
            [array(output.dtype, *output.shape) for output in outputs],
            outputs[0],
            exchange(outputs[1], near_mask),
            flops=ROUND_FLOPS // 16 * len(totals),
        )
        totals.append(total)
        sent.append(piece)
    sent[0], late_seq = lax.optimization_barrier((sent[0], seq_ids[None]))
    sent[1], late_targets = lax.optimization_barrier((sent[1], targets[None]))
    arrived = [exchange(piece, far_mask) for piece in sent]

    columns, *late = call(
        functools.partial(late_kernel, tok_rows, bits, far_bit),
        [
            array(jnp.float32, 3, half, 128),
            array(jnp.bfloat16, 2 * tok_rows, features),
            array(jnp.float32, 2 * tok_rows, features),
            array(jnp.float32, 2 * tok_rows, 128),
        ],
        late_targets,
        late_seq,
        first,
        second,
        *totals,
        arrived[0],
        last_gain,
    )
    stats = call(
        functools.partial(head_kernel, far_bit),
        array(jnp.float32, 8, half),
        *late,
        arrived[1],
        last_gain,
        columns,
        adapter_down.T,
        head_weight,
        exchange(head_weight, 1),
        adapter_up,
        exchange(adapter_up, 1),
        flops=2 * devices * tok_rows * features * head_weight.shape[1],
    )
    for mask in (far_mask, near_mask):
        stats = call(merge_kernel, array(jnp.float32, 8, half), stats, exchange(stats, mask))
    policy_own, ratio_own, seq_sums = call(
        lambda *refs: result_kernel(tok_rows, *refs),
        [array(jnp.float32, 1, tok_rows)] * 2 + [array(jnp.float32, 1, SEQS)],
        stats,
        exchange(stats, 1),
        columns,
    )
    return (policy_own[0], ratio_own[0], seq_sums[0])


def solution(mesh):
    in_specs = (
        P(("dp", "tensor"), None),
        P(("dp", "tensor"), None),
        P(("dp", "tensor"), None),
        P("dp"),
        P("dp"),
        P(),
        P(None, "tensor"),
        P(None, "tensor"),
        P("tensor", None),
        P(),
        P(None, "tensor"),
        P(),
        P(None, "tensor"),
    )
    out_specs = (P(("dp", "tensor")), P(("dp", "tensor")), P("dp"))
    devices = mesh.shape["tensor"]

    def on_device(hidden_in, expert_ids, *others):
        both_experts = expert_ids.shape[1] == 2 and devices == 2 * SPLIT
        step = dense_on_device if both_experts else routed_on_device
        return step(hidden_in, expert_ids, *others)

    return jax.shard_map(
        on_device, mesh=mesh, in_specs=in_specs, out_specs=out_specs, check_vma=False
    )
```

```python
import functools

import jax
import jax.numpy as jnp
from jax import lax
from jax.experimental import pallas as pl
from jax.experimental.pallas import tpu as pltpu
from jax.sharding import PartitionSpec as P

SPLIT = 4
SEQS = 16
ROUND_FLOPS = 16 << 30


epsilon = 1e-06


def rms_norm(values, norm_gain):
    mean_sq = jnp.mean(values * values, axis=-1, keepdims=True)
    return values * lax.rsqrt(mean_sq + epsilon) * norm_gain


def expert_piece(arrived, w_gate, w_up, w_down):
    features = arrived.shape[-1]
    flat_rows = arrived.reshape(-1, features)
    gate_proj = jnp.dot(flat_rows, w_gate, preferred_element_type=jnp.float32)
    up_proj = jnp.dot(flat_rows, w_up, preferred_element_type=jnp.float32)
    inner_act = (jax.nn.silu(gate_proj) * up_proj).astype(jnp.bfloat16)
    partial_value = jnp.dot(inner_act, w_down, preferred_element_type=jnp.float32)
    return lax.all_to_all(
        partial_value.reshape(arrived.shape), "tensor", split_axis=0, concat_axis=0, tiled=True
    )


def routed_on_device(
    hidden_in,
    expert_ids,
    gate_weights,
    targets,
    seq_ids,
    moe_gain,
    w_gate,
    w_up,
    w_down,
    final_gain,
    head_weight,
    adapter_down,
    adapter_up,
):
    tok_rows, features = hidden_in.shape
    top_count = expert_ids.shape[1]
    devices = lax.axis_size("tensor")
    experts = devices // SPLIT
    capacity = min(tok_rows, 2 * tok_rows * top_count // experts)
    my_index = lax.axis_index("tensor")
    moe_input = rms_norm(hidden_in.astype(jnp.float32), moe_gain).astype(jnp.bfloat16)
    flat_ids = expert_ids.reshape(-1)
    chosen_hot = (flat_ids[:, None] == jnp.arange(experts, dtype=jnp.int32)[None, :]).astype(
        jnp.int32
    )
    slot_pos = jnp.sum((jnp.cumsum(chosen_hot, axis=0) - chosen_hot) * chosen_hot, axis=1)
    target_slot = flat_ids * capacity + slot_pos
    placed = (
        target_slot[:, None] == jnp.arange(experts * capacity, dtype=jnp.int32)[None, :]
    ).reshape(tok_rows, top_count, experts * capacity)
    spread = jnp.any(placed, axis=1).astype(jnp.bfloat16)
    packed = lax.dot_general(
        spread, moe_input, (((0,), (0,)), ((), ())), preferred_element_type=jnp.float32
    ).astype(jnp.bfloat16)
    outgoing = jnp.broadcast_to(
        packed.reshape(experts, 1, capacity, features), (experts, SPLIT, capacity, features)
    ).reshape(devices, capacity, features)
    returned = expert_piece(
        lax.all_to_all(outgoing, "tensor", split_axis=0, concat_axis=0, tiled=True),
        w_gate,
        w_up,
        w_down,
    )
    summed = jnp.sum(returned.reshape(experts, SPLIT, capacity, features), axis=1).reshape(
        experts * capacity, features
    )
    mixing = jnp.sum(placed.astype(jnp.float32) * gate_weights[:, :, None], axis=1)
    residual_sum = hidden_in.astype(jnp.float32) + jnp.dot(
        mixing, summed, precision=lax.Precision.HIGHEST
    )
    final_input = rms_norm(residual_sum, final_gain).astype(jnp.bfloat16)
    vocab_dev = head_weight.shape[1]
    vocab_start = my_index * vocab_dev
    columns = jnp.arange(vocab_dev, dtype=jnp.int32)

    def summary(block_rows, block_latent, row_start):
        row_count = block_rows.shape[0]
        base_logits = jnp.dot(block_rows, head_weight, preferred_element_type=jnp.float32)
        policy_logits = base_logits + jnp.dot(
            block_latent, adapter_up, preferred_element_type=jnp.float32
        )
        wanted = lax.dynamic_slice_in_dim(targets, row_start, row_count) - vocab_start
        is_target = wanted[:, None] == columns[None, :]

        def reduce_logits(logits):
            top_value = jnp.max(logits, axis=1)
            exp_total = jnp.sum(jnp.exp(logits - top_value[:, None]), axis=1)
            picked = jnp.sum(jnp.where(is_target, logits, 0.0), axis=1)
            return (top_value, exp_total, picked)

        base_stats = reduce_logits(base_logits)
        policy_stats = reduce_logits(policy_logits)
        return tuple(
            (
                jnp.stack([earlier, later], axis=1)
                for earlier, later in zip(base_stats, policy_stats)
            )
        )

    def blocked(shard_rows, shard_latent, row_start):
        row_count = shard_rows.shape[0]
        block_size = 512 if row_count % 512 == 0 else row_count
        if block_size == row_count:
            return summary(shard_rows, shard_latent, row_start)

        def one_block(block_index):
            offset = block_index * block_size
            return summary(
                lax.dynamic_slice_in_dim(shard_rows, offset, block_size),
                lax.dynamic_slice_in_dim(shard_latent, offset, block_size),
                row_start + offset,
            )

        results = lax.map(one_block, jnp.arange(row_count // block_size, dtype=jnp.int32))
        return tuple((member.reshape(row_count, 2) for member in results))

    shard_rows = lax.all_gather(final_input, "tensor", axis=0, tiled=True)
    shard_latent = jnp.dot(shard_rows, adapter_down, preferred_element_type=jnp.float32).astype(
        jnp.bfloat16
    )
    block_stats = blocked(shard_rows, shard_latent, jnp.int32(0))
    maxima, exp_sums, target_logits = tuple((update for update in block_stats))
    ceiling = lax.pmax(maxima, "tensor")
    totals, picked_all = lax.psum((exp_sums * jnp.exp(maxima - ceiling), target_logits), "tensor")
    log_probs = picked_all - ceiling - jnp.log(totals)
    log_ratio = log_probs[:, 1] - log_probs[:, 0]
    seq_match = (seq_ids[None, :] == jnp.arange(SEQS, dtype=jnp.int32)[:, None]).astype(jnp.float32)
    seq_sums = jnp.dot(seq_match, log_ratio, precision=lax.Precision.HIGHEST)
    own_start = my_index * tok_rows
    policy_own = lax.dynamic_slice_in_dim(log_probs[:, 1], own_start, tok_rows)
    ratio_own = lax.dynamic_slice_in_dim(log_ratio, own_start, tok_rows)
    return (policy_own, ratio_own, seq_sums)


def exchange(values, mask):
    devices = lax.axis_size("tensor")
    return lax.ppermute(values, "tensor", [(i, i ^ mask) for i in range(devices)])


def bit(number, place):
    return (number >> place) & 1


def in_order(late, mine, other):
    return jnp.concatenate([jnp.where(late, other, mine), jnp.where(late, mine, other)], axis=0)


def token_at(place, tok_rows, bits):
    devices = 1 << bits
    rank = place // tok_rows
    parity = rank >> (bits - 1)
    device = parity * 0
    low = parity
    for b in range(1, bits):
        one = (rank >> (b - 1)) & 1
        device = device + one * (1 << b)
        low = low ^ one
    return (device + low) * tok_rows + place % tok_rows


TRANSPOSED = (((1,), (1,)), ((), ()))


def places(tok_rows, bits):
    my_index = lax.axis_index("tensor")
    parity = sum(bit(my_index, b) for b in range(bits)) & 1
    return my_index, parity, tok_rows << (bits - 1)


def early_kernel(tok_rows, bits, *refs):
    (ids_ref, gates_ref), (mixing_ref,) = refs[0:2], refs[7:8]
    for in_ref, out_ref in zip(refs[2:7], refs[8:13]):
        out_ref[...] = in_ref[...]
    my_index, parity, half = places(tok_rows, bits)
    experts = gates_ref.shape[0]
    rows = [
        sum(
            jnp.where(ids_ref[k : k + 1] == expert, gates_ref[k : k + 1], 0.0)
            for k in range(ids_ref.shape[0])
        )
        for expert in range(experts)
    ]
    weights = jnp.concatenate(rows, axis=0)
    high = weights.astype(jnp.bfloat16).astype(jnp.float32)
    middle = (weights - high).astype(jnp.bfloat16).astype(jnp.float32)
    low = weights - high - middle
    rows = [high, middle, low, jnp.zeros((8 - 3 * experts, tok_rows), jnp.float32)]
    rows = [jnp.concatenate(rows, axis=0), jnp.zeros((8, 128 - tok_rows), jnp.float32)]
    parts = jnp.concatenate(rows, axis=1).T[:tok_rows]
    parts = jnp.concatenate([parts] * 16, axis=1)
    lane = lax.broadcasted_iota(jnp.int32, parts.shape, 1)
    token = token_at(lane // 8 * tok_rows + parity * half, tok_rows, bits)
    mine = (lane < half // tok_rows * 8) & (token // tok_rows == my_index)
    mixing = jnp.where(mine, parts, 0.0)
    mixing_ref[...] = jnp.concatenate([mixing, jnp.zeros_like(mixing)], axis=0)


def columns_kernel(tok_rows, bits, targets_ref, seq_ref, columns_ref):
    my_index, parity, half = places(tok_rows, bits)
    row = lax.broadcasted_iota(jnp.int32, (half, 128), 0)
    lane = lax.broadcasted_iota(jnp.int32, (half, 128), 1)
    token = token_at(row + parity * half, tok_rows, bits) - my_index * tok_rows
    wanted = half_columns(targets_ref[...], tok_rows, bits, parity)
    own_seq = half_columns(seq_ref[...], tok_rows, bits, parity)
    other_seq = half_columns(seq_ref[...], tok_rows, bits, 1 - parity)
    picks = (token == lane) & (lane < tok_rows) | (own_seq == lane - 64) & (lane >= 64)
    columns_ref[0] = jnp.where(lane == 0, wanted, 0).astype(jnp.float32)
    columns_ref[1] = picks.astype(jnp.float32)
    columns_ref[2] = ((other_seq == lane - 64) & (lane >= 64)).astype(jnp.float32)


def flags_kernel(flags_ref):
    row = lax.broadcasted_iota(jnp.int32, flags_ref.shape, 0)
    flags_ref[...] = bit(lax.axis_index("tensor"), row)


def order_kernel(place, flags_ref, mine_ref, other_ref, out_ref):
    late = flags_ref[place : place + 1, 0:1] == 1
    rows = in_order(late, *(ref[...].astype(jnp.float32) for ref in (mine_ref, other_ref)))
    out_ref[...] = rows.astype(out_ref.dtype)


def expert_kernel(rows_ref, gain_ref, *refs):
    far_refs, near_refs, mixing_refs, (total_ref, sent_ref) = (
        refs[0:3],
        refs[3:6],
        refs[6:-2],
        refs[-2:],
    )
    hidden = rows_ref[...].astype(jnp.float32)
    scale = lax.rsqrt(jnp.mean(hidden * hidden, axis=-1, keepdims=True) + epsilon)
    moe_input = (hidden * gain_ref[...]).astype(jnp.bfloat16)

    def units(gate_ref, up_ref, down_ref):
        projections = [
            scale
            * lax.dot_general(moe_input, ref[...], TRANSPOSED, preferred_element_type=jnp.float32)
            for ref in (gate_ref, up_ref)
        ]
        inner_act = (jax.nn.silu(projections[0]) * projections[1]).astype(jnp.bfloat16)
        return jnp.dot(inner_act, down_ref[...], preferred_element_type=jnp.float32)

    total = units(*near_refs) + units(*far_refs)
    total = jnp.concatenate([total, *(ref[...] for ref in mixing_refs)], axis=1)
    total_ref[...] = total
    sent_ref[...] = total.astype(jnp.bfloat16)


def add_kernel(total_ref, arrived_ref, sum_ref, sent_ref):
    total = total_ref[...] + arrived_ref[...].astype(jnp.float32)
    sum_ref[...] = total
    sent_ref[...] = total.astype(jnp.bfloat16)


def head_rows(rows, wanted, down_ref, weight_refs):
    my_index = lax.axis_index("tensor")
    wanted = wanted.astype(jnp.int32)
    latent = lax.dot_general(rows, down_ref[...], TRANSPOSED, preferred_element_type=jnp.float32)
    latent = latent.astype(jnp.bfloat16)
    lane = lax.broadcasted_iota(jnp.int32, (rows.shape[0], 128), 1)
    packed = jnp.zeros(lane.shape, jnp.float32)
    base, policy, matches = [], [], []
    for index, head_ref, up_ref in zip((my_index, my_index ^ 1), weight_refs[:2], weight_refs[2:]):
        logits = jnp.dot(rows, head_ref[...], preferred_element_type=jnp.float32)
        base.append(logits)
        change = jnp.dot(latent, up_ref[...], preferred_element_type=jnp.float32)
        policy.append(logits + change)
        column = lax.broadcasted_iota(jnp.int32, logits.shape, 1)
        matches.append(column == wanted - index * logits.shape[1])
    is_target = jnp.concatenate(matches, axis=1)
    for at, parts in enumerate((base, policy)):
        logits = jnp.concatenate(parts, axis=1)
        top_value = jnp.max(logits, axis=1, keepdims=True)
        exp_total = jnp.sum(jnp.exp(logits - top_value), axis=1, keepdims=True)
        picked = jnp.sum(jnp.where(is_target, logits, 0.0), axis=1, keepdims=True)
        for kind, value in enumerate((top_value, exp_total, picked)):
            packed = jnp.where(lane == 2 * kind + at, value, packed)
    return packed


def late_kernel(
    tok_rows,
    bits,
    place,
    targets_ref,
    seq_ref,
    first_ref,
    second_ref,
    first_total_ref,
    second_total_ref,
    arrived_ref,
    gain_ref,
    down_ref,
    head_ref,
    far_head_ref,
    up_ref,
    far_up_ref,
    columns_ref,
    later_ref,
    partial_ref,
    weight_ref,
):
    columns_kernel(tok_rows, bits, targets_ref, seq_ref, columns_ref)
    features = first_ref.shape[1]
    my_index = lax.axis_index("tensor")
    expert = my_index // SPLIT
    mixing = first_total_ref[:tok_rows, features:]
    mixing = mixing + arrived_ref[:, features:].astype(jnp.float32)[:tok_rows]
    lane = lax.broadcasted_iota(jnp.int32, mixing.shape, 1)

    def weights(side, which):
        blocks = [
            jnp.sum(
                jnp.where((lane // 8 == 2 * side + k) & (lane % 2 == which), mixing, 0.0),
                axis=1,
                keepdims=True,
            )
            for k in range(2)
        ]
        return jnp.concatenate(blocks, axis=0)

    side = bit(my_index, place)
    partial_value = weights(side, expert) * first_total_ref[:, :features]
    partial_ref[...] = first_ref[...].astype(jnp.float32) + partial_value
    weight_ref[...] = jnp.broadcast_to(weights(side, 1 - expert), weight_ref.shape)
    mixed = second_ref[...].astype(jnp.float32)
    mixed = mixed + weights(1 - side, expert) * second_total_ref[...]
    arrived = arrived_ref[:, :features].astype(jnp.float32)
    mixed = mixed + weights(1 - side, 1 - expert) * arrived
    rows = rms_norm(mixed, gain_ref[...]).astype(jnp.bfloat16)
    piece = rows.shape[0]
    wanted = columns_ref[0][:, 0:1]
    wanted = jnp.where(side == 1, wanted[:piece], wanted[piece:])
    weight_refs = (head_ref, far_head_ref, up_ref, far_up_ref)
    later_ref[...] = head_rows(rows, wanted, down_ref, weight_refs)


def half_columns(values, tok_rows, bits, parity):
    tokens = values.shape[1]
    half = tokens // 2
    place = lax.broadcasted_iota(jnp.int32, (half, tokens), 0) + parity * half
    token = lax.broadcasted_iota(jnp.int32, (half, tokens), 1)
    here = token_at(place, tok_rows, bits) == token
    column = jnp.sum(jnp.where(here, values.astype(jnp.float32), 0.0), axis=1, keepdims=True)
    return column.astype(jnp.int32)


def head_kernel(place, *refs):
    (later_ref, partial_ref, weight_ref, arrived_ref, gain_ref, columns_ref, down_ref) = refs[0:7]
    weight_refs, (stats_ref,) = refs[7:11], refs[11:]
    late = bit(lax.axis_index("tensor"), place) == 1
    mixed = partial_ref[...] + weight_ref[:, 0:1] * arrived_ref[...].astype(jnp.float32)
    rows = rms_norm(mixed, gain_ref[...]).astype(jnp.bfloat16)
    piece = rows.shape[0]
    wanted = columns_ref[0][:, 0:1]
    wanted = jnp.where(late, wanted[piece:], wanted[:piece])
    packed = head_rows(rows, wanted, down_ref, weight_refs)
    stats_ref[...] = in_order(late, packed, later_ref[...]).T[:8]


def merge_kernel(one_ref, two_ref, out_ref):
    one, two = one_ref[...], two_ref[...]
    ceiling = jnp.maximum(one[0:2], two[0:2])
    exp_total = one[2:4] * jnp.exp(one[0:2] - ceiling) + two[2:4] * jnp.exp(two[0:2] - ceiling)
    out_ref[...] = jnp.concatenate([ceiling, exp_total, one[4:8] + two[4:8]], axis=0)


def result_kernel(tok_rows, own_ref, other_ref, columns_ref, policy_ref, ratio_ref, sums_ref):
    half = own_ref.shape[1]
    picked = []
    for ref, columns in ((own_ref, columns_ref[1]), (other_ref, columns_ref[2])):
        stats = ref[...]
        log_probs = stats[4:6] - stats[0:2] - jnp.log(stats[2:4])
        policy = log_probs[1:2]
        values = jnp.concatenate([policy, policy - log_probs[0:1]], axis=0)
        high = values.astype(jnp.bfloat16).astype(jnp.float32)
        middle = (values - high).astype(jnp.bfloat16).astype(jnp.float32)
        parts = [high, middle, values - high - middle, jnp.zeros_like(values)]
        rows = jnp.concatenate(parts, axis=0).astype(jnp.bfloat16)
        parts = jnp.dot(
            rows, columns.astype(jnp.bfloat16), preferred_element_type=jnp.float32
        )
        picked.append(parts[0:2] + parts[2:4] + parts[4:6])
    policy_ref[...] = picked[0][0:1, :tok_rows]
    ratio_ref[...] = picked[0][1:2, :tok_rows]
    sums_ref[...] = (picked[0] + picked[1])[1:2, 64 : 64 + SEQS]


def call(kernel, shapes, *operands, flops=0):
    size = sum(operand.size * operand.dtype.itemsize for operand in operands)
    return pl.pallas_call(
        kernel,
        out_shape=shapes,
        compiler_params=pltpu.CompilerParams(vmem_limit_bytes=32 << 20),
        cost_estimate=pl.CostEstimate(flops=flops, bytes_accessed=size, transcendentals=0),
    )(*operands)


def dense_on_device(
    hidden_in,
    expert_ids,
    gate_weights,
    targets,
    seq_ids,
    moe_gain,
    w_gate,
    w_up,
    w_down,
    final_gain,
    head_weight,
    adapter_down,
    adapter_up,
):
    tok_rows, features = hidden_in.shape
    devices = lax.axis_size("tensor")
    bits = devices.bit_length() - 1
    half = devices * tok_rows // 2
    my_index = lax.axis_index("tensor")
    (near_bit, near_mask), (far_bit, far_mask) = ((b, (1 << b) + 1) for b in range(1, bits))

    def array(dtype, *shape):
        return jax.ShapeDtypeStruct(shape, dtype)

    flags = call(flags_kernel, array(jnp.int32, 8, 128), flops=ROUND_FLOPS)
    flags, sent_d = lax.optimization_barrier((flags, w_down))
    mixing, held_rows, gain, last_gain, held_targets, held_seq = call(
        functools.partial(early_kernel, tok_rows, bits),
        [
            array(jnp.float32, 2 * tok_rows, 128),
            array(jnp.bfloat16, tok_rows, features),
            array(jnp.float32, 1, features),
            array(jnp.float32, 1, features),
            array(jnp.int32, 1, 2 * half),
            array(jnp.int32, 1, 2 * half),
        ],
        expert_ids.T,
        gate_weights.T,
        hidden_in,
        moe_gain[None],
        final_gain[None],
        targets[None],
        seq_ids[None],
    )
    first = call(
        functools.partial(order_kernel, near_bit),
        array(jnp.bfloat16, 2 * tok_rows, features),
        flags,
        held_rows,
        exchange(hidden_in, near_mask),
        flops=ROUND_FLOPS,
    )
    second = exchange(first, far_mask)
    units = [w_gate.T, w_up.T, w_down]
    units = [exchange(unit, 1) for unit in (units[0], units[1], sent_d)] + units
    totals, sent = [], []
    for rows, more in ((first, [mixing]), (second, [])):
        outputs = call(
            expert_kernel,
            [
                array(dtype, 2 * tok_rows, features + 128 * len(more))
                for dtype in (jnp.float32, jnp.bfloat16)
            ],
            rows,
            gain,
            *units,
            *more,
            flops=3 * devices * tok_rows * features * w_gate.shape[1],
        )
        total, piece = call(
            add_kernel,
            [array(output.dtype, *output.shape) for output in outputs],
            outputs[0],
            exchange(outputs[1], near_mask),
            flops=ROUND_FLOPS // 16 * len(totals),
        )
        totals.append(total)
        sent.append(piece)
    sent[0], late_seq = lax.optimization_barrier((sent[0], held_seq))
    sent[1], late_targets = lax.optimization_barrier((sent[1], held_targets))
    arrived = [exchange(piece, far_mask) for piece in sent]

    vocabulary = [adapter_down.T, head_weight, exchange(head_weight, 1)]
    vocabulary += [adapter_up, exchange(adapter_up, 1)]
    columns, *late = call(
        functools.partial(late_kernel, tok_rows, bits, far_bit),
        [
            array(jnp.float32, 3, half, 128),
            array(jnp.float32, 2 * tok_rows, 128),
            array(jnp.float32, 2 * tok_rows, features),
            array(jnp.float32, 2 * tok_rows, 128),
        ],
        late_targets,
        late_seq,
        first,
        second,
        *totals,
        arrived[0],
        last_gain,
        *vocabulary,
    )
    stats = call(
        functools.partial(head_kernel, far_bit),
        array(jnp.float32, 8, half),
        *late,
        arrived[1],
        last_gain,
        columns,
        *vocabulary,
        flops=2 * devices * tok_rows * features * head_weight.shape[1],
    )
    for mask in (far_mask, near_mask):
        stats = call(merge_kernel, array(jnp.float32, 8, half), stats, exchange(stats, mask))
    policy_own, ratio_own, seq_sums = call(
        lambda *refs: result_kernel(tok_rows, *refs),
        [array(jnp.float32, 1, tok_rows)] * 2 + [array(jnp.float32, 1, SEQS)],
        stats,
        exchange(stats, 1),
        columns,
    )
    return (policy_own[0], ratio_own[0], seq_sums[0])


def solution(mesh):
    in_specs = (
        P(("dp", "tensor"), None),
        P(("dp", "tensor"), None),
        P(("dp", "tensor"), None),
        P("dp"),
        P("dp"),
        P(),
        P(None, "tensor"),
        P(None, "tensor"),
        P("tensor", None),
        P(),
        P(None, "tensor"),
        P(),
        P(None, "tensor"),
    )
    out_specs = (P(("dp", "tensor")), P(("dp", "tensor")), P("dp"))
    devices = mesh.shape["tensor"]

    def on_device(hidden_in, expert_ids, *others):
        both_experts = expert_ids.shape[1] == 2 and devices == 2 * SPLIT
        step = dense_on_device if both_experts else routed_on_device
        return step(hidden_in, expert_ids, *others)

    return jax.shard_map(
        on_device, mesh=mesh, in_specs=in_specs, out_specs=out_specs, check_vma=False
    )
```

```python
import functools

import jax
import jax.numpy as jnp
from jax import lax
from jax.experimental import pallas as pl
from jax.experimental.pallas import tpu as pltpu
from jax.sharding import PartitionSpec as P

SPLIT = 4
SEQS = 16
ROUND_FLOPS = 32 << 30


epsilon = 1e-06


def rms_norm(values, norm_gain):
    mean_sq = jnp.mean(values * values, axis=-1, keepdims=True)
    return values * lax.rsqrt(mean_sq + epsilon) * norm_gain


def expert_piece(arrived, w_gate, w_up, w_down):
    features = arrived.shape[-1]
    flat_rows = arrived.reshape(-1, features)
    gate_proj = jnp.dot(flat_rows, w_gate, preferred_element_type=jnp.float32)
    up_proj = jnp.dot(flat_rows, w_up, preferred_element_type=jnp.float32)
    inner_act = (jax.nn.silu(gate_proj) * up_proj).astype(jnp.bfloat16)
    partial_value = jnp.dot(inner_act, w_down, preferred_element_type=jnp.float32)
    return lax.all_to_all(
        partial_value.reshape(arrived.shape), "tensor", split_axis=0, concat_axis=0, tiled=True
    )


def routed_on_device(
    hidden_in,
    expert_ids,
    gate_weights,
    targets,
    seq_ids,
    moe_gain,
    w_gate,
    w_up,
    w_down,
    final_gain,
    head_weight,
    adapter_down,
    adapter_up,
):
    tok_rows, features = hidden_in.shape
    top_count = expert_ids.shape[1]
    devices = lax.axis_size("tensor")
    experts = devices // SPLIT
    capacity = min(tok_rows, 2 * tok_rows * top_count // experts)
    my_index = lax.axis_index("tensor")
    moe_input = rms_norm(hidden_in.astype(jnp.float32), moe_gain).astype(jnp.bfloat16)
    flat_ids = expert_ids.reshape(-1)
    chosen_hot = (flat_ids[:, None] == jnp.arange(experts, dtype=jnp.int32)[None, :]).astype(
        jnp.int32
    )
    slot_pos = jnp.sum((jnp.cumsum(chosen_hot, axis=0) - chosen_hot) * chosen_hot, axis=1)
    target_slot = flat_ids * capacity + slot_pos
    placed = (
        target_slot[:, None] == jnp.arange(experts * capacity, dtype=jnp.int32)[None, :]
    ).reshape(tok_rows, top_count, experts * capacity)
    spread = jnp.any(placed, axis=1).astype(jnp.bfloat16)
    packed = lax.dot_general(
        spread, moe_input, (((0,), (0,)), ((), ())), preferred_element_type=jnp.float32
    ).astype(jnp.bfloat16)
    outgoing = jnp.broadcast_to(
        packed.reshape(experts, 1, capacity, features), (experts, SPLIT, capacity, features)
    ).reshape(devices, capacity, features)
    returned = expert_piece(
        lax.all_to_all(outgoing, "tensor", split_axis=0, concat_axis=0, tiled=True),
        w_gate,
        w_up,
        w_down,
    )
    summed = jnp.sum(returned.reshape(experts, SPLIT, capacity, features), axis=1).reshape(
        experts * capacity, features
    )
    mixing = jnp.sum(placed.astype(jnp.float32) * gate_weights[:, :, None], axis=1)
    residual_sum = hidden_in.astype(jnp.float32) + jnp.dot(
        mixing, summed, precision=lax.Precision.HIGHEST
    )
    final_input = rms_norm(residual_sum, final_gain).astype(jnp.bfloat16)
    vocab_dev = head_weight.shape[1]
    vocab_start = my_index * vocab_dev
    columns = jnp.arange(vocab_dev, dtype=jnp.int32)

    def summary(block_rows, block_latent, row_start):
        row_count = block_rows.shape[0]
        base_logits = jnp.dot(block_rows, head_weight, preferred_element_type=jnp.float32)
        policy_logits = base_logits + jnp.dot(
            block_latent, adapter_up, preferred_element_type=jnp.float32
        )
        wanted = lax.dynamic_slice_in_dim(targets, row_start, row_count) - vocab_start
        is_target = wanted[:, None] == columns[None, :]

        def reduce_logits(logits):
            top_value = jnp.max(logits, axis=1)
            exp_total = jnp.sum(jnp.exp(logits - top_value[:, None]), axis=1)
            picked = jnp.sum(jnp.where(is_target, logits, 0.0), axis=1)
            return (top_value, exp_total, picked)

        base_stats = reduce_logits(base_logits)
        policy_stats = reduce_logits(policy_logits)
        return tuple(
            (
                jnp.stack([earlier, later], axis=1)
                for earlier, later in zip(base_stats, policy_stats)
            )
        )

    def blocked(shard_rows, shard_latent, row_start):
        row_count = shard_rows.shape[0]
        block_size = 512 if row_count % 512 == 0 else row_count
        if block_size == row_count:
            return summary(shard_rows, shard_latent, row_start)

        def one_block(block_index):
            offset = block_index * block_size
            return summary(
                lax.dynamic_slice_in_dim(shard_rows, offset, block_size),
                lax.dynamic_slice_in_dim(shard_latent, offset, block_size),
                row_start + offset,
            )

        results = lax.map(one_block, jnp.arange(row_count // block_size, dtype=jnp.int32))
        return tuple((member.reshape(row_count, 2) for member in results))

    shard_rows = lax.all_gather(final_input, "tensor", axis=0, tiled=True)
    shard_latent = jnp.dot(shard_rows, adapter_down, preferred_element_type=jnp.float32).astype(
        jnp.bfloat16
    )
    block_stats = blocked(shard_rows, shard_latent, jnp.int32(0))
    maxima, exp_sums, target_logits = tuple((update for update in block_stats))
    ceiling = lax.pmax(maxima, "tensor")
    totals, picked_all = lax.psum((exp_sums * jnp.exp(maxima - ceiling), target_logits), "tensor")
    log_probs = picked_all - ceiling - jnp.log(totals)
    log_ratio = log_probs[:, 1] - log_probs[:, 0]
    seq_match = (seq_ids[None, :] == jnp.arange(SEQS, dtype=jnp.int32)[:, None]).astype(jnp.float32)
    seq_sums = jnp.dot(seq_match, log_ratio, precision=lax.Precision.HIGHEST)
    own_start = my_index * tok_rows
    policy_own = lax.dynamic_slice_in_dim(log_probs[:, 1], own_start, tok_rows)
    ratio_own = lax.dynamic_slice_in_dim(log_ratio, own_start, tok_rows)
    return (policy_own, ratio_own, seq_sums)


def exchange(values, mask):
    devices = lax.axis_size("tensor")
    return lax.ppermute(values, "tensor", [(i, i ^ mask) for i in range(devices)])


def bit(number, place):
    return (number >> place) & 1


def in_order(late, mine, other):
    return jnp.concatenate([jnp.where(late, other, mine), jnp.where(late, mine, other)], axis=0)


def token_at(place, tok_rows, bits):
    devices = 1 << bits
    rank = place // tok_rows
    parity = rank >> (bits - 1)
    device = parity * 0
    low = parity
    for b in range(1, bits):
        one = (rank >> (b - 1)) & 1
        device = device + one * (1 << b)
        low = low ^ one
    return (device + low) * tok_rows + place % tok_rows


TRANSPOSED = (((1,), (1,)), ((), ()))


def places(tok_rows, bits):
    my_index = lax.axis_index("tensor")
    parity = sum(bit(my_index, b) for b in range(bits)) & 1
    return my_index, parity, tok_rows << (bits - 1)


def early_kernel(tok_rows, bits, *refs):
    (ids_ref, gates_ref), (mixing_ref,) = refs[0:2], refs[5:6]
    for in_ref, out_ref in zip(refs[2:5], refs[6:9]):
        out_ref[...] = in_ref[...]
    my_index, parity, half = places(tok_rows, bits)
    experts = gates_ref.shape[0]
    rows = [
        sum(
            jnp.where(ids_ref[k : k + 1] == expert, gates_ref[k : k + 1], 0.0)
            for k in range(ids_ref.shape[0])
        )
        for expert in range(experts)
    ]
    weights = jnp.concatenate(rows, axis=0)
    high = weights.astype(jnp.bfloat16).astype(jnp.float32)
    middle = (weights - high).astype(jnp.bfloat16).astype(jnp.float32)
    low = weights - high - middle
    rows = [high, middle, low, jnp.zeros((8 - 3 * experts, tok_rows), jnp.float32)]
    rows = [jnp.concatenate(rows, axis=0), jnp.zeros((8, 128 - tok_rows), jnp.float32)]
    parts = jnp.concatenate(rows, axis=1).T[:tok_rows]
    parts = jnp.concatenate([parts] * 16, axis=1)
    lane = lax.broadcasted_iota(jnp.int32, parts.shape, 1)
    token = token_at(lane // 8 * tok_rows + parity * half, tok_rows, bits)
    mine = (lane < half // tok_rows * 8) & (token // tok_rows == my_index)
    mixing = jnp.where(mine, parts, 0.0)
    mixing_ref[...] = jnp.concatenate([mixing, jnp.zeros_like(mixing)], axis=0)


def columns_kernel(tok_rows, bits, targets_ref, seq_ref, columns_ref):
    my_index, parity, half = places(tok_rows, bits)
    row = lax.broadcasted_iota(jnp.int32, (half, 128), 0)
    lane = lax.broadcasted_iota(jnp.int32, (half, 128), 1)
    token = token_at(row + parity * half, tok_rows, bits) - my_index * tok_rows
    wanted = half_columns(targets_ref[...], tok_rows, bits, parity)
    own_seq = half_columns(seq_ref[...], tok_rows, bits, parity)
    other_seq = half_columns(seq_ref[...], tok_rows, bits, 1 - parity)
    picks = (token == lane) & (lane < tok_rows) | (own_seq == lane - 64) & (lane >= 64)
    columns_ref[0] = jnp.where(lane == 0, wanted, 0).astype(jnp.float32)
    columns_ref[1] = picks.astype(jnp.float32)
    columns_ref[2] = ((other_seq == lane - 64) & (lane >= 64)).astype(jnp.float32)


def flags_kernel(flags_ref):
    row = lax.broadcasted_iota(jnp.int32, flags_ref.shape, 0)
    flags_ref[...] = bit(lax.axis_index("tensor"), row)


def order_kernel(place, flags_ref, mine_ref, other_ref, out_ref):
    late = flags_ref[place : place + 1, 0:1] == 1
    rows = in_order(late, *(ref[...].astype(jnp.float32) for ref in (mine_ref, other_ref)))
    out_ref[...] = rows.astype(out_ref.dtype)


def expert_kernel(rows_ref, gain_ref, *refs):
    far_refs, near_refs, mixing_refs, (total_ref, sent_ref) = (
        refs[0:3],
        refs[3:6],
        refs[6:-2],
        refs[-2:],
    )
    hidden = rows_ref[...].astype(jnp.float32)
    scale = lax.rsqrt(jnp.mean(hidden * hidden, axis=-1, keepdims=True) + epsilon)
    moe_input = (hidden * gain_ref[...]).astype(jnp.bfloat16)

    def units(gate_ref, up_ref, down_ref):
        projections = [
            scale
            * lax.dot_general(moe_input, ref[...], TRANSPOSED, preferred_element_type=jnp.float32)
            for ref in (gate_ref, up_ref)
        ]
        inner_act = (jax.nn.silu(projections[0]) * projections[1]).astype(jnp.bfloat16)
        return jnp.dot(inner_act, down_ref[...], preferred_element_type=jnp.float32)

    total = units(*near_refs) + units(*far_refs)
    total = jnp.concatenate([total, *(ref[...] for ref in mixing_refs)], axis=1)
    total_ref[...] = total
    sent_ref[...] = total.astype(jnp.bfloat16)


def add_kernel(total_ref, arrived_ref, sum_ref, sent_ref):
    total = total_ref[...] + arrived_ref[...].astype(jnp.float32)
    sum_ref[...] = total
    sent_ref[...] = total.astype(jnp.bfloat16)


def late_kernel(
    tok_rows,
    bits,
    place,
    targets_ref,
    seq_ref,
    first_ref,
    second_ref,
    first_total_ref,
    second_total_ref,
    arrived_ref,
    gain_ref,
    columns_ref,
    final_ref,
    partial_ref,
    weight_ref,
):
    columns_kernel(tok_rows, bits, targets_ref, seq_ref, columns_ref)
    features = first_ref.shape[1]
    my_index = lax.axis_index("tensor")
    expert = my_index // SPLIT
    mixing = first_total_ref[:tok_rows, features:]
    mixing = mixing + arrived_ref[:, features:].astype(jnp.float32)[:tok_rows]
    lane = lax.broadcasted_iota(jnp.int32, mixing.shape, 1)

    def weights(side, which):
        blocks = [
            jnp.sum(
                jnp.where((lane // 8 == 2 * side + k) & (lane % 2 == which), mixing, 0.0),
                axis=1,
                keepdims=True,
            )
            for k in range(2)
        ]
        return jnp.concatenate(blocks, axis=0)

    side = bit(my_index, place)
    partial_value = weights(side, expert) * first_total_ref[:, :features]
    partial_ref[...] = first_ref[...].astype(jnp.float32) + partial_value
    weight_ref[...] = jnp.broadcast_to(weights(side, 1 - expert), weight_ref.shape)
    mixed = second_ref[...].astype(jnp.float32)
    mixed = mixed + weights(1 - side, expert) * second_total_ref[...]
    arrived = arrived_ref[:, :features].astype(jnp.float32)
    mixed = mixed + weights(1 - side, 1 - expert) * arrived
    final_ref[...] = rms_norm(mixed, gain_ref[...]).astype(jnp.bfloat16)


def half_columns(values, tok_rows, bits, parity):
    tokens = values.shape[1]
    half = tokens // 2
    place = lax.broadcasted_iota(jnp.int32, (half, tokens), 0) + parity * half
    token = lax.broadcasted_iota(jnp.int32, (half, tokens), 1)
    here = token_at(place, tok_rows, bits) == token
    column = jnp.sum(jnp.where(here, values.astype(jnp.float32), 0.0), axis=1, keepdims=True)
    return column.astype(jnp.int32)


def head_kernel(place, *refs):
    (final_ref, partial_ref, weight_ref, arrived_ref, gain_ref, columns_ref, down_ref) = refs[0:7]
    weight_refs, (stats_ref,) = refs[7:11], refs[11:]
    my_index = lax.axis_index("tensor")
    mixed = partial_ref[...] + weight_ref[:, 0:1] * arrived_ref[...].astype(jnp.float32)
    first = rms_norm(mixed, gain_ref[...]).astype(jnp.bfloat16)
    rows = in_order(bit(my_index, place) == 1, first, final_ref[...])
    tokens = rows.shape[0]
    wanted = columns_ref[0][:, 0:1].astype(jnp.int32)
    latent = lax.dot_general(rows, down_ref[...], TRANSPOSED, preferred_element_type=jnp.float32)
    latent = latent.astype(jnp.bfloat16)
    lane = lax.broadcasted_iota(jnp.int32, (tokens, 128), 1)
    packed = jnp.zeros((tokens, 128), jnp.float32)
    base, policy, matches = [], [], []
    for index, head_ref, up_ref in zip((my_index, my_index ^ 1), weight_refs[:2], weight_refs[2:]):
        logits = jnp.dot(rows, head_ref[...], preferred_element_type=jnp.float32)
        base.append(logits)
        change = jnp.dot(latent, up_ref[...], preferred_element_type=jnp.float32)
        policy.append(logits + change)
        column = lax.broadcasted_iota(jnp.int32, logits.shape, 1)
        matches.append(column == wanted - index * logits.shape[1])
    is_target = jnp.concatenate(matches, axis=1)
    for at, parts in enumerate((base, policy)):
        logits = jnp.concatenate(parts, axis=1)
        top_value = jnp.max(logits, axis=1, keepdims=True)
        exp_total = jnp.sum(jnp.exp(logits - top_value), axis=1, keepdims=True)
        picked = jnp.sum(jnp.where(is_target, logits, 0.0), axis=1, keepdims=True)
        for kind, value in enumerate((top_value, exp_total, picked)):
            packed = jnp.where(lane == 2 * kind + at, value, packed)
    stats_ref[...] = packed.T[:8]


def merge_kernel(one_ref, two_ref, out_ref):
    one, two = one_ref[...], two_ref[...]
    ceiling = jnp.maximum(one[0:2], two[0:2])
    exp_total = one[2:4] * jnp.exp(one[0:2] - ceiling) + two[2:4] * jnp.exp(two[0:2] - ceiling)
    out_ref[...] = jnp.concatenate([ceiling, exp_total, one[4:8] + two[4:8]], axis=0)


def result_kernel(tok_rows, own_ref, other_ref, columns_ref, policy_ref, ratio_ref, sums_ref):
    half = own_ref.shape[1]
    picked = []
    for ref, columns in ((own_ref, columns_ref[1]), (other_ref, columns_ref[2])):
        stats = ref[...]
        log_probs = stats[4:6] - stats[0:2] - jnp.log(stats[2:4])
        policy = log_probs[1:2]
        values = jnp.concatenate([policy, policy - log_probs[0:1]], axis=0)
        high = values.astype(jnp.bfloat16).astype(jnp.float32)
        middle = (values - high).astype(jnp.bfloat16).astype(jnp.float32)
        parts = [high, middle, values - high - middle, jnp.zeros_like(values)]
        rows = jnp.concatenate(parts, axis=0).astype(jnp.bfloat16)
        parts = jnp.dot(
            rows, columns.astype(jnp.bfloat16), preferred_element_type=jnp.float32
        )
        picked.append(parts[0:2] + parts[2:4] + parts[4:6])
    policy_ref[...] = picked[0][0:1, :tok_rows]
    ratio_ref[...] = picked[0][1:2, :tok_rows]
    sums_ref[...] = (picked[0] + picked[1])[1:2, 64 : 64 + SEQS]


def call(kernel, shapes, *operands, flops=0):
    size = sum(operand.size * operand.dtype.itemsize for operand in operands)
    return pl.pallas_call(
        kernel,
        out_shape=shapes,
        compiler_params=pltpu.CompilerParams(vmem_limit_bytes=32 << 20),
        cost_estimate=pl.CostEstimate(flops=flops, bytes_accessed=size, transcendentals=0),
    )(*operands)


def dense_on_device(
    hidden_in,
    expert_ids,
    gate_weights,
    targets,
    seq_ids,
    moe_gain,
    w_gate,
    w_up,
    w_down,
    final_gain,
    head_weight,
    adapter_down,
    adapter_up,
):
    tok_rows, features = hidden_in.shape
    devices = lax.axis_size("tensor")
    bits = devices.bit_length() - 1
    half = devices * tok_rows // 2
    my_index = lax.axis_index("tensor")
    (near_bit, near_mask), (far_bit, far_mask) = ((b, (1 << b) + 1) for b in range(1, bits))

    def array(dtype, *shape):
        return jax.ShapeDtypeStruct(shape, dtype)

    flags = call(flags_kernel, array(jnp.int32, 8, 128), flops=ROUND_FLOPS)
    flags, sent_d = lax.optimization_barrier((flags, w_down))
    mixing, held_rows, gain, last_gain = call(
        functools.partial(early_kernel, tok_rows, bits),
        [
            array(jnp.float32, 2 * tok_rows, 128),
            array(jnp.bfloat16, tok_rows, features),
            array(jnp.float32, 1, features),
            array(jnp.float32, 1, features),
        ],
        expert_ids.T,
        gate_weights.T,
        hidden_in,
        moe_gain[None],
        final_gain[None],
    )
    first = call(
        functools.partial(order_kernel, near_bit),
        array(jnp.bfloat16, 2 * tok_rows, features),
        flags,
        held_rows,
        exchange(hidden_in, near_mask),
        flops=ROUND_FLOPS,
    )
    second = exchange(first, far_mask)
    units = [w_gate.T, w_up.T, w_down]
    units = [exchange(unit, 1) for unit in (units[0], units[1], sent_d)] + units
    totals, sent = [], []
    for rows, more in ((first, [mixing]), (second, [])):
        outputs = call(
            expert_kernel,
            [
                array(dtype, 2 * tok_rows, features + 128 * len(more))
                for dtype in (jnp.float32, jnp.bfloat16)
            ],
            rows,
            gain,
            *units,
            *more,
            flops=3 * devices * tok_rows * features * w_gate.shape[1],
        )
        total, piece = call(
            add_kernel,
            [array(output.dtype, *output.shape) for output in outputs],
            outputs[0],
            exchange(outputs[1], near_mask),
            flops=ROUND_FLOPS // 16 * len(totals),
        )
        totals.append(total)
        sent.append(piece)
    sent[0], late_seq = lax.optimization_barrier((sent[0], seq_ids[None]))
    sent[1], late_targets = lax.optimization_barrier((sent[1], targets[None]))
    arrived = [exchange(piece, far_mask) for piece in sent]

    columns, *late = call(
        functools.partial(late_kernel, tok_rows, bits, far_bit),
        [
            array(jnp.float32, 3, half, 128),
            array(jnp.bfloat16, 2 * tok_rows, features),
            array(jnp.float32, 2 * tok_rows, features),
            array(jnp.float32, 2 * tok_rows, 128),
        ],
        late_targets,
        late_seq,
        first,
        second,
        *totals,
        arrived[0],
        last_gain,
    )
    stats = call(
        functools.partial(head_kernel, far_bit),
        array(jnp.float32, 8, half),
        *late,
        arrived[1],
        last_gain,
        columns,
        adapter_down.T,
        head_weight,
        exchange(head_weight, 1),
        adapter_up,
        exchange(adapter_up, 1),
        flops=2 * devices * tok_rows * features * head_weight.shape[1],
    )
    for mask in (far_mask, near_mask):
        stats = call(merge_kernel, array(jnp.float32, 8, half), stats, exchange(stats, mask))
    policy_own, ratio_own, seq_sums = call(
        lambda *refs: result_kernel(tok_rows, *refs),
        [array(jnp.float32, 1, tok_rows)] * 2 + [array(jnp.float32, 1, SEQS)],
        stats,
        exchange(stats, 1),
        columns,
    )
    return (policy_own[0], ratio_own[0], seq_sums[0])


def solution(mesh):
    in_specs = (
        P(("dp", "tensor"), None),
        P(("dp", "tensor"), None),
        P(("dp", "tensor"), None),
        P("dp"),
        P("dp"),
        P(),
        P(None, "tensor"),
        P(None, "tensor"),
        P("tensor", None),
        P(),
        P(None, "tensor"),
        P(),
        P(None, "tensor"),
    )
    out_specs = (P(("dp", "tensor")), P(("dp", "tensor")), P("dp"))
    devices = mesh.shape["tensor"]

    def on_device(hidden_in, expert_ids, *others):
        both_experts = expert_ids.shape[1] == 2 and devices == 2 * SPLIT
        step = dense_on_device if both_experts else routed_on_device
        return step(hidden_in, expert_ids, *others)

    return jax.shard_map(
        on_device, mesh=mesh, in_specs=in_specs, out_specs=out_specs, check_vma=False
    )
```

```python
import functools

import jax
import jax.numpy as jnp
from jax import lax
from jax.experimental import pallas as pl
from jax.experimental.pallas import tpu as pltpu
from jax.sharding import PartitionSpec as P

SPLIT = 4
SEQS = 16
ROUND_FLOPS = 32 << 30


epsilon = 1e-06


def rms_norm(values, norm_gain):
    mean_sq = jnp.mean(values * values, axis=-1, keepdims=True)
    return values * lax.rsqrt(mean_sq + epsilon) * norm_gain


def expert_piece(arrived, w_gate, w_up, w_down):
    features = arrived.shape[-1]
    flat_rows = arrived.reshape(-1, features)
    gate_proj = jnp.dot(flat_rows, w_gate, preferred_element_type=jnp.float32)
    up_proj = jnp.dot(flat_rows, w_up, preferred_element_type=jnp.float32)
    inner_act = (jax.nn.silu(gate_proj) * up_proj).astype(jnp.bfloat16)
    partial_value = jnp.dot(inner_act, w_down, preferred_element_type=jnp.float32)
    return lax.all_to_all(
        partial_value.reshape(arrived.shape), "tensor", split_axis=0, concat_axis=0, tiled=True
    )


def routed_on_device(
    hidden_in,
    expert_ids,
    gate_weights,
    targets,
    seq_ids,
    moe_gain,
    w_gate,
    w_up,
    w_down,
    final_gain,
    head_weight,
    adapter_down,
    adapter_up,
):
    tok_rows, features = hidden_in.shape
    top_count = expert_ids.shape[1]
    devices = lax.axis_size("tensor")
    experts = devices // SPLIT
    capacity = min(tok_rows, 2 * tok_rows * top_count // experts)
    my_index = lax.axis_index("tensor")
    moe_input = rms_norm(hidden_in.astype(jnp.float32), moe_gain).astype(jnp.bfloat16)
    flat_ids = expert_ids.reshape(-1)
    chosen_hot = (flat_ids[:, None] == jnp.arange(experts, dtype=jnp.int32)[None, :]).astype(
        jnp.int32
    )
    slot_pos = jnp.sum((jnp.cumsum(chosen_hot, axis=0) - chosen_hot) * chosen_hot, axis=1)
    target_slot = flat_ids * capacity + slot_pos
    placed = (
        target_slot[:, None] == jnp.arange(experts * capacity, dtype=jnp.int32)[None, :]
    ).reshape(tok_rows, top_count, experts * capacity)
    spread = jnp.any(placed, axis=1).astype(jnp.bfloat16)
    packed = lax.dot_general(
        spread, moe_input, (((0,), (0,)), ((), ())), preferred_element_type=jnp.float32
    ).astype(jnp.bfloat16)
    outgoing = jnp.broadcast_to(
        packed.reshape(experts, 1, capacity, features), (experts, SPLIT, capacity, features)
    ).reshape(devices, capacity, features)
    returned = expert_piece(
        lax.all_to_all(outgoing, "tensor", split_axis=0, concat_axis=0, tiled=True),
        w_gate,
        w_up,
        w_down,
    )
    summed = jnp.sum(returned.reshape(experts, SPLIT, capacity, features), axis=1).reshape(
        experts * capacity, features
    )
    mixing = jnp.sum(placed.astype(jnp.float32) * gate_weights[:, :, None], axis=1)
    residual_sum = hidden_in.astype(jnp.float32) + jnp.dot(
        mixing, summed, precision=lax.Precision.HIGHEST
    )
    final_input = rms_norm(residual_sum, final_gain).astype(jnp.bfloat16)
    vocab_dev = head_weight.shape[1]
    vocab_start = my_index * vocab_dev
    columns = jnp.arange(vocab_dev, dtype=jnp.int32)

    def summary(block_rows, block_latent, row_start):
        row_count = block_rows.shape[0]
        base_logits = jnp.dot(block_rows, head_weight, preferred_element_type=jnp.float32)
        policy_logits = base_logits + jnp.dot(
            block_latent, adapter_up, preferred_element_type=jnp.float32
        )
        wanted = lax.dynamic_slice_in_dim(targets, row_start, row_count) - vocab_start
        is_target = wanted[:, None] == columns[None, :]

        def reduce_logits(logits):
            top_value = jnp.max(logits, axis=1)
            exp_total = jnp.sum(jnp.exp(logits - top_value[:, None]), axis=1)
            picked = jnp.sum(jnp.where(is_target, logits, 0.0), axis=1)
            return (top_value, exp_total, picked)

        base_stats = reduce_logits(base_logits)
        policy_stats = reduce_logits(policy_logits)
        return tuple(
            (
                jnp.stack([earlier, later], axis=1)
                for earlier, later in zip(base_stats, policy_stats)
            )
        )

    def blocked(shard_rows, shard_latent, row_start):
        row_count = shard_rows.shape[0]
        block_size = 512 if row_count % 512 == 0 else row_count
        if block_size == row_count:
            return summary(shard_rows, shard_latent, row_start)

        def one_block(block_index):
            offset = block_index * block_size
            return summary(
                lax.dynamic_slice_in_dim(shard_rows, offset, block_size),
                lax.dynamic_slice_in_dim(shard_latent, offset, block_size),
                row_start + offset,
            )

        results = lax.map(one_block, jnp.arange(row_count // block_size, dtype=jnp.int32))
        return tuple((member.reshape(row_count, 2) for member in results))

    shard_rows = lax.all_gather(final_input, "tensor", axis=0, tiled=True)
    shard_latent = jnp.dot(shard_rows, adapter_down, preferred_element_type=jnp.float32).astype(
        jnp.bfloat16
    )
    block_stats = blocked(shard_rows, shard_latent, jnp.int32(0))
    maxima, exp_sums, target_logits = tuple((update for update in block_stats))
    ceiling = lax.pmax(maxima, "tensor")
    totals, picked_all = lax.psum((exp_sums * jnp.exp(maxima - ceiling), target_logits), "tensor")
    log_probs = picked_all - ceiling - jnp.log(totals)
    log_ratio = log_probs[:, 1] - log_probs[:, 0]
    seq_match = (seq_ids[None, :] == jnp.arange(SEQS, dtype=jnp.int32)[:, None]).astype(jnp.float32)
    seq_sums = jnp.dot(seq_match, log_ratio, precision=lax.Precision.HIGHEST)
    own_start = my_index * tok_rows
    policy_own = lax.dynamic_slice_in_dim(log_probs[:, 1], own_start, tok_rows)
    ratio_own = lax.dynamic_slice_in_dim(log_ratio, own_start, tok_rows)
    return (policy_own, ratio_own, seq_sums)


def exchange(values, mask):
    devices = lax.axis_size("tensor")
    return lax.ppermute(values, "tensor", [(i, i ^ mask) for i in range(devices)])


def bit(number, place):
    return (number >> place) & 1


def in_order(late, mine, other):
    return jnp.concatenate([jnp.where(late, other, mine), jnp.where(late, mine, other)], axis=0)


def token_at(place, tok_rows, bits):
    devices = 1 << bits
    rank = place // tok_rows
    parity = rank >> (bits - 1)
    device = parity * 0
    low = parity
    for b in range(1, bits):
        one = (rank >> (b - 1)) & 1
        device = device + one * (1 << b)
        low = low ^ one
    return (device + low) * tok_rows + place % tok_rows


TRANSPOSED = (((1,), (1,)), ((), ()))


def places(tok_rows, bits):
    my_index = lax.axis_index("tensor")
    parity = sum(bit(my_index, b) for b in range(bits)) & 1
    return my_index, parity, tok_rows << (bits - 1)


def early_kernel(tok_rows, bits, *refs):
    (ids_ref, gates_ref), (mixing_ref,) = refs[0:2], refs[5:6]
    for in_ref, out_ref in zip(refs[2:5], refs[6:9]):
        out_ref[...] = in_ref[...]
    my_index, parity, half = places(tok_rows, bits)
    experts = gates_ref.shape[0]
    rows = [
        sum(
            jnp.where(ids_ref[k : k + 1] == expert, gates_ref[k : k + 1], 0.0)
            for k in range(ids_ref.shape[0])
        )
        for expert in range(experts)
    ]
    weights = jnp.concatenate(rows, axis=0)
    high = weights.astype(jnp.bfloat16).astype(jnp.float32)
    middle = (weights - high).astype(jnp.bfloat16).astype(jnp.float32)
    low = weights - high - middle
    rows = [high, middle, low, jnp.zeros((8 - 3 * experts, tok_rows), jnp.float32)]
    rows = [jnp.concatenate(rows, axis=0), jnp.zeros((8, 128 - tok_rows), jnp.float32)]
    parts = jnp.concatenate(rows, axis=1).T[:tok_rows]
    parts = jnp.concatenate([parts] * 16, axis=1)
    lane = lax.broadcasted_iota(jnp.int32, parts.shape, 1)
    token = token_at(lane // 8 * tok_rows + parity * half, tok_rows, bits)
    mine = (lane < half // tok_rows * 8) & (token // tok_rows == my_index)
    mixing = jnp.where(mine, parts, 0.0)
    mixing_ref[...] = jnp.concatenate([mixing, jnp.zeros_like(mixing)], axis=0)


def columns_kernel(tok_rows, bits, targets_ref, seq_ref, columns_ref):
    my_index, parity, half = places(tok_rows, bits)
    row = lax.broadcasted_iota(jnp.int32, (half, 128), 0)
    lane = lax.broadcasted_iota(jnp.int32, (half, 128), 1)
    token = token_at(row + parity * half, tok_rows, bits) - my_index * tok_rows
    wanted = half_columns(targets_ref[...], tok_rows, bits, parity)
    own_seq = half_columns(seq_ref[...], tok_rows, bits, parity)
    other_seq = half_columns(seq_ref[...], tok_rows, bits, 1 - parity)
    picks = (token == lane) & (lane < tok_rows) | (own_seq == lane - 64) & (lane >= 64)
    columns_ref[0] = jnp.where(lane == 0, wanted, 0).astype(jnp.float32)
    columns_ref[1] = picks.astype(jnp.float32)
    columns_ref[2] = ((other_seq == lane - 64) & (lane >= 64)).astype(jnp.float32)


def flags_kernel(flags_ref):
    row = lax.broadcasted_iota(jnp.int32, flags_ref.shape, 0)
    flags_ref[...] = bit(lax.axis_index("tensor"), row)


def order_kernel(place, flags_ref, mine_ref, other_ref, out_ref):
    late = flags_ref[place : place + 1, 0:1] == 1
    rows = in_order(late, *(ref[...].astype(jnp.float32) for ref in (mine_ref, other_ref)))
    out_ref[...] = rows.astype(out_ref.dtype)


def expert_kernel(rows_ref, gain_ref, *refs):
    far_refs, near_refs, mixing_refs, (total_ref, sent_ref) = (
        refs[0:3],
        refs[3:6],
        refs[6:-2],
        refs[-2:],
    )
    hidden = rows_ref[...].astype(jnp.float32)
    scale = lax.rsqrt(jnp.mean(hidden * hidden, axis=-1, keepdims=True) + epsilon)
    moe_input = (hidden * gain_ref[...]).astype(jnp.bfloat16)

    def units(gate_ref, up_ref, down_ref):
        projections = [
            scale
            * lax.dot_general(moe_input, ref[...], TRANSPOSED, preferred_element_type=jnp.float32)
            for ref in (gate_ref, up_ref)
        ]
        inner_act = (jax.nn.silu(projections[0]) * projections[1]).astype(jnp.bfloat16)
        return jnp.dot(inner_act, down_ref[...], preferred_element_type=jnp.float32)

    total = units(*near_refs) + units(*far_refs)
    total = jnp.concatenate([total, *(ref[...] for ref in mixing_refs)], axis=1)
    total_ref[...] = total
    sent_ref[...] = total.astype(jnp.bfloat16)


def add_kernel(total_ref, arrived_ref, sum_ref, sent_ref):
    total = total_ref[...] + arrived_ref[...].astype(jnp.float32)
    sum_ref[...] = total
    sent_ref[...] = total.astype(jnp.bfloat16)


def head_rows(rows, wanted, down_ref, weight_refs):
    my_index = lax.axis_index("tensor")
    wanted = wanted.astype(jnp.int32)
    latent = lax.dot_general(rows, down_ref[...], TRANSPOSED, preferred_element_type=jnp.float32)
    latent = latent.astype(jnp.bfloat16)
    lane = lax.broadcasted_iota(jnp.int32, (rows.shape[0], 128), 1)
    packed = jnp.zeros(lane.shape, jnp.float32)
    base, policy, matches = [], [], []
    for index, head_ref, up_ref in zip((my_index, my_index ^ 1), weight_refs[:2], weight_refs[2:]):
        logits = jnp.dot(rows, head_ref[...], preferred_element_type=jnp.float32)
        base.append(logits)
        change = jnp.dot(latent, up_ref[...], preferred_element_type=jnp.float32)
        policy.append(logits + change)
        column = lax.broadcasted_iota(jnp.int32, logits.shape, 1)
        matches.append(column == wanted - index * logits.shape[1])
    is_target = jnp.concatenate(matches, axis=1)
    for at, parts in enumerate((base, policy)):
        logits = jnp.concatenate(parts, axis=1)
        top_value = jnp.max(logits, axis=1, keepdims=True)
        exp_total = jnp.sum(jnp.exp(logits - top_value), axis=1, keepdims=True)
        picked = jnp.sum(jnp.where(is_target, logits, 0.0), axis=1, keepdims=True)
        for kind, value in enumerate((top_value, exp_total, picked)):
            packed = jnp.where(lane == 2 * kind + at, value, packed)
    return packed


def late_kernel(
    tok_rows,
    bits,
    place,
    targets_ref,
    seq_ref,
    first_ref,
    second_ref,
    first_total_ref,
    second_total_ref,
    arrived_ref,
    gain_ref,
    down_ref,
    head_ref,
    far_head_ref,
    up_ref,
    far_up_ref,
    columns_ref,
    later_ref,
    partial_ref,
    weight_ref,
):
    columns_kernel(tok_rows, bits, targets_ref, seq_ref, columns_ref)
    features = first_ref.shape[1]
    my_index = lax.axis_index("tensor")
    expert = my_index // SPLIT
    mixing = first_total_ref[:tok_rows, features:]
    mixing = mixing + arrived_ref[:, features:].astype(jnp.float32)[:tok_rows]
    lane = lax.broadcasted_iota(jnp.int32, mixing.shape, 1)

    def weights(side, which):
        blocks = [
            jnp.sum(
                jnp.where((lane // 8 == 2 * side + k) & (lane % 2 == which), mixing, 0.0),
                axis=1,
                keepdims=True,
            )
            for k in range(2)
        ]
        return jnp.concatenate(blocks, axis=0)

    side = bit(my_index, place)
    partial_value = weights(side, expert) * first_total_ref[:, :features]
    partial_ref[...] = first_ref[...].astype(jnp.float32) + partial_value
    weight_ref[...] = jnp.broadcast_to(weights(side, 1 - expert), weight_ref.shape)
    mixed = second_ref[...].astype(jnp.float32)
    mixed = mixed + weights(1 - side, expert) * second_total_ref[...]
    arrived = arrived_ref[:, :features].astype(jnp.float32)
    mixed = mixed + weights(1 - side, 1 - expert) * arrived
    rows = rms_norm(mixed, gain_ref[...]).astype(jnp.bfloat16)
    piece = rows.shape[0]
    wanted = columns_ref[0][:, 0:1]
    wanted = jnp.where(side == 1, wanted[:piece], wanted[piece:])
    weight_refs = (head_ref, far_head_ref, up_ref, far_up_ref)
    later_ref[...] = head_rows(rows, wanted, down_ref, weight_refs)


def half_columns(values, tok_rows, bits, parity):
    tokens = values.shape[1]
    half = tokens // 2
    place = lax.broadcasted_iota(jnp.int32, (half, tokens), 0) + parity * half
    token = lax.broadcasted_iota(jnp.int32, (half, tokens), 1)
    here = token_at(place, tok_rows, bits) == token
    column = jnp.sum(jnp.where(here, values.astype(jnp.float32), 0.0), axis=1, keepdims=True)
    return column.astype(jnp.int32)


def head_kernel(place, *refs):
    (later_ref, partial_ref, weight_ref, arrived_ref, gain_ref, columns_ref, down_ref) = refs[0:7]
    weight_refs, (stats_ref,) = refs[7:11], refs[11:]
    late = bit(lax.axis_index("tensor"), place) == 1
    mixed = partial_ref[...] + weight_ref[:, 0:1] * arrived_ref[...].astype(jnp.float32)
    rows = rms_norm(mixed, gain_ref[...]).astype(jnp.bfloat16)
    piece = rows.shape[0]
    wanted = columns_ref[0][:, 0:1]
    wanted = jnp.where(late, wanted[piece:], wanted[:piece])
    packed = head_rows(rows, wanted, down_ref, weight_refs)
    stats_ref[...] = in_order(late, packed, later_ref[...]).T[:8]


def merge_kernel(one_ref, two_ref, out_ref):
    one, two = one_ref[...], two_ref[...]
    ceiling = jnp.maximum(one[0:2], two[0:2])
    exp_total = one[2:4] * jnp.exp(one[0:2] - ceiling) + two[2:4] * jnp.exp(two[0:2] - ceiling)
    out_ref[...] = jnp.concatenate([ceiling, exp_total, one[4:8] + two[4:8]], axis=0)


def result_kernel(tok_rows, own_ref, other_ref, columns_ref, policy_ref, ratio_ref, sums_ref):
    half = own_ref.shape[1]
    picked = []
    for ref, columns in ((own_ref, columns_ref[1]), (other_ref, columns_ref[2])):
        stats = ref[...]
        log_probs = stats[4:6] - stats[0:2] - jnp.log(stats[2:4])
        policy = log_probs[1:2]
        values = jnp.concatenate([policy, policy - log_probs[0:1]], axis=0)
        high = values.astype(jnp.bfloat16).astype(jnp.float32)
        middle = (values - high).astype(jnp.bfloat16).astype(jnp.float32)
        parts = [high, middle, values - high - middle, jnp.zeros_like(values)]
        rows = jnp.concatenate(parts, axis=0).astype(jnp.bfloat16)
        parts = jnp.dot(
            rows, columns.astype(jnp.bfloat16), preferred_element_type=jnp.float32
        )
        picked.append(parts[0:2] + parts[2:4] + parts[4:6])
    policy_ref[...] = picked[0][0:1, :tok_rows]
    ratio_ref[...] = picked[0][1:2, :tok_rows]
    sums_ref[...] = (picked[0] + picked[1])[1:2, 64 : 64 + SEQS]


def call(kernel, shapes, *operands, flops=0):
    size = sum(operand.size * operand.dtype.itemsize for operand in operands)
    return pl.pallas_call(
        kernel,
        out_shape=shapes,
        compiler_params=pltpu.CompilerParams(vmem_limit_bytes=32 << 20),
        cost_estimate=pl.CostEstimate(flops=flops, bytes_accessed=size, transcendentals=0),
    )(*operands)


def dense_on_device(
    hidden_in,
    expert_ids,
    gate_weights,
    targets,
    seq_ids,
    moe_gain,
    w_gate,
    w_up,
    w_down,
    final_gain,
    head_weight,
    adapter_down,
    adapter_up,
):
    tok_rows, features = hidden_in.shape
    devices = lax.axis_size("tensor")
    bits = devices.bit_length() - 1
    half = devices * tok_rows // 2
    my_index = lax.axis_index("tensor")
    (near_bit, near_mask), (far_bit, far_mask) = ((b, (1 << b) + 1) for b in range(1, bits))

    def array(dtype, *shape):
        return jax.ShapeDtypeStruct(shape, dtype)

    flags = call(flags_kernel, array(jnp.int32, 8, 128), flops=ROUND_FLOPS)
    flags, sent_d = lax.optimization_barrier((flags, w_down))
    mixing, held_rows, gain, last_gain = call(
        functools.partial(early_kernel, tok_rows, bits),
        [
            array(jnp.float32, 2 * tok_rows, 128),
            array(jnp.bfloat16, tok_rows, features),
            array(jnp.float32, 1, features),
            array(jnp.float32, 1, features),
        ],
        expert_ids.T,
        gate_weights.T,
        hidden_in,
        moe_gain[None],
        final_gain[None],
    )
    first = call(
        functools.partial(order_kernel, near_bit),
        array(jnp.bfloat16, 2 * tok_rows, features),
        flags,
        held_rows,
        exchange(hidden_in, near_mask),
        flops=ROUND_FLOPS,
    )
    second = exchange(first, far_mask)
    units = [w_gate.T, w_up.T, w_down]
    units = [exchange(unit, 1) for unit in (units[0], units[1], sent_d)] + units
    totals, sent = [], []
    for rows, more in ((first, [mixing]), (second, [])):
        outputs = call(
            expert_kernel,
            [
                array(dtype, 2 * tok_rows, features + 128 * len(more))
                for dtype in (jnp.float32, jnp.bfloat16)
            ],
            rows,
            gain,
            *units,
            *more,
            flops=3 * devices * tok_rows * features * w_gate.shape[1],
        )
        total, piece = call(
            add_kernel,
            [array(output.dtype, *output.shape) for output in outputs],
            outputs[0],
            exchange(outputs[1], near_mask),
            flops=ROUND_FLOPS // 16 * len(totals),
        )
        totals.append(total)
        sent.append(piece)
    sent[0], late_seq, late_targets = lax.optimization_barrier(
        (sent[0], seq_ids[None], targets[None])
    )
    arrived = [exchange(piece, far_mask) for piece in sent]

    vocabulary = [adapter_down.T, head_weight, exchange(head_weight, 1)]
    vocabulary += [adapter_up, exchange(adapter_up, 1)]
    columns, *late = call(
        functools.partial(late_kernel, tok_rows, bits, far_bit),
        [
            array(jnp.float32, 3, half, 128),
            array(jnp.float32, 2 * tok_rows, 128),
            array(jnp.float32, 2 * tok_rows, features),
            array(jnp.float32, 2 * tok_rows, 128),
        ],
        late_targets,
        late_seq,
        first,
        second,
        *totals,
        arrived[0],
        last_gain,
        *vocabulary,
    )
    stats = call(
        functools.partial(head_kernel, far_bit),
        array(jnp.float32, 8, half),
        *late,
        arrived[1],
        last_gain,
        columns,
        *vocabulary,
        flops=2 * devices * tok_rows * features * head_weight.shape[1],
    )
    for mask in (far_mask, near_mask):
        stats = call(merge_kernel, array(jnp.float32, 8, half), stats, exchange(stats, mask))
    policy_own, ratio_own, seq_sums = call(
        lambda *refs: result_kernel(tok_rows, *refs),
        [array(jnp.float32, 1, tok_rows)] * 2 + [array(jnp.float32, 1, SEQS)],
        stats,
        exchange(stats, 1),
        columns,
    )
    return (policy_own[0], ratio_own[0], seq_sums[0])


def solution(mesh):
    in_specs = (
        P(("dp", "tensor"), None),
        P(("dp", "tensor"), None),
        P(("dp", "tensor"), None),
        P("dp"),
        P("dp"),
        P(),
        P(None, "tensor"),
        P(None, "tensor"),
        P("tensor", None),
        P(),
        P(None, "tensor"),
        P(),
        P(None, "tensor"),
    )
    out_specs = (P(("dp", "tensor")), P(("dp", "tensor")), P("dp"))
    devices = mesh.shape["tensor"]

    def on_device(hidden_in, expert_ids, *others):
        both_experts = expert_ids.shape[1] == 2 and devices == 2 * SPLIT
        step = dense_on_device if both_experts else routed_on_device
        return step(hidden_in, expert_ids, *others)

    return jax.shard_map(
        on_device, mesh=mesh, in_specs=in_specs, out_specs=out_specs, check_vma=False
    )
```
